32 devices in a mesh: rep: 2 (over y), dec: 4 (over z), tp: 4 (over x, core).
Axes of the slice: x: 2, y: 2, z: 4, core: 2. Of those that a mesh axis runs over, the one named last changes fastest.
Arguments:
- token_states: bfloat16 [64, 2, 5120], P(('rep', 'dec')), parts along dimension 0, may hold values from -6 to 6
- query_rows: bfloat16 [64, 2, 4096], P(('rep', 'dec'), None, 'tp'), parts along dimension 0, may hold values from -400 to 400
- key_weight: bfloat16 [5120, 512], P(None, 'tp'), may hold values from -0.078125 to 0.078125
- value_weight: bfloat16 [5120, 512], P(None, 'tp'), may hold values from -0.078125 to 0.078125
- out_weight: bfloat16 [4096, 2560], P('tp'), may hold values from -0.5 to 0.5
- key_pool: bfloat16 [256, 4, 128, 128], P(('rep', 'dec'), 'tp'), parts along dimension 0, may hold values from -6 to 6
- value_pool: bfloat16 [256, 4, 128, 128], P(('rep', 'dec'), 'tp'), parts along dimension 0, may hold values from -6 to 6
- cached_len: int32 [8, 8], P('rep'), parts along dimension 0, may hold values from 0 to 510, as said below
- page_table: int32 [8, 8, 4], P(('rep', 'dec')), parts along dimension 0, may hold values from 0 to 31, as said below
- migrations: int32 [8, 4], P('rep'), parts along dimension 0, may hold values from 0 to 7, as said below
Outputs:
- mixed: bfloat16 [64, 2, 2560], P(('rep', 'dec')), parts along dimension 0
- key_pool_out: bfloat16 [256, 4, 128, 128], P(('rep', 'dec'), 'tp'), parts along dimension 0
- value_pool_out: bfloat16 [256, 4, 128, 128], P(('rep', 'dec'), 'tp'), parts along dimension 0
The draws below stay inside these ranges and needn't reach their ends.
There are 2 independent parts, one for each index of `rep`. The reference program is written for one: setup_inputs(seed, part) draws one part's arguments, and reference() takes and returns one part's arrays. A program takes and returns all parts, laid end to end along the dimension named above; an argument that names none is the same for every part. Nothing has to cross between parts.
Inputs may be any that keep to these rules, and one draw needn't show every extreme that they name: `migrations`: the groups form pairs g and g + 2; in each pair one group sends and the other receives. The sender of pair i sends one response from each of 2 distinct slots, to the receivers of pairs i and i + 1 (mod 2); every receiver gets 2 responses into distinct slots. Rows are in any order. `cached_len`: 0 exactly for the slots that receive a response; sending groups' slots hold 255 or more tokens, receiving groups' other slots 128 or fewer; in every draw at least one moving response has exactly 510 tokens. `page_table`: each group's table names every page 0 to 31 of its pool once.
All inputs are finite; a program needn't handle non-finite values.
Results may differ from the reference program's by a relative error of at most 0.0059.
Values may be sent and summed in bfloat16 or wider, within the bound.
No kernel may reach another device: no remote copies, remote signals or barrier semaphores. Data moves between devices by JAX's collectives and lax.ppermute only.
A program may use at most 64 MiB of HBM per device.

```python
import jax
import jax.numpy as jnp
from jax import lax

D = 5120
DWIN = 2560
QH = 32
KVH = 4
HD = 128
PAGE = 128
MAXP = 4
STEPS = 2
MIG = 2
SLOTS = 8
GROUPS = 4
POOL = 32
NMOVES = 4
MAXLEN = 510


def migration_plan(key):
    half = GROUPS // 2
    keys = jax.random.split(key, 7)
    bits = jax.random.randint(keys[0], (half,), 0, 2)
    pairs = jnp.arange(half, dtype=jnp.int32)
    busy = pairs + bits * half
    freed = pairs + (1 - bits) * half
    source_perm = jax.vmap(lambda k: jax.random.permutation(k, SLOTS))(jax.random.split(keys[1], half))
    target_perm = jax.vmap(lambda k: jax.random.permutation(k, SLOTS))(jax.random.split(keys[2], half))
    blocks = []
    for t in range(MIG):
        target = (pairs + t) % half
        blocks.append(jnp.stack([busy, source_perm[:, t], freed[target], target_perm[target, t]], 1))
    moves = jnp.concatenate(blocks, 0)
    moves = moves[jax.random.permutation(keys[3], NMOVES)]
    is_busy = jnp.zeros((GROUPS,), jnp.int32).at[busy].set(1)
    longer = jax.random.randint(keys[4], (GROUPS, SLOTS), MAXLEN // 2, MAXLEN + 1)
    shorter = jax.random.randint(keys[5], (GROUPS, SLOTS), 1, PAGE + 1)
    lengths = jnp.where(is_busy[:, None] == 1, longer, shorter)
    lengths = lengths.at[freed[:, None], target_perm[:, :MIG]].set(0)
    picked = jax.random.randint(keys[6], (), 0, half)
    lengths = lengths.at[busy[picked], source_perm[picked, 0]].set(MAXLEN)
    return (moves.astype(jnp.int32), lengths.astype(jnp.int32))


def draw_migrations(key, part):
    moves, lengths = migration_plan(key)
    return moves


def draw_cached_len(key, part):
    moves, lengths = migration_plan(key)
    return lengths


def draw_page_table(key, part):
    key = jax.random.fold_in(key, 11)
    tables = jax.vmap(lambda k: jax.random.permutation(k, POOL))(jax.random.split(key, GROUPS))
    return tables.reshape(GROUPS, SLOTS, MAXP).astype(jnp.int32)


def draw_query_rows(key, part):
    key = jax.random.fold_in(key, 23)
    keys = jax.random.split(key, 1)
    count = GROUPS * SLOTS
    base = jnp.clip(jax.random.normal(keys[0], (count, STEPS, QH, HD), jnp.float32), -4.0, 4.0)
    return base.reshape(count, STEPS, QH * HD).astype(jnp.bfloat16)


def block_scale(own_key, shape, shards, smallest, largest):
    gain = 1.0
    for axis_at, shards_of in shards:
        draws = jax.random.uniform(jax.random.fold_in(jax.random.fold_in(own_key, 6), axis_at), (shards_of,), jnp.float32, smallest / len(shards), largest / len(shards))
        gain = gain * jnp.repeat(jnp.exp(draws), shape[axis_at] // shards_of).reshape((-1,) + (1,) * (len(shape) - 1 - axis_at))
    return gain


def bell_draw(key, dims, scale, most, shards=(), kind=jnp.bfloat16):
    values = scale * jax.random.normal(key, dims, jnp.float32)
    if shards:
        values = values * block_scale(key, dims, shards, -0.22, 0.18)
    return jnp.clip(values, -most, most).astype(kind)


def setup_inputs(seed: int = 0, part: int = 0) -> dict:
    splits = jax.random.split(jax.random.key(seed), 11)
    part_splits = jax.random.split(jax.random.fold_in(splits[10], part), 11)
    return {
        "token_states": bell_draw(part_splits[0], (GROUPS * SLOTS, STEPS, D), 1.0, 6.0, ((0, 4),)),
        "query_rows": draw_query_rows(jax.random.fold_in(jax.random.fold_in(splits[10], part), 71), part),
        "key_weight": bell_draw(splits[2], (D, KVH * HD), D ** -0.5, 0.078125, ((1, 4),)),
        "value_weight": bell_draw(splits[3], (D, KVH * HD), D ** -0.5, 0.078125, ((1, 4),)),
        "out_weight": bell_draw(splits[4], (QH * HD, DWIN), HD ** -0.5, 0.5, ((0, 4),)),
        "key_pool": bell_draw(part_splits[5], (GROUPS * POOL, KVH, PAGE, HD), 1.0, 6.0, ((0, 4), (1, 4))),
        "value_pool": bell_draw(part_splits[6], (GROUPS * POOL, KVH, PAGE, HD), 1.0, 6.0, ((0, 4), (1, 4))),
        "cached_len": draw_cached_len(jax.random.fold_in(jax.random.fold_in(splits[10], part), 71), part),
        "page_table": draw_page_table(jax.random.fold_in(jax.random.fold_in(splits[10], part), 71), part),
        "migrations": draw_migrations(jax.random.fold_in(jax.random.fold_in(splits[10], part), 71), part),
    }


def attend(query, states, cache_k, cache_v, key_weight, value_weight, length):
    count, step_count, hidden = states.shape
    pages, kv_heads, page_len, head_dim = cache_k.shape[1:]
    flat = states.reshape(count * step_count, hidden)
    new_k = jnp.dot(flat, key_weight, preferred_element_type=jnp.float32).astype(jnp.bfloat16)
    new_k = new_k.reshape(count, step_count, kv_heads, head_dim)
    new_v = jnp.dot(flat, value_weight, preferred_element_type=jnp.float32).astype(jnp.bfloat16)
    new_v = new_v.reshape(count, step_count, kv_heads, head_dim)
    query = query.reshape(count, step_count, kv_heads, -1, head_dim).astype(jnp.float32)
    group_size = query.shape[3]
    scaling = head_dim ** -0.5
    positions = jnp.arange(pages, dtype=jnp.int32)[:, None] * page_len + jnp.arange(page_len, dtype=jnp.int32)[None, :]
    inside = positions[None] < length[:, None, None]
    cached = jnp.einsum('nskgd,nmkpd->nskgmp', query, cache_k.astype(jnp.float32)) * scaling
    cached = jnp.where(inside[:, None, None, None], cached, -jnp.inf)
    fresh = jnp.einsum('nskgd,ntkd->nskgt', query, new_k.astype(jnp.float32)) * scaling
    causal = jnp.arange(step_count)[None, :] <= jnp.arange(step_count)[:, None]
    fresh = jnp.where(causal[None, :, None, None, :], fresh, -jnp.inf)
    span = pages * page_len
    scores = jnp.concatenate([cached.reshape(count, step_count, kv_heads, group_size, span), fresh], -1)
    peak = jnp.max(scores, -1, keepdims=True)
    weights = jnp.exp(scores - peak)
    weights = (weights / jnp.sum(weights, -1, keepdims=True)).astype(jnp.bfloat16)
    cache_weights = weights[..., :span].reshape(count, step_count, kv_heads, group_size, pages, page_len).astype(jnp.float32)
    fresh_weights = weights[..., span:].astype(jnp.float32)
    out = jnp.einsum('nskgmp,nmkpd->nskgd', cache_weights, cache_v.astype(jnp.float32))
    out = out + jnp.einsum('nskgt,ntkd->nskgd', fresh_weights, new_v.astype(jnp.float32))
    attention = out.astype(jnp.bfloat16).reshape(count, step_count, kv_heads * group_size * head_dim)
    return attention, new_k, new_v


def write_new(cache, fresh, length, live):
    pages, page_len = cache.shape[1], cache.shape[3]
    positions = jnp.arange(pages, dtype=jnp.int32)[:, None] * page_len + jnp.arange(page_len, dtype=jnp.int32)[None, :]
    for t in range(fresh.shape[1]):
        hot = live[:, None, None] & (positions[None] == (length + t)[:, None, None])
        cache = jnp.where(hot[:, :, None, :, None], fresh[:, t][:, None, :, None, :], cache)
    return cache


def reference(token_states, query_rows, key_weight, value_weight, out_weight, key_pool, value_pool, cached_len, page_table, migrations):
    source_group = migrations[:, 0]
    source_slot = migrations[:, 1]
    target_group = migrations[:, 2]
    target_slot = migrations[:, 3]
    owner_group = jnp.broadcast_to(jnp.arange(GROUPS, dtype=jnp.int32)[:, None], (GROUPS, SLOTS))
    owner_slot = jnp.broadcast_to(jnp.arange(SLOTS, dtype=jnp.int32)[None, :], (GROUPS, SLOTS))
    owner_group = owner_group.at[target_group, target_slot].set(source_group)
    owner_slot = owner_slot.at[target_group, target_slot].set(source_slot)
    received = jnp.zeros((GROUPS, SLOTS), bool).at[target_group, target_slot].set(True)
    sent = jnp.zeros((GROUPS, SLOTS), bool).at[source_group, source_slot].set(True)
    live = received | ((cached_len > 0) & ~sent)
    length = cached_len[owner_group, owner_slot]
    read_pages = owner_group[:, :, None] * POOL + page_table[owner_group, owner_slot]
    write_pages = jnp.arange(GROUPS, dtype=jnp.int32)[:, None, None] * POOL + page_table
    positions = jnp.arange(MAXP, dtype=jnp.int32)[:, None] * PAGE + jnp.arange(PAGE, dtype=jnp.int32)[None, :]
    zero = jnp.zeros((), key_pool.dtype)

    def one_group(group):
        rows = owner_group[group] * SLOTS + owner_slot[group]
        states = token_states[rows]
        query = query_rows[rows]
        chosen = read_pages[group].reshape(-1)
        keep = (positions[None] < length[group][:, None, None]) | ~received[group][:, None, None]
        keep = keep[:, :, None, :, None]
        cache_k = jnp.where(keep, key_pool[chosen].reshape(SLOTS, MAXP, KVH, PAGE, HD), zero)
        cache_v = jnp.where(keep, value_pool[chosen].reshape(SLOTS, MAXP, KVH, PAGE, HD), zero)
        attention, new_k, new_v = attend(query, states, cache_k, cache_v, key_weight, value_weight, length[group])
        mixed = jnp.dot(attention.reshape(SLOTS * STEPS, QH * HD), out_weight, preferred_element_type=jnp.float32)
        mixed = jnp.where(live[group][:, None, None], mixed.reshape(SLOTS, STEPS, DWIN), 0.0).astype(jnp.bfloat16)
        slot_k = write_new(cache_k, new_k, length[group], live[group])
        slot_v = write_new(cache_v, new_v, length[group], live[group])
        return mixed, slot_k, slot_v

    mixed, slot_k, slot_v = lax.map(one_group, jnp.arange(GROUPS, dtype=jnp.int32))
    flat_pages = write_pages.reshape(-1)
    key_out = key_pool.at[flat_pages].set(slot_k.reshape(GROUPS * POOL, KVH, PAGE, HD))
    value_out = value_pool.at[flat_pages].set(slot_v.reshape(GROUPS * POOL, KVH, PAGE, HD))
    return mixed.reshape(GROUPS * SLOTS, STEPS, DWIN), key_out, value_out
```

```python
import functools

import jax
import jax.numpy as jnp
from jax import lax
from jax.experimental import pallas as pl
from jax.experimental.pallas import tpu as pltpu
from jax.sharding import PartitionSpec as P

F32 = jnp.float32
BF16 = jnp.bfloat16
SMEM = pl.BlockSpec(memory_space=pltpu.SMEM)
HBM = pl.BlockSpec(memory_space=pltpu.HBM)
ANY = pl.BlockSpec(memory_space=pl.ANY)
VMEM = pl.BlockSpec(memory_space=pltpu.VMEM)


def ring(count, by):
    return [(i, (i + by) % count) for i in range(count)]


def outgoing(mig, me, groups):
    half = groups // 2
    near = jnp.int32(-1)
    far = jnp.int32(-1)
    for m in range(mig.shape[0]):
        mine = mig[m, 0] == me
        gap = lax.rem(mig[m, 2] - me + groups, groups)
        near = jnp.where(mine & (gap == half), mig[m, 1], near)
        far = jnp.where(mine & (gap != half), mig[m, 1], far)
    return near, far


def incoming(mig, lens, me, groups):
    half = groups // 2
    near, far = jnp.int32(-1), jnp.int32(-1)
    near_len, far_len, far_gap = jnp.int32(0), jnp.int32(0), jnp.int32(0)
    for m in range(mig.shape[0]):
        mine = mig[m, 2] == me
        gap = lax.rem(me - mig[m, 0] + groups, groups)
        length = lens[mig[m, 0], mig[m, 1]]
        is_near = mine & (gap == half)
        is_far = mine & (gap != half)
        near = jnp.where(is_near, mig[m, 3], near)
        near_len = jnp.where(is_near, length, near_len)
        far = jnp.where(is_far, mig[m, 3], far)
        far_len = jnp.where(is_far, length, far_len)
        far_gap = jnp.where(is_far, gap, far_gap)
    return near, near_len, far, far_len, far_gap


def pack_kernel(groups, mig, table, key_pool, value_pool, near_out, far_out, sems):
    me = lax.axis_index("dec")
    pages = table.shape[1]
    slots = outgoing(mig, me, groups)
    for n, (slot, out) in enumerate(zip(slots, (near_out, far_out))):

        @pl.when(slot >= 0)
        def _():
            for p in range(pages):
                page = table[0, p, slot]
                pltpu.make_async_copy(key_pool.at[page], out.at[p], sems.at[n, 0, p]).start()
                pltpu.make_async_copy(value_pool.at[page], out.at[pages + p], sems.at[n, 1, p]).start()

    for n, (slot, out) in enumerate(zip(slots, (near_out, far_out))):

        @pl.when(slot >= 0)
        def _():
            for p in range(pages):
                page = table[0, p, slot]
                pltpu.make_async_copy(key_pool.at[page], out.at[p], sems.at[n, 0, p]).wait()
                pltpu.make_async_copy(value_pool.at[page], out.at[pages + p], sems.at[n, 1, p]).wait()


def attend_kernel(
    groups,
    mig,
    lens,
    table,
    states,
    query,
    key_weight,
    value_weight,
    out_weight,
    key_pool,
    value_pool,
    key_out,
    value_out,
    partial,
    new_rows,
    wk,
    wv,
    wo,
    kp,
    vp,
    q_scr,
    a_scr,
    n_scr,
    sems,
):
    me = lax.axis_index("dec")
    slot_count, steps, _ = states.shape
    rows = slot_count * steps
    pages = table.shape[1]
    page_len, head_dim = kp.shape[1:]
    heads = query.shape[2] // head_dim
    span = pages * page_len
    loads = [
        pltpu.make_async_copy(src, dst, sems.at[n])
        for n, (src, dst) in enumerate(
            ((key_weight, wk), (value_weight, wv), (key_pool, kp), (value_pool, vp), (out_weight, wo))
        )
    ]
    for load in loads:
        load.start()
    near, far = outgoing(mig, me, groups)

    qf = query[...].astype(F32)
    for s in range(slot_count):
        for h in range(heads):
            q_scr[pl.ds(h * rows + s * steps, steps), :] = qf[s, :, h * head_dim : (h + 1) * head_dim]
    x = jnp.concatenate([states[s].astype(F32) for s in range(slot_count)], 0).astype(BF16)
    loads[0].wait()
    new_k = jnp.dot(x, wk[...], preferred_element_type=F32).astype(BF16)
    loads[1].wait()
    new_v = jnp.dot(x, wv[...], preferred_element_type=F32).astype(BF16)
    new_rows[:, :head_dim] = new_k
    new_rows[:, head_dim:] = new_v
    n_scr[:, :head_dim] = new_k.astype(F32)
    n_scr[:, head_dim:] = new_v.astype(F32)
    loads[2].wait()
    loads[3].wait()

    scaling = head_dim**-0.5
    count = steps * heads
    fresh_col = lax.broadcasted_iota(jnp.int32, (count, rows), 1)
    fresh_step = lax.broadcasted_iota(jnp.int32, (count, rows), 0) // heads
    position = lax.broadcasted_iota(jnp.int32, (count, span), 1)
    nt = (((1,), (1,)), ((), ()))
    for s in range(slot_count):
        length = lens[me, s]
        numbers = [table[0, p, s] for p in range(pages)]
        keys = jnp.concatenate([kp[n] for n in numbers], 0)
        values = jnp.concatenate([vp[n] for n in numbers], 0)
        qs = jnp.concatenate(
            [q_scr[pl.ds(s * steps + t, heads, stride=rows), :] for t in range(steps)], 0
        ).astype(BF16)
        cached = lax.dot_general(qs, keys, nt, preferred_element_type=F32) * scaling
        cached = jnp.where(position < length, cached, -jnp.inf)
        fresh = lax.dot_general(qs, new_k, nt, preferred_element_type=F32) * scaling
        ok = (fresh_col >= s * steps) & (fresh_col <= s * steps + fresh_step)
        fresh = jnp.where(ok, fresh, -jnp.inf)
        peak = jnp.maximum(jnp.max(cached, 1, keepdims=True), jnp.max(fresh, 1, keepdims=True))
        cached = jnp.exp(cached - peak)
        fresh = jnp.exp(fresh - peak)
        total = jnp.sum(cached, 1, keepdims=True) + jnp.sum(fresh, 1, keepdims=True)
        cached_w = (cached / total).astype(BF16)
        fresh_w = (fresh / total).astype(BF16)
        out = jnp.dot(cached_w, values, preferred_element_type=F32)
        out = out + jnp.dot(fresh_w, new_v, preferred_element_type=F32)
        for t in range(steps):
            a_scr[pl.ds(s * steps + t, heads, stride=rows), :] = out[t * heads : (t + 1) * heads]

    tile = 16
    row = lax.broadcasted_iota(jnp.int32, (tile, head_dim), 0)
    for s in range(slot_count):
        length = lens[me, s]

        @pl.when((length > 0) & (s != near) & (s != far))
        def _():
            for t in range(steps):
                at = length + t
                page = table[0, at // page_len, s]
                offset = lax.rem(at, page_len)
                base = pl.multiple_of(offset // tile * tile, tile)
                hot = row == offset - base
                for pool, low in ((kp, 0), (vp, head_dim)):
                    old = pool[page, pl.ds(base, tile), :].astype(F32)
                    fresh_row = n_scr[s * steps + t : s * steps + t + 1, low : low + head_dim]
                    pool[page, pl.ds(base, tile), :] = jnp.where(hot, fresh_row, old).astype(BF16)

    stores = [
        pltpu.make_async_copy(kp, key_out, sems.at[0]),
        pltpu.make_async_copy(vp, value_out, sems.at[1]),
    ]
    for store in stores:
        store.start()
    attention = jnp.concatenate([a_scr[h * rows : (h + 1) * rows, :].astype(BF16) for h in range(heads)], 1)
    loads[4].wait()
    partial[...] = jnp.dot(attention, wo[...], preferred_element_type=F32).astype(BF16)
    for store in stores:
        store.wait()


def finish_rows_kernel(groups, mig, mine, other, new_rows, total, near_out, far_out, scr):
    me = lax.axis_index("dec")
    near, far = outgoing(mig, me, groups)
    width = mine.shape[1]
    both = (mine[...].astype(F32) + other[...].astype(F32)).astype(BF16)
    total[...] = both
    slot_count, steps, _ = scr.shape
    for s in range(slot_count):
        scr[s, :, :width] = both[s * steps : (s + 1) * steps].astype(F32)
        scr[s, :, width:] = new_rows[s * steps : (s + 1) * steps, :].astype(F32)
    for slot, out in ((near, near_out), (far, far_out)):
        out[...] = scr[jnp.maximum(slot, 0)].astype(BF16)


def mixed_kernel(groups, mig, lens, total, near_in, far_in_a, far_in_b, mixed):
    me = lax.axis_index("dec")
    slot_count, steps, width = mixed.shape
    out_near, out_far = outgoing(mig, me, groups)
    near, _, far, _, far_gap = incoming(mig, lens, me, groups)
    near_rows = near_in[:, :width]
    far_rows = jnp.where(far_gap == 1, far_in_a[:, :width].astype(F32), far_in_b[:, :width].astype(F32))
    for s in range(slot_count):
        live = (lens[me, s] > 0) & (s != out_near) & (s != out_far)
        own = jnp.where(live, total[s * steps : (s + 1) * steps, :].astype(F32), 0.0)
        got = jnp.where(s == near, near_rows.astype(F32), far_rows)
        mixed[s] = jnp.where((s == near) | (s == far), got, own).astype(BF16)


def place_kernel(
    groups,
    mig,
    lens,
    table,
    near_pages,
    far_pages_a,
    far_pages_b,
    near_rows,
    far_rows_a,
    far_rows_b,
    key_in,
    value_in,
    key_out,
    value_out,
    stage,
    in_sems,
    out_sems,
):
    del key_in, value_in
    me = lax.axis_index("dec")
    pages = table.shape[1]
    page_len, head_dim = stage.shape[2:]
    steps = near_rows.shape[0]
    width = near_rows.shape[1] - 2 * head_dim
    near, near_len, far, far_len, far_gap = incoming(mig, lens, me, groups)
    row = lax.broadcasted_iota(jnp.int32, (page_len, head_dim), 0)

    def load(n, source):
        return pltpu.make_async_copy(source, stage.at[n], in_sems.at[n])

    @pl.when(near >= 0)
    def _():
        load(0, near_pages).start()

    @pl.when((far >= 0) & (far_gap == 1))
    def _():
        load(1, far_pages_a).start()

    @pl.when((far >= 0) & (far_gap != 1))
    def _():
        load(1, far_pages_b).start()

    def store(n, slot, p, which):
        pool = (key_out, value_out)[which]
        return pltpu.make_async_copy(
            stage.at[n, which * pages + p], pool.at[table[0, p, slot]], out_sems.at[n, which, p]
        )

    far_rows = jnp.where(far_gap == 1, far_rows_a[:, width:].astype(F32), far_rows_b[:, width:].astype(F32))
    cases = (
        (near, near_len, near_pages, near_rows[:, width:].astype(F32)),
        (far, far_len, far_pages_a, far_rows),
    )
    for n, (slot, length, source, fresh) in enumerate(cases):

        @pl.when(slot >= 0)
        def _():
            load(n, source).wait()
            for p in range(pages):
                at = row + p * page_len
                for which in range(2):
                    page = stage[n, which * pages + p].astype(F32)
                    page = jnp.where(at < length, page, 0.0)
                    for t in range(steps):
                        line = fresh[t : t + 1, which * head_dim : (which + 1) * head_dim]
                        page = jnp.where(at == length + t, line, page)
                    stage[n, which * pages + p] = page.astype(BF16)
                    store(n, slot, p, which).start()

    for n, (slot, _, _, _) in enumerate(cases):

        @pl.when(slot >= 0)
        def _():
            for p in range(pages):
                for which in range(2):
                    store(n, slot, p, which).wait()


def local(
    token_states,
    query_rows,
    key_weight,
    value_weight,
    out_weight,
    key_pool,
    value_pool,
    cached_len,
    page_table,
    migrations,
):
    groups = lax.axis_size("dec")
    half = groups // 2
    tp = lax.axis_size("tp")
    slot_count, steps, model = token_states.shape
    pool_pages, _, page_len, head_dim = key_pool.shape
    rows = slot_count * steps
    width = out_weight.shape[1]
    heads = query_rows.shape[2] // head_dim
    keys = key_pool.reshape(pool_pages, page_len, head_dim)
    values = value_pool.reshape(pool_pages, page_len, head_dim)
    table = jnp.swapaxes(page_table, 1, 2)
    pages = table.shape[1]
    pool_shape = jax.ShapeDtypeStruct(keys.shape, BF16)
    moved_shape = jax.ShapeDtypeStruct((2 * pages, page_len, head_dim), BF16)
    limit = pltpu.CompilerParams(vmem_limit_bytes=48 * 2**20)

    near, far = pl.pallas_call(
        functools.partial(pack_kernel, groups),
        out_shape=(moved_shape, moved_shape),
        in_specs=[SMEM, SMEM, HBM, HBM],
        out_specs=(HBM, HBM),
        scratch_shapes=[pltpu.SemaphoreType.DMA((2, 2, pages))],
        name="pack",
    )(migrations, table, keys, values)
    near_pages = lax.ppermute(near, "dec", ring(groups, half))
    far_pages_a = lax.ppermute(far, "dec", ring(groups, 1))
    far_pages_b = lax.ppermute(far, "dec", ring(groups, 1 + half))

    key_mid, value_mid, partial, new_rows = pl.pallas_call(
        functools.partial(attend_kernel, groups),
        out_shape=(
            pool_shape,
            pool_shape,
            jax.ShapeDtypeStruct((rows, width), BF16),
            jax.ShapeDtypeStruct((rows, 2 * head_dim), BF16),
        ),
        in_specs=[SMEM, SMEM, SMEM, VMEM, VMEM, HBM, HBM, HBM, HBM, HBM],
        out_specs=(HBM, HBM, VMEM, VMEM),
        scratch_shapes=[
            pltpu.VMEM(key_weight.shape, BF16),
            pltpu.VMEM(value_weight.shape, BF16),
            pltpu.VMEM(out_weight.shape, BF16),
            pltpu.VMEM(keys.shape, BF16),
            pltpu.VMEM(values.shape, BF16),
            pltpu.VMEM((heads * rows, head_dim), F32),
            pltpu.VMEM((heads * rows, head_dim), F32),
            pltpu.VMEM((rows, 2 * head_dim), F32),
            pltpu.SemaphoreType.DMA((5,)),
        ],
        compiler_params=limit,
        cost_estimate=pl.CostEstimate(flops=400_000_000, bytes_accessed=14_000_000, transcendentals=65536),
        name="attend",
    )(
        migrations,
        cached_len,
        table,
        token_states,
        query_rows,
        key_weight,
        value_weight,
        out_weight,
        keys,
        values,
    )

    mine, other = partial, lax.ppermute(partial, "tp", [(i, i ^ 1) for i in range(tp)])
    level = 2
    while level < tp:
        mine = (mine.astype(F32) + other.astype(F32)).astype(BF16)
        other = lax.ppermute(mine, "tp", [(i, i ^ level) for i in range(tp)])
        level *= 2
    row_shape = jax.ShapeDtypeStruct((steps, width + 2 * head_dim), BF16)
    total, near_row, far_row = pl.pallas_call(
        functools.partial(finish_rows_kernel, groups),
        out_shape=(jax.ShapeDtypeStruct((rows, width), BF16), row_shape, row_shape),
        in_specs=[SMEM, VMEM, VMEM, VMEM],
        out_specs=(VMEM, VMEM, VMEM),
        scratch_shapes=[pltpu.VMEM((slot_count, steps, width + 2 * head_dim), F32)],
        name="rows",
    )(migrations, mine, other, new_rows)
    near_rows = lax.ppermute(near_row, "dec", ring(groups, half))
    far_rows_a = lax.ppermute(far_row, "dec", ring(groups, 1))
    far_rows_b = lax.ppermute(far_row, "dec", ring(groups, 1 + half))
    mixed = pl.pallas_call(
        functools.partial(mixed_kernel, groups),
        out_shape=jax.ShapeDtypeStruct((slot_count, steps, width), BF16),
        in_specs=[SMEM, SMEM, VMEM, VMEM, VMEM, VMEM],
        out_specs=VMEM,
        name="mixed",
    )(migrations, cached_len, total, near_rows, far_rows_a, far_rows_b)

    key_out, value_out = pl.pallas_call(
        functools.partial(place_kernel, groups),
        out_shape=(pool_shape, pool_shape),
        in_specs=[SMEM, SMEM, SMEM, ANY, ANY, ANY, VMEM, VMEM, VMEM, HBM, HBM],
        out_specs=(HBM, HBM),
        scratch_shapes=[
            pltpu.VMEM((2, 2 * pages, page_len, head_dim), BF16),
            pltpu.SemaphoreType.DMA((2,)),
            pltpu.SemaphoreType.DMA((2, 2, pages)),
        ],
        input_output_aliases={9: 0, 10: 1},
        name="place",
    )(
        migrations,
        cached_len,
        table,
        near_pages,
        far_pages_a,
        far_pages_b,
        near_rows,
        far_rows_a,
        far_rows_b,
        key_mid,
        value_mid,
    )
    return mixed, key_out.reshape(key_pool.shape), value_out.reshape(value_pool.shape)


def solution(mesh):
    placed = (
        P(("rep", "dec"), None, None),
        P(("rep", "dec"), None, "tp"),
        P(None, "tp"),
        P(None, "tp"),
        P("tp", None),
        P(("rep", "dec"), "tp", None, None),
        P(("rep", "dec"), "tp", None, None),
        P("rep", None),
        P(("rep", "dec"), None, None),
        P("rep", None),
    )
    return jax.shard_map(
        local,
        mesh=mesh,
        in_specs=placed,
        out_specs=(
            P(("rep", "dec"), None, None),
            P(("rep", "dec"), "tp", None, None),
            P(("rep", "dec"), "tp", None, None),
        ),
        check_vma=False,
    )
```

```python
import functools

import jax
import jax.numpy as jnp
from jax import lax
from jax.experimental import pallas as pl
from jax.experimental.pallas import tpu as pltpu
from jax.sharding import PartitionSpec as P

F32 = jnp.float32
BF16 = jnp.bfloat16
SMEM = pl.BlockSpec(memory_space=pltpu.SMEM)
HBM = pl.BlockSpec(memory_space=pltpu.HBM)
ANY = pl.BlockSpec(memory_space=pl.ANY)
VMEM = pl.BlockSpec(memory_space=pltpu.VMEM)


def ring(count, by):
    return [(i, (i + by) % count) for i in range(count)]


def outgoing(mig, me, groups):
    half = groups // 2
    near = jnp.int32(-1)
    far = jnp.int32(-1)
    for m in range(mig.shape[0]):
        mine = mig[m, 0] == me
        gap = lax.rem(mig[m, 2] - me + groups, groups)
        near = jnp.where(mine & (gap == half), mig[m, 1], near)
        far = jnp.where(mine & (gap != half), mig[m, 1], far)
    return near, far


def incoming(mig, lens, me, groups):
    half = groups // 2
    near, far = jnp.int32(-1), jnp.int32(-1)
    near_len, far_len, far_gap = jnp.int32(0), jnp.int32(0), jnp.int32(0)
    for m in range(mig.shape[0]):
        mine = mig[m, 2] == me
        gap = lax.rem(me - mig[m, 0] + groups, groups)
        length = lens[mig[m, 0], mig[m, 1]]
        is_near = mine & (gap == half)
        is_far = mine & (gap != half)
        near = jnp.where(is_near, mig[m, 3], near)
        near_len = jnp.where(is_near, length, near_len)
        far = jnp.where(is_far, mig[m, 3], far)
        far_len = jnp.where(is_far, length, far_len)
        far_gap = jnp.where(is_far, gap, far_gap)
    return near, near_len, far, far_len, far_gap


def pack_kernel(groups, mig, table, key_pool, value_pool, near_out, far_out, token, stage, in_sems, out_sems):
    me = lax.axis_index("dec")
    pages = table.shape[1]
    slots = outgoing(mig, me, groups)
    outs = (near_out, far_out)

    def load(n, which, p):
        page = table[0, p, slots[n]]
        pool = (key_pool, value_pool)[which]
        return pltpu.make_async_copy(pool.at[page], stage.at[n, which * pages + p], in_sems.at[n, which, p])

    def store(n):
        return pltpu.make_async_copy(stage.at[n], outs[n], out_sems.at[n])

    def each(do):
        for n in range(2):

            @pl.when(slots[n] >= 0)
            def _():
                do(n)

    def start(n):
        for p in range(pages):
            for which in range(2):
                load(n, which, p).start()

    def send(n):
        for p in range(pages):
            for which in range(2):
                load(n, which, p).wait()
        store(n).start()

    each(start)
    each(send)
    token[0] = me
    each(lambda n: store(n).wait())


def attend_kernel(
    groups,
    token,
    mig,
    lens,
    table,
    states,
    query,
    key_weight,
    value_weight,
    out_weight,
    key_pool,
    value_pool,
    key_out,
    value_out,
    partial,
    new_rows,
    wk,
    wv,
    wo,
    kp,
    vp,
    q_scr,
    a_scr,
    n_scr,
    sems,
):
    del token
    me = lax.axis_index("dec")
    slot_count, steps, _ = states.shape
    rows = slot_count * steps
    pages = table.shape[1]
    page_len, head_dim = kp.shape[1:]
    heads = query.shape[2] // head_dim
    span = pages * page_len
    loads = [
        pltpu.make_async_copy(src, dst, sems.at[n])
        for n, (src, dst) in enumerate(
            ((key_weight, wk), (value_weight, wv), (key_pool, kp), (value_pool, vp), (out_weight, wo))
        )
    ]
    for load in loads:
        load.start()
    near, far = outgoing(mig, me, groups)

    qf = query[...].astype(F32)
    for s in range(slot_count):
        for h in range(heads):
            q_scr[pl.ds(h * rows + s * steps, steps), :] = qf[s, :, h * head_dim : (h + 1) * head_dim]
    x = jnp.concatenate([states[s].astype(F32) for s in range(slot_count)], 0).astype(BF16)
    loads[0].wait()
    new_k = jnp.dot(x, wk[...], preferred_element_type=F32).astype(BF16)
    loads[1].wait()
    new_v = jnp.dot(x, wv[...], preferred_element_type=F32).astype(BF16)
    new_rows[:, :head_dim] = new_k
    new_rows[:, head_dim:] = new_v
    n_scr[:, :head_dim] = new_k.astype(F32)
    n_scr[:, head_dim:] = new_v.astype(F32)
    loads[2].wait()
    loads[3].wait()

    scaling = head_dim**-0.5
    count = steps * heads
    fresh_col = lax.broadcasted_iota(jnp.int32, (count, rows), 1)
    fresh_step = lax.broadcasted_iota(jnp.int32, (count, rows), 0) // heads
    position = lax.broadcasted_iota(jnp.int32, (count, span), 1)
    nt = (((1,), (1,)), ((), ()))
    for s in range(slot_count):
        length = lens[me, s]
        numbers = [table[0, p, s] for p in range(pages)]
        keys = jnp.concatenate([kp[n] for n in numbers], 0)
        values = jnp.concatenate([vp[n] for n in numbers], 0)
        qs = jnp.concatenate(
            [q_scr[pl.ds(s * steps + t, heads, stride=rows), :] for t in range(steps)], 0
        ).astype(BF16)
        cached = lax.dot_general(qs, keys, nt, preferred_element_type=F32) * scaling
        cached = jnp.where(position < length, cached, -jnp.inf)
        fresh = lax.dot_general(qs, new_k, nt, preferred_element_type=F32) * scaling
        ok = (fresh_col >= s * steps) & (fresh_col <= s * steps + fresh_step)
        fresh = jnp.where(ok, fresh, -jnp.inf)
        peak = jnp.maximum(jnp.max(cached, 1, keepdims=True), jnp.max(fresh, 1, keepdims=True))
        cached = jnp.exp(cached - peak)
        fresh = jnp.exp(fresh - peak)
        total = jnp.sum(cached, 1, keepdims=True) + jnp.sum(fresh, 1, keepdims=True)
        cached_w = (cached / total).astype(BF16)
        fresh_w = (fresh / total).astype(BF16)
        out = jnp.dot(cached_w, values, preferred_element_type=F32)
        out = out + jnp.dot(fresh_w, new_v, preferred_element_type=F32)
        for t in range(steps):
            a_scr[pl.ds(s * steps + t, heads, stride=rows), :] = out[t * heads : (t + 1) * heads]

    tile = 16
    row = lax.broadcasted_iota(jnp.int32, (tile, head_dim), 0)
    for s in range(slot_count):
        length = lens[me, s]

        @pl.when((length > 0) & (s != near) & (s != far))
        def _():
            for t in range(steps):
                at = length + t
                page = table[0, at // page_len, s]
                offset = lax.rem(at, page_len)
                base = pl.multiple_of(offset // tile * tile, tile)
                hot = row == offset - base
                for pool, low in ((kp, 0), (vp, head_dim)):
                    old = pool[page, pl.ds(base, tile), :].astype(F32)
                    fresh_row = n_scr[s * steps + t : s * steps + t + 1, low : low + head_dim]
                    pool[page, pl.ds(base, tile), :] = jnp.where(hot, fresh_row, old).astype(BF16)

    stores = [
        pltpu.make_async_copy(kp, key_out, sems.at[0]),
        pltpu.make_async_copy(vp, value_out, sems.at[1]),
    ]
    for store in stores:
        store.start()
    attention = jnp.concatenate([a_scr[h * rows : (h + 1) * rows, :].astype(BF16) for h in range(heads)], 1)
    loads[4].wait()
    partial[...] = jnp.dot(attention, wo[...], preferred_element_type=F32).astype(BF16)
    for store in stores:
        store.wait()


def finish_rows_kernel(groups, mig, new_rows, *refs):
    *parts, total, near_out, far_out, scr = refs
    me = lax.axis_index("dec")
    near, far = outgoing(mig, me, groups)
    width = parts[0].shape[1]
    terms = [part[...].astype(F32) for part in parts]
    level = 1
    while level < len(terms):
        terms = [terms[n] + terms[n ^ level] for n in range(len(terms))]
        level *= 2
    both = terms[0].astype(BF16)
    total[...] = both
    slot_count, steps, _ = scr.shape
    for s in range(slot_count):
        scr[s, :, :width] = both[s * steps : (s + 1) * steps].astype(F32)
        scr[s, :, width:] = new_rows[s * steps : (s + 1) * steps, :].astype(F32)
    for slot, out in ((near, near_out), (far, far_out)):
        out[...] = scr[jnp.maximum(slot, 0)].astype(BF16)


def mix_rows(mig, lens, me, groups, total, near_in, far_in_a, far_in_b, mixed):
    slot_count, steps, width = mixed.shape
    out_near, out_far = outgoing(mig, me, groups)
    near, _, far, _, far_gap = incoming(mig, lens, me, groups)
    near_rows = near_in[:, :width]
    far_rows = jnp.where(far_gap == 1, far_in_a[:, :width].astype(F32), far_in_b[:, :width].astype(F32))
    for s in range(slot_count):
        live = (lens[me, s] > 0) & (s != out_near) & (s != out_far)
        own = jnp.where(live, total[s * steps : (s + 1) * steps, :].astype(F32), 0.0)
        got = jnp.where(s == near, near_rows.astype(F32), far_rows)
        mixed[s] = jnp.where((s == near) | (s == far), got, own).astype(BF16)


def place_kernel(
    groups,
    mig,
    lens,
    table,
    near_pages,
    far_pages_a,
    far_pages_b,
    near_rows,
    far_rows_a,
    far_rows_b,
    total,
    key_in,
    value_in,
    mixed,
    key_out,
    value_out,
    stage,
    in_sems,
    out_sems,
):
    del key_in, value_in
    me = lax.axis_index("dec")
    pages = table.shape[1]
    page_len, head_dim = stage.shape[2:]
    steps = near_rows.shape[0]
    width = near_rows.shape[1] - 2 * head_dim
    near, near_len, far, far_len, far_gap = incoming(mig, lens, me, groups)
    row = lax.broadcasted_iota(jnp.int32, (page_len, head_dim), 0)

    def load(n, source):
        return pltpu.make_async_copy(source, stage.at[n], in_sems.at[n])

    @pl.when(near >= 0)
    def _():
        load(0, near_pages).start()

    @pl.when((far >= 0) & (far_gap == 1))
    def _():
        load(1, far_pages_a).start()

    @pl.when((far >= 0) & (far_gap != 1))
    def _():
        load(1, far_pages_b).start()

    def store(n, slot, p, which):
        pool = (key_out, value_out)[which]
        return pltpu.make_async_copy(
            stage.at[n, which * pages + p], pool.at[table[0, p, slot]], out_sems.at[n, which, p]
        )

    far_rows = jnp.where(far_gap == 1, far_rows_a[:, width:].astype(F32), far_rows_b[:, width:].astype(F32))
    cases = (
        (near, near_len, near_pages, near_rows[:, width:].astype(F32)),
        (far, far_len, far_pages_a, far_rows),
    )
    for n, (slot, length, source, fresh) in enumerate(cases):

        @pl.when(slot >= 0)
        def _():
            load(n, source).wait()
            for p in range(pages):
                at = row + p * page_len
                for which in range(2):
                    page = stage[n, which * pages + p].astype(F32)
                    page = jnp.where(at < length, page, 0.0)
                    for t in range(steps):
                        line = fresh[t : t + 1, which * head_dim : (which + 1) * head_dim]
                        page = jnp.where(at == length + t, line, page)
                    stage[n, which * pages + p] = page.astype(BF16)
                    store(n, slot, p, which).start()

    mix_rows(mig, lens, me, groups, total, near_rows, far_rows_a, far_rows_b, mixed)

    for n, (slot, _, _, _) in enumerate(cases):

        @pl.when(slot >= 0)
        def _():
            for p in range(pages):
                for which in range(2):
                    store(n, slot, p, which).wait()


def local(
    token_states,
    query_rows,
    key_weight,
    value_weight,
    out_weight,
    key_pool,
    value_pool,
    cached_len,
    page_table,
    migrations,
):
    groups = lax.axis_size("dec")
    half = groups // 2
    tp = lax.axis_size("tp")
    slot_count, steps, model = token_states.shape
    pool_pages, _, page_len, head_dim = key_pool.shape
    rows = slot_count * steps
    width = out_weight.shape[1]
    heads = query_rows.shape[2] // head_dim
    keys = key_pool.reshape(pool_pages, page_len, head_dim)
    values = value_pool.reshape(pool_pages, page_len, head_dim)
    table = jnp.swapaxes(page_table, 1, 2)
    pages = table.shape[1]
    pool_shape = jax.ShapeDtypeStruct(keys.shape, BF16)
    moved_shape = jax.ShapeDtypeStruct((2 * pages, page_len, head_dim), BF16)
    limit = pltpu.CompilerParams(vmem_limit_bytes=60 * 2**20)

    near, far, token = pl.pallas_call(
        functools.partial(pack_kernel, groups),
        out_shape=(moved_shape, moved_shape, jax.ShapeDtypeStruct((1,), jnp.int32)),
        in_specs=[SMEM, SMEM, HBM, HBM],
        out_specs=(HBM, HBM, SMEM),
        scratch_shapes=[
            pltpu.VMEM((2, 2 * pages, page_len, head_dim), BF16),
            pltpu.SemaphoreType.DMA((2, 2, pages)),
            pltpu.SemaphoreType.DMA((2,)),
        ],
        compiler_params=limit,
        name="pack",
    )(migrations, table, keys, values)
    near_pages = lax.ppermute(near, "dec", ring(groups, half))
    far_pages_a = lax.ppermute(far, "dec", ring(groups, 1))
    far_pages_b = lax.ppermute(far, "dec", ring(groups, 1 + half))

    key_mid, value_mid, partial, new_rows = pl.pallas_call(
        functools.partial(attend_kernel, groups),
        out_shape=(
            pool_shape,
            pool_shape,
            jax.ShapeDtypeStruct((rows, width), BF16),
            jax.ShapeDtypeStruct((rows, 2 * head_dim), BF16),
        ),
        in_specs=[SMEM, SMEM, SMEM, SMEM, VMEM, VMEM, HBM, HBM, HBM, HBM, HBM],
        out_specs=(HBM, HBM, VMEM, VMEM),
        scratch_shapes=[
            pltpu.VMEM(key_weight.shape, BF16),
            pltpu.VMEM(value_weight.shape, BF16),
            pltpu.VMEM(out_weight.shape, BF16),
            pltpu.VMEM(keys.shape, BF16),
            pltpu.VMEM(values.shape, BF16),
            pltpu.VMEM((heads * rows, head_dim), F32),
            pltpu.VMEM((heads * rows, head_dim), F32),
            pltpu.VMEM((rows, 2 * head_dim), F32),
            pltpu.SemaphoreType.DMA((5,)),
        ],
        compiler_params=limit,
        cost_estimate=pl.CostEstimate(flops=1_000_000, bytes_accessed=1_000_000, transcendentals=0),
        name="attend",
    )(
        token,
        migrations,
        cached_len,
        table,
        token_states,
        query_rows,
        key_weight,
        value_weight,
        out_weight,
        keys,
        values,
    )

    others = [lax.ppermute(partial, "tp", [(i, i ^ n) for i in range(tp)]) for n in range(1, tp)]
    row_shape = jax.ShapeDtypeStruct((steps, width + 2 * head_dim), BF16)
    total, near_row, far_row = pl.pallas_call(
        functools.partial(finish_rows_kernel, groups),
        out_shape=(jax.ShapeDtypeStruct((rows, width), BF16), row_shape, row_shape),
        in_specs=[SMEM, VMEM] + [VMEM] * tp,
        out_specs=(VMEM, VMEM, VMEM),
        scratch_shapes=[pltpu.VMEM((slot_count, steps, width + 2 * head_dim), F32)],
        compiler_params=limit,
        name="rows",
    )(migrations, new_rows, partial, *others)
    near_rows = lax.ppermute(near_row, "dec", ring(groups, half))
    far_rows_a = lax.ppermute(far_row, "dec", ring(groups, 1))
    far_rows_b = lax.ppermute(far_row, "dec", ring(groups, 1 + half))
    mixed, key_out, value_out = pl.pallas_call(
        functools.partial(place_kernel, groups),
        out_shape=(jax.ShapeDtypeStruct((slot_count, steps, width), BF16), pool_shape, pool_shape),
        in_specs=[SMEM, SMEM, SMEM, ANY, ANY, ANY, VMEM, VMEM, VMEM, VMEM, HBM, HBM],
        out_specs=(VMEM, HBM, HBM),
        scratch_shapes=[
            pltpu.VMEM((2, 2 * pages, page_len, head_dim), BF16),
            pltpu.SemaphoreType.DMA((2,)),
            pltpu.SemaphoreType.DMA((2, 2, pages)),
        ],
        input_output_aliases={10: 1, 11: 2},
        compiler_params=limit,
        name="place",
    )(
        migrations,
        cached_len,
        table,
        near_pages,
        far_pages_a,
        far_pages_b,
        near_rows,
        far_rows_a,
        far_rows_b,
        total,
        key_mid,
        value_mid,
    )
    return mixed, key_out.reshape(key_pool.shape), value_out.reshape(value_pool.shape)


def solution(mesh):
    placed = (
        P(("rep", "dec"), None, None),
        P(("rep", "dec"), None, "tp"),
        P(None, "tp"),
        P(None, "tp"),
        P("tp", None),
        P(("rep", "dec"), "tp", None, None),
        P(("rep", "dec"), "tp", None, None),
        P("rep", None),
        P(("rep", "dec"), None, None),
        P("rep", None),
    )
    return jax.shard_map(
        local,
        mesh=mesh,
        in_specs=placed,
        out_specs=(
            P(("rep", "dec"), None, None),
            P(("rep", "dec"), "tp", None, None),
            P(("rep", "dec"), "tp", None, None),
        ),
        check_vma=False,
    )
```

```python
import functools

import jax
import jax.numpy as jnp
from jax import lax
from jax.experimental import pallas as pl
from jax.experimental.pallas import tpu as pltpu
from jax.sharding import PartitionSpec as P

F32 = jnp.float32
BF16 = jnp.bfloat16
SMEM = pl.BlockSpec(memory_space=pltpu.SMEM)
HBM = pl.BlockSpec(memory_space=pltpu.HBM)
ANY = pl.BlockSpec(memory_space=pl.ANY)
VMEM = pl.BlockSpec(memory_space=pltpu.VMEM)


def outgoing(mig, me, groups):
    half = groups // 2
    near = far = jnp.int32(-1)
    near_to = far_to = jnp.int32(0)
    for m in range(mig.shape[0]):
        mine = mig[m, 0] == me
        gap = lax.rem(mig[m, 2] - me + groups, groups)
        near = jnp.where(mine & (gap == half), mig[m, 1], near)
        near_to = jnp.where(mine & (gap == half), mig[m, 2], near_to)
        far = jnp.where(mine & (gap != half), mig[m, 1], far)
        far_to = jnp.where(mine & (gap != half), mig[m, 2], far_to)
    return (near, far), (near_to, far_to)


def incoming(mig, lens, me, groups):
    half = groups // 2
    near = far = jnp.int32(-1)
    near_len = far_len = near_from = far_from = jnp.int32(0)
    for m in range(mig.shape[0]):
        mine = mig[m, 2] == me
        gap = lax.rem(me - mig[m, 0] + groups, groups)
        length = lens[mig[m, 0], mig[m, 1]]
        is_near = mine & (gap == half)
        is_far = mine & (gap != half)
        near = jnp.where(is_near, mig[m, 3], near)
        near_len = jnp.where(is_near, length, near_len)
        near_from = jnp.where(is_near, mig[m, 0], near_from)
        far = jnp.where(is_far, mig[m, 3], far)
        far_len = jnp.where(is_far, length, far_len)
        far_from = jnp.where(is_far, mig[m, 0], far_from)
    return (near, near_len, near_from), (far, far_len, far_from)


def pack_kernel(groups, mig, table, key_pool, value_pool, out, token, stage, in_sems, out_sems):
    me = lax.axis_index("dec")
    pages = table.shape[1]
    slots, targets = outgoing(mig, me, groups)

    def load(n, which, p):
        page = table[0, p, slots[n]]
        pool = (key_pool, value_pool)[which]
        return pltpu.make_async_copy(pool.at[page], stage.at[n, which * pages + p], in_sems.at[n, which, p])

    def store(n):
        return pltpu.make_async_copy(stage.at[n], out.at[targets[n]], out_sems.at[n])

    def each(do):
        for n in range(2):

            @pl.when(slots[n] >= 0)
            def _():
                do(n)

    def start(n):
        for p in range(pages):
            for which in range(2):
                load(n, which, p).start()

    def send(n):
        for p in range(pages):
            for which in range(2):
                load(n, which, p).wait()
        store(n).start()

    each(start)
    each(send)
    token[0] = me
    each(lambda n: store(n).wait())


def attend_kernel(
    groups,
    token,
    mig,
    lens,
    table,
    states,
    query,
    key_weight,
    value_weight,
    out_weight,
    key_pool,
    value_pool,
    key_out,
    value_out,
    partial,
    new_rows,
    wk,
    wv,
    wo,
    kp,
    vp,
    q_scr,
    a_scr,
    n_scr,
    sems,
):
    del token
    me = lax.axis_index("dec")
    slot_count, steps, _ = states.shape
    rows = slot_count * steps
    pages = table.shape[1]
    page_len, head_dim = kp.shape[1:]
    heads = query.shape[2] // head_dim
    span = pages * page_len
    loads = [
        pltpu.make_async_copy(src, dst, sems.at[n])
        for n, (src, dst) in enumerate(
            ((key_weight, wk), (value_weight, wv), (key_pool, kp), (value_pool, vp), (out_weight, wo))
        )
    ]
    for load in loads:
        load.start()
    (near, far), _ = outgoing(mig, me, groups)

    qf = query[...].astype(F32)
    for s in range(slot_count):
        for h in range(heads):
            q_scr[pl.ds(h * rows + s * steps, steps), :] = qf[s, :, h * head_dim : (h + 1) * head_dim]
    x = jnp.concatenate([states[s].astype(F32) for s in range(slot_count)], 0).astype(BF16)
    loads[0].wait()
    new_k = jnp.dot(x, wk[...], preferred_element_type=F32).astype(BF16)
    loads[1].wait()
    new_v = jnp.dot(x, wv[...], preferred_element_type=F32).astype(BF16)
    new_rows[:, :head_dim] = new_k
    new_rows[:, head_dim:] = new_v
    n_scr[:, :head_dim] = new_k.astype(F32)
    n_scr[:, head_dim:] = new_v.astype(F32)
    loads[2].wait()
    loads[3].wait()

    scaling = head_dim**-0.5
    count = steps * heads
    fresh_col = lax.broadcasted_iota(jnp.int32, (count, rows), 1)
    fresh_step = lax.broadcasted_iota(jnp.int32, (count, rows), 0) // heads
    position = lax.broadcasted_iota(jnp.int32, (count, span), 1)
    nt = (((1,), (1,)), ((), ()))
    for s in range(slot_count):
        length = lens[me, s]
        numbers = [table[0, p, s] for p in range(pages)]
        keys = jnp.concatenate([kp[n] for n in numbers], 0)
        values = jnp.concatenate([vp[n] for n in numbers], 0)
        qs = jnp.concatenate(
            [q_scr[pl.ds(s * steps + t, heads, stride=rows), :] for t in range(steps)], 0
        ).astype(BF16)
        cached = lax.dot_general(qs, keys, nt, preferred_element_type=F32) * scaling
        cached = jnp.where(position < length, cached, -jnp.inf)
        fresh = lax.dot_general(qs, new_k, nt, preferred_element_type=F32) * scaling
        ok = (fresh_col >= s * steps) & (fresh_col <= s * steps + fresh_step)
        fresh = jnp.where(ok, fresh, -jnp.inf)
        peak = jnp.maximum(jnp.max(cached, 1, keepdims=True), jnp.max(fresh, 1, keepdims=True))
        cached = jnp.exp(cached - peak)
        fresh = jnp.exp(fresh - peak)
        total = jnp.sum(cached, 1, keepdims=True) + jnp.sum(fresh, 1, keepdims=True)
        cached_w = (cached / total).astype(BF16)
        fresh_w = (fresh / total).astype(BF16)
        out = jnp.dot(cached_w, values, preferred_element_type=F32)
        out = out + jnp.dot(fresh_w, new_v, preferred_element_type=F32)
        for t in range(steps):
            a_scr[pl.ds(s * steps + t, heads, stride=rows), :] = out[t * heads : (t + 1) * heads]

    tile = 16
    row = lax.broadcasted_iota(jnp.int32, (tile, head_dim), 0)
    for s in range(slot_count):
        length = lens[me, s]

        @pl.when((length > 0) & (s != near) & (s != far))
        def _():
            for t in range(steps):
                at = length + t
                page = table[0, at // page_len, s]
                offset = lax.rem(at, page_len)
                base = pl.multiple_of(offset // tile * tile, tile)
                hot = row == offset - base
                for pool, low in ((kp, 0), (vp, head_dim)):
                    old = pool[page, pl.ds(base, tile), :].astype(F32)
                    fresh_row = n_scr[s * steps + t : s * steps + t + 1, low : low + head_dim]
                    pool[page, pl.ds(base, tile), :] = jnp.where(hot, fresh_row, old).astype(BF16)

    stores = [
        pltpu.make_async_copy(kp, key_out, sems.at[0]),
        pltpu.make_async_copy(vp, value_out, sems.at[1]),
    ]
    for store in stores:
        store.start()
    attention = jnp.concatenate([a_scr[h * rows : (h + 1) * rows, :].astype(BF16) for h in range(heads)], 1)
    loads[4].wait()
    partial[...] = jnp.dot(attention, wo[...], preferred_element_type=F32).astype(BF16)
    for store in stores:
        store.wait()


def finish_rows_kernel(groups, mig, new_rows, *refs):
    *parts, total, out, scr = refs
    me = lax.axis_index("dec")
    slots, targets = outgoing(mig, me, groups)
    width = parts[0].shape[1]
    terms = [part[...].astype(F32) for part in parts]
    level = 1
    while level < len(terms):
        terms = [terms[n] + terms[n ^ level] for n in range(len(terms))]
        level *= 2
    both = terms[0].astype(BF16)
    total[...] = both
    slot_count, steps, _ = scr.shape
    for s in range(slot_count):
        scr[s, :, :width] = both[s * steps : (s + 1) * steps].astype(F32)
        scr[s, :, width:] = new_rows[s * steps : (s + 1) * steps, :].astype(F32)
    for slot, target in zip(slots, targets):

        @pl.when(slot >= 0)
        def _():
            out[target] = scr[slot].astype(BF16)


def place_kernel(
    groups,
    mig,
    lens,
    table,
    pages_in,
    rows_in,
    total,
    key_in,
    value_in,
    mixed,
    key_out,
    value_out,
    stage,
    in_sems,
    out_sems,
):
    del key_in, value_in
    me = lax.axis_index("dec")
    pages = table.shape[1]
    page_len, head_dim = stage.shape[2:]
    slot_count, steps, width = mixed.shape
    cases = incoming(mig, lens, me, groups)
    (out_near, out_far), _ = outgoing(mig, me, groups)
    row = lax.broadcasted_iota(jnp.int32, (page_len, head_dim), 0)

    def load(n):
        return pltpu.make_async_copy(pages_in.at[cases[n][2]], stage.at[n], in_sems.at[n])

    def store(n, p, which):
        pool = (key_out, value_out)[which]
        page = table[0, p, cases[n][0]]
        return pltpu.make_async_copy(stage.at[n, which * pages + p], pool.at[page], out_sems.at[n, which, p])

    def each(do):
        for n in range(2):

            @pl.when(cases[n][0] >= 0)
            def _():
                do(n)

    def patch(n):
        _, length, source = cases[n]
        fresh = rows_in[source].astype(F32)
        load(n).wait()
        for p in range(pages):
            at = row + p * page_len
            for which in range(2):
                page = stage[n, which * pages + p].astype(F32)
                page = jnp.where(at < length, page, 0.0)
                for t in range(steps):
                    low = width + which * head_dim
                    page = jnp.where(at == length + t, fresh[t : t + 1, low : low + head_dim], page)
                stage[n, which * pages + p] = page.astype(BF16)
                store(n, p, which).start()

    def finish(n):
        for p in range(pages):
            for which in range(2):
                store(n, p, which).wait()

    each(lambda n: load(n).start())
    for s in range(slot_count):
        live = (lens[me, s] > 0) & (s != out_near) & (s != out_far)
        mixed[s] = jnp.where(live, total[s * steps : (s + 1) * steps, :].astype(F32), 0.0).astype(BF16)

    def mix(n):
        slot, _, source = cases[n]
        mixed[slot] = rows_in[source, :, :width]

    each(mix)
    each(patch)
    each(finish)


def local(
    token_states,
    query_rows,
    key_weight,
    value_weight,
    out_weight,
    key_pool,
    value_pool,
    cached_len,
    page_table,
    migrations,
):
    groups = lax.axis_size("dec")
    tp = lax.axis_size("tp")
    slot_count, steps, model = token_states.shape
    pool_pages, _, page_len, head_dim = key_pool.shape
    rows = slot_count * steps
    width = out_weight.shape[1]
    heads = query_rows.shape[2] // head_dim
    keys = key_pool.reshape(pool_pages, page_len, head_dim)
    values = value_pool.reshape(pool_pages, page_len, head_dim)
    table = jnp.swapaxes(page_table, 1, 2)
    pages = table.shape[1]
    pool_shape = jax.ShapeDtypeStruct(keys.shape, BF16)
    moved_shape = jax.ShapeDtypeStruct((groups, 2 * pages, page_len, head_dim), BF16)
    limit = pltpu.CompilerParams(vmem_limit_bytes=60 * 2**20)

    packed, token = pl.pallas_call(
        functools.partial(pack_kernel, groups),
        out_shape=(moved_shape, jax.ShapeDtypeStruct((1,), jnp.int32)),
        in_specs=[SMEM, SMEM, HBM, HBM],
        out_specs=(HBM, SMEM),
        scratch_shapes=[
            pltpu.VMEM((2, 2 * pages, page_len, head_dim), BF16),
            pltpu.SemaphoreType.DMA((2, 2, pages)),
            pltpu.SemaphoreType.DMA((2,)),
        ],
        compiler_params=limit,
        name="pack",
    )(migrations, table, keys, values)
    pages_in = lax.all_to_all(packed, "dec", 0, 0)

    key_mid, value_mid, partial, new_rows = pl.pallas_call(
        functools.partial(attend_kernel, groups),
        out_shape=(
            pool_shape,
            pool_shape,
            jax.ShapeDtypeStruct((rows, width), BF16),
            jax.ShapeDtypeStruct((rows, 2 * head_dim), BF16),
        ),
        in_specs=[SMEM, SMEM, SMEM, SMEM, VMEM, VMEM, HBM, HBM, HBM, HBM, HBM],
        out_specs=(HBM, HBM, VMEM, VMEM),
        scratch_shapes=[
            pltpu.VMEM(key_weight.shape, BF16),
            pltpu.VMEM(value_weight.shape, BF16),
            pltpu.VMEM(out_weight.shape, BF16),
            pltpu.VMEM(keys.shape, BF16),
            pltpu.VMEM(values.shape, BF16),
            pltpu.VMEM((heads * rows, head_dim), F32),
            pltpu.VMEM((heads * rows, head_dim), F32),
            pltpu.VMEM((rows, 2 * head_dim), F32),
            pltpu.SemaphoreType.DMA((5,)),
        ],
        compiler_params=limit,
        cost_estimate=pl.CostEstimate(flops=1_000_000, bytes_accessed=1_000_000, transcendentals=0),
        name="attend",
    )(
        token,
        migrations,
        cached_len,
        table,
        token_states,
        query_rows,
        key_weight,
        value_weight,
        out_weight,
        keys,
        values,
    )

    others = [lax.ppermute(partial, "tp", [(i, i ^ n) for i in range(tp)]) for n in range(1, tp)]
    total, moved_rows = pl.pallas_call(
        functools.partial(finish_rows_kernel, groups),
        out_shape=(
            jax.ShapeDtypeStruct((rows, width), BF16),
            jax.ShapeDtypeStruct((groups, steps, width + 2 * head_dim), BF16),
        ),
        in_specs=[SMEM, VMEM] + [VMEM] * tp,
        out_specs=(VMEM, VMEM),
        scratch_shapes=[pltpu.VMEM((slot_count, steps, width + 2 * head_dim), F32)],
        compiler_params=limit,
        name="rows",
    )(migrations, new_rows, partial, *others)
    rows_in = lax.all_to_all(moved_rows, "dec", 0, 0)
    mixed, key_out, value_out = pl.pallas_call(
        functools.partial(place_kernel, groups),
        out_shape=(jax.ShapeDtypeStruct((slot_count, steps, width), BF16), pool_shape, pool_shape),
        in_specs=[SMEM, SMEM, SMEM, ANY, VMEM, VMEM, HBM, HBM],
        out_specs=(VMEM, HBM, HBM),
        scratch_shapes=[
            pltpu.VMEM((2, 2 * pages, page_len, head_dim), BF16),
            pltpu.SemaphoreType.DMA((2,)),
            pltpu.SemaphoreType.DMA((2, 2, pages)),
        ],
        input_output_aliases={6: 1, 7: 2},
        compiler_params=limit,
        name="place",
    )(migrations, cached_len, table, pages_in, rows_in, total, key_mid, value_mid)
    return mixed, key_out.reshape(key_pool.shape), value_out.reshape(value_pool.shape)


def solution(mesh):
    placed = (
        P(("rep", "dec"), None, None),
        P(("rep", "dec"), None, "tp"),
        P(None, "tp"),
        P(None, "tp"),
        P("tp", None),
        P(("rep", "dec"), "tp", None, None),
        P(("rep", "dec"), "tp", None, None),
        P("rep", None),
        P(("rep", "dec"), None, None),
        P("rep", None),
    )
    return jax.shard_map(
        local,
        mesh=mesh,
        in_specs=placed,
        out_specs=(
            P(("rep", "dec"), None, None),
            P(("rep", "dec"), "tp", None, None),
            P(("rep", "dec"), "tp", None, None),
        ),
        check_vma=False,
    )
```

```python
import functools

import jax
import jax.numpy as jnp
from jax import lax
from jax.experimental import pallas as pl
from jax.experimental.pallas import tpu as pltpu
from jax.sharding import PartitionSpec as P

F32 = jnp.float32
BF16 = jnp.bfloat16
SMEM = pl.BlockSpec(memory_space=pltpu.SMEM)
HBM = pl.BlockSpec(memory_space=pltpu.HBM)
ANY = pl.BlockSpec(memory_space=pl.ANY)
VMEM = pl.BlockSpec(memory_space=pltpu.VMEM)


def shifted(count, by):
    return [(i, (i + by) % count) for i in range(count)]


def outgoing(mig, me, groups):
    half = groups // 2
    near = far = jnp.int32(-1)
    for m in range(mig.shape[0]):
        mine = mig[m, 0] == me
        gap = lax.rem(mig[m, 2] - me + groups, groups)
        near = jnp.where(mine & (gap == half), mig[m, 1], near)
        far = jnp.where(mine & (gap != half), mig[m, 1], far)
    return near, far


def incoming(mig, lens, me, groups):
    half = groups // 2
    near = far = jnp.int32(-1)
    near_len = far_len = far_gap = jnp.int32(0)
    for m in range(mig.shape[0]):
        mine = mig[m, 2] == me
        gap = lax.rem(me - mig[m, 0] + groups, groups)
        length = lens[mig[m, 0], mig[m, 1]]
        is_near = mine & (gap == half)
        is_far = mine & (gap != half)
        near = jnp.where(is_near, mig[m, 3], near)
        near_len = jnp.where(is_near, length, near_len)
        far = jnp.where(is_far, mig[m, 3], far)
        far_len = jnp.where(is_far, length, far_len)
        far_gap = jnp.where(is_far, gap, far_gap)
    return (near, near_len), (far, far_len), far_gap


def pack_kernel(groups, mig, table, key_pool, value_pool, near_out, far_out, token, stage, in_sems, out_sems):
    me = lax.axis_index("dec")
    pages = table.shape[1]
    slots = outgoing(mig, me, groups)
    outs = (near_out, far_out)

    def load(n, which, p):
        page = table[0, p, slots[n]]
        pool = (key_pool, value_pool)[which]
        return pltpu.make_async_copy(pool.at[page], stage.at[n, which * pages + p], in_sems.at[n, which, p])

    def store(n):
        return pltpu.make_async_copy(stage.at[n], outs[n], out_sems.at[n])

    def each(do):
        for n in range(2):

            @pl.when(slots[n] >= 0)
            def _():
                do(n)

    def start(n):
        for p in range(pages):
            for which in range(2):
                load(n, which, p).start()

    def send(n):
        for p in range(pages):
            for which in range(2):
                load(n, which, p).wait()
        store(n).start()

    each(start)
    each(send)
    token[0] = me
    each(lambda n: store(n).wait())


def attend_kernel(
    groups,
    token,
    mig,
    lens,
    table,
    states,
    query,
    key_weight,
    value_weight,
    out_weight,
    key_pool,
    value_pool,
    key_out,
    value_out,
    partial,
    new_rows,
    wk,
    wv,
    wo,
    kp,
    vp,
    q_scr,
    a_scr,
    n_scr,
    sems,
):
    del token
    me = lax.axis_index("dec")
    slot_count, steps, _ = states.shape
    rows = slot_count * steps
    pages = table.shape[1]
    page_len, head_dim = kp.shape[1:]
    heads = query.shape[2] // head_dim
    span = pages * page_len
    loads = [
        pltpu.make_async_copy(src, dst, sems.at[n])
        for n, (src, dst) in enumerate(
            ((key_weight, wk), (value_weight, wv), (key_pool, kp), (value_pool, vp), (out_weight, wo))
        )
    ]
    for load in loads:
        load.start()
    near, far = outgoing(mig, me, groups)

    qf = query[...].astype(F32)
    for s in range(slot_count):
        for h in range(heads):
            q_scr[pl.ds(h * rows + s * steps, steps), :] = qf[s, :, h * head_dim : (h + 1) * head_dim]
    x = jnp.concatenate([states[s].astype(F32) for s in range(slot_count)], 0).astype(BF16)
    loads[0].wait()
    new_k = jnp.dot(x, wk[...], preferred_element_type=F32).astype(BF16)
    loads[1].wait()
    new_v = jnp.dot(x, wv[...], preferred_element_type=F32).astype(BF16)
    new_rows[:, :head_dim] = new_k
    new_rows[:, head_dim:] = new_v
    n_scr[:, :head_dim] = new_k.astype(F32)
    n_scr[:, head_dim:] = new_v.astype(F32)
    loads[2].wait()
    loads[3].wait()

    scaling = head_dim**-0.5
    count = steps * heads
    fresh_col = lax.broadcasted_iota(jnp.int32, (count, rows), 1)
    fresh_step = lax.broadcasted_iota(jnp.int32, (count, rows), 0) // heads
    position = lax.broadcasted_iota(jnp.int32, (count, span), 1)
    nt = (((1,), (1,)), ((), ()))
    for s in range(slot_count):
        length = lens[me, s]
        numbers = [table[0, p, s] for p in range(pages)]
        keys = jnp.concatenate([kp[n] for n in numbers], 0)
        values = jnp.concatenate([vp[n] for n in numbers], 0)
        qs = jnp.concatenate(
            [q_scr[pl.ds(s * steps + t, heads, stride=rows), :] for t in range(steps)], 0
        ).astype(BF16)
        cached = lax.dot_general(qs, keys, nt, preferred_element_type=F32) * scaling
        cached = jnp.where(position < length, cached, -jnp.inf)
        fresh = lax.dot_general(qs, new_k, nt, preferred_element_type=F32) * scaling
        ok = (fresh_col >= s * steps) & (fresh_col <= s * steps + fresh_step)
        fresh = jnp.where(ok, fresh, -jnp.inf)
        peak = jnp.maximum(jnp.max(cached, 1, keepdims=True), jnp.max(fresh, 1, keepdims=True))
        cached = jnp.exp(cached - peak)
        fresh = jnp.exp(fresh - peak)
        total = jnp.sum(cached, 1, keepdims=True) + jnp.sum(fresh, 1, keepdims=True)
        cached_w = (cached / total).astype(BF16)
        fresh_w = (fresh / total).astype(BF16)
        out = jnp.dot(cached_w, values, preferred_element_type=F32)
        out = out + jnp.dot(fresh_w, new_v, preferred_element_type=F32)
        for t in range(steps):
            a_scr[pl.ds(s * steps + t, heads, stride=rows), :] = out[t * heads : (t + 1) * heads]

    tile = 16
    row = lax.broadcasted_iota(jnp.int32, (tile, head_dim), 0)
    for s in range(slot_count):
        length = lens[me, s]

        @pl.when((length > 0) & (s != near) & (s != far))
        def _():
            for t in range(steps):
                at = length + t
                page = table[0, at // page_len, s]
                offset = lax.rem(at, page_len)
                base = pl.multiple_of(offset // tile * tile, tile)
                hot = row == offset - base
                for pool, low in ((kp, 0), (vp, head_dim)):
                    old = pool[page, pl.ds(base, tile), :].astype(F32)
                    fresh_row = n_scr[s * steps + t : s * steps + t + 1, low : low + head_dim]
                    pool[page, pl.ds(base, tile), :] = jnp.where(hot, fresh_row, old).astype(BF16)

    stores = [
        pltpu.make_async_copy(kp, key_out, sems.at[0]),
        pltpu.make_async_copy(vp, value_out, sems.at[1]),
    ]
    for store in stores:
        store.start()
    attention = jnp.concatenate([a_scr[h * rows : (h + 1) * rows, :].astype(BF16) for h in range(heads)], 1)
    loads[4].wait()
    partial[...] = jnp.dot(attention, wo[...], preferred_element_type=F32).astype(BF16)
    for store in stores:
        store.wait()


def finish_rows_kernel(groups, mig, new_rows, *refs):
    *parts, total, near_out, far_out, scr = refs
    me = lax.axis_index("dec")
    slots = outgoing(mig, me, groups)
    width = parts[0].shape[1]
    terms = [part[...].astype(F32) for part in parts]
    level = 1
    while level < len(terms):
        terms = [terms[n] + terms[n ^ level] for n in range(len(terms))]
        level *= 2
    both = terms[0].astype(BF16)
    total[...] = both
    slot_count, steps, _ = scr.shape
    for s in range(slot_count):
        scr[s, :, :width] = both[s * steps : (s + 1) * steps].astype(F32)
        scr[s, :, width:] = new_rows[s * steps : (s + 1) * steps, :].astype(F32)
    for slot, out in zip(slots, (near_out, far_out)):
        out[...] = scr[jnp.maximum(slot, 0)].astype(BF16)


def place_kernel(groups, ways, mig, lens, table, *refs):
    near_pages, *far_pages = refs[: 1 + ways]
    near_rows, *far_rows = refs[1 + ways : 2 + 2 * ways]
    total, _, _, mixed, key_out, value_out, stage, in_sems, out_sems = refs[2 + 2 * ways :]
    me = lax.axis_index("dec")
    pages = table.shape[1]
    page_len, head_dim = stage.shape[2:]
    slot_count, steps, width = mixed.shape
    *cases, far_gap = incoming(mig, lens, me, groups)
    out_near, out_far = outgoing(mig, me, groups)
    row = lax.broadcasted_iota(jnp.int32, (page_len, head_dim), 0)
    pages_in = (near_pages, far_pages[0])
    rows_in = [near_rows[...].astype(F32), far_rows[0][...].astype(F32)]
    if ways == 2:
        rows_in[1] = jnp.where(far_gap == 1, rows_in[1], far_rows[1][...].astype(F32))

    def load(n, source):
        return pltpu.make_async_copy(source, stage.at[n], in_sems.at[n])

    def store(n, p, which):
        pool = (key_out, value_out)[which]
        page = table[0, p, cases[n][0]]
        return pltpu.make_async_copy(stage.at[n, which * pages + p], pool.at[page], out_sems.at[n, which, p])

    def each(do):
        for n in range(2):

            @pl.when(cases[n][0] >= 0)
            def _():
                do(n)

    def fetch(n):
        if n == 0 or ways == 1:
            load(n, pages_in[n]).start()
            return
        for way in range(ways):

            @pl.when((far_gap == 1) == (way == 0))
            def _():
                load(n, far_pages[way]).start()

    def patch(n):
        _, length = cases[n]
        load(n, pages_in[n]).wait()
        for p in range(pages):
            at = row + p * page_len
            for which in range(2):
                page = stage[n, which * pages + p].astype(F32)
                page = jnp.where(at < length, page, 0.0)
                for t in range(steps):
                    low = width + which * head_dim
                    page = jnp.where(at == length + t, rows_in[n][t : t + 1, low : low + head_dim], page)
                stage[n, which * pages + p] = page.astype(BF16)
                store(n, p, which).start()

    def finish(n):
        for p in range(pages):
            for which in range(2):
                store(n, p, which).wait()

    each(fetch)
    for s in range(slot_count):
        live = (lens[me, s] > 0) & (s != out_near) & (s != out_far)
        mixed[s] = jnp.where(live, total[s * steps : (s + 1) * steps, :].astype(F32), 0.0).astype(BF16)

    def mix(n):
        mixed[cases[n][0]] = rows_in[n][:, :width].astype(BF16)

    each(mix)
    each(patch)
    each(finish)


def run(
    near_hops,
    far_hops,
    table,
    token_states,
    query_rows,
    key_weight,
    value_weight,
    out_weight,
    keys,
    values,
    cached_len,
    migrations,
):
    groups = lax.axis_size("dec")
    tp = lax.axis_size("tp")
    slot_count, steps, model = token_states.shape
    _, page_len, head_dim = keys.shape
    rows = slot_count * steps
    width = out_weight.shape[1]
    heads = query_rows.shape[2] // head_dim
    pages = table.shape[1]
    pool_shape = jax.ShapeDtypeStruct(keys.shape, BF16)
    moved_shape = jax.ShapeDtypeStruct((2 * pages, page_len, head_dim), BF16)
    limit = pltpu.CompilerParams(vmem_limit_bytes=63 * 2**20)

    near, far, token = pl.pallas_call(
        functools.partial(pack_kernel, groups),
        out_shape=(moved_shape, moved_shape, jax.ShapeDtypeStruct((1,), jnp.int32)),
        in_specs=[SMEM, SMEM, HBM, HBM],
        out_specs=(HBM, HBM, SMEM),
        scratch_shapes=[
            pltpu.VMEM((2, 2 * pages, page_len, head_dim), BF16),
            pltpu.SemaphoreType.DMA((2, 2, pages)),
            pltpu.SemaphoreType.DMA((2,)),
        ],
        compiler_params=limit,
        name="pack",
    )(migrations, table, keys, values)
    pages_in = [lax.ppermute(near, "dec", near_hops)] + [lax.ppermute(far, "dec", hops) for hops in far_hops]

    key_mid, value_mid, partial, new_rows = pl.pallas_call(
        functools.partial(attend_kernel, groups),
        out_shape=(
            pool_shape,
            pool_shape,
            jax.ShapeDtypeStruct((rows, width), BF16),
            jax.ShapeDtypeStruct((rows, 2 * head_dim), BF16),
        ),
        in_specs=[SMEM, SMEM, SMEM, SMEM, VMEM, VMEM, HBM, HBM, HBM, HBM, HBM],
        out_specs=(HBM, HBM, VMEM, VMEM),
        scratch_shapes=[
            pltpu.VMEM(key_weight.shape, BF16),
            pltpu.VMEM(value_weight.shape, BF16),
            pltpu.VMEM(out_weight.shape, BF16),
            pltpu.VMEM(keys.shape, BF16),
            pltpu.VMEM(values.shape, BF16),
            pltpu.VMEM((heads * rows, head_dim), F32),
            pltpu.VMEM((heads * rows, head_dim), F32),
            pltpu.VMEM((rows, 2 * head_dim), F32),
            pltpu.SemaphoreType.DMA((5,)),
        ],
        compiler_params=limit,
        cost_estimate=pl.CostEstimate(flops=1_000_000, bytes_accessed=1_000_000, transcendentals=0),
        name="attend",
    )(
        token,
        migrations,
        cached_len,
        table,
        token_states,
        query_rows,
        key_weight,
        value_weight,
        out_weight,
        keys,
        values,
    )

    others = [lax.ppermute(partial, "tp", [(i, i ^ n) for i in range(tp)]) for n in range(1, tp)]
    row_shape = jax.ShapeDtypeStruct((steps, width + 2 * head_dim), BF16)
    total, near_row, far_row = pl.pallas_call(
        functools.partial(finish_rows_kernel, groups),
        out_shape=(jax.ShapeDtypeStruct((rows, width), BF16), row_shape, row_shape),
        in_specs=[SMEM, VMEM] + [VMEM] * tp,
        out_specs=(VMEM, VMEM, VMEM),
        scratch_shapes=[pltpu.VMEM((slot_count, steps, width + 2 * head_dim), F32)],
        compiler_params=limit,
        name="rows",
    )(migrations, new_rows, partial, *others)
    rows_in = [lax.ppermute(near_row, "dec", near_hops)] + [lax.ppermute(far_row, "dec", hops) for hops in far_hops]
    return pages_in, rows_in, total, key_mid, value_mid


def moved(table, inputs):
    groups = lax.axis_size("dec")
    half = groups // 2
    if half != 2:
        return run(shifted(groups, half), (shifted(groups, 1), shifted(groups, 1 + half)), table, *inputs)
    source_group = inputs[-1][:, 0]
    second = [jnp.any(source_group == pair + half) for pair in range(half)]
    branches = []
    for case in range(2**half):
        senders = [pair + half * (case >> pair & 1) for pair in range(half)]
        receivers = [(sender + half) % groups for sender in senders]
        near_hops = [(senders[pair], receivers[pair]) for pair in range(half)]
        far_hops = [(senders[pair], receivers[(pair + 1) % half]) for pair in range(half)]
        branches.append(functools.partial(run, near_hops, (far_hops,)))
    number = sum(bit.astype(jnp.int32) << pair for pair, bit in enumerate(second))
    return lax.switch(number, branches, table, *inputs)


def local(
    token_states,
    query_rows,
    key_weight,
    value_weight,
    out_weight,
    key_pool,
    value_pool,
    cached_len,
    page_table,
    migrations,
):
    groups = lax.axis_size("dec")
    pool_pages, _, page_len, head_dim = key_pool.shape
    slot_count, steps, _ = token_states.shape
    keys = key_pool.reshape(pool_pages, page_len, head_dim)
    values = value_pool.reshape(pool_pages, page_len, head_dim)
    table = jnp.swapaxes(page_table, 1, 2)
    pages = table.shape[1]
    inputs = (
        token_states,
        query_rows,
        key_weight,
        value_weight,
        out_weight,
        keys,
        values,
        cached_len,
        migrations,
    )
    pages_in, rows_in, total, key_mid, value_mid = moved(table, inputs)
    ways = len(pages_in) - 1
    pool_shape = jax.ShapeDtypeStruct(keys.shape, BF16)
    mixed_shape = jax.ShapeDtypeStruct((slot_count, steps, out_weight.shape[1]), BF16)
    mixed, key_out, value_out = pl.pallas_call(
        functools.partial(place_kernel, groups, ways),
        out_shape=(mixed_shape, pool_shape, pool_shape),
        in_specs=[SMEM] * 3 + [ANY] * (1 + ways) + [VMEM] * (2 + ways) + [HBM] * 2,
        out_specs=(VMEM, HBM, HBM),
        scratch_shapes=[
            pltpu.VMEM((2, 2 * pages, page_len, head_dim), BF16),
            pltpu.SemaphoreType.DMA((2,)),
            pltpu.SemaphoreType.DMA((2, 2, pages)),
        ],
        input_output_aliases={6 + 2 * ways: 1, 7 + 2 * ways: 2},
        compiler_params=pltpu.CompilerParams(vmem_limit_bytes=63 * 2**20),
        name="place",
    )(migrations, cached_len, table, *pages_in, *rows_in, total, key_mid, value_mid)
    return mixed, key_out.reshape(key_pool.shape), value_out.reshape(value_pool.shape)


def solution(mesh):
    placed = (
        P(("rep", "dec"), None, None),
        P(("rep", "dec"), None, "tp"),
        P(None, "tp"),
        P(None, "tp"),
        P("tp", None),
        P(("rep", "dec"), "tp", None, None),
        P(("rep", "dec"), "tp", None, None),
        P("rep", None),
        P(("rep", "dec"), None, None),
        P("rep", None),
    )
    return jax.shard_map(
        local,
        mesh=mesh,
        in_specs=placed,
        out_specs=(
            P(("rep", "dec"), None, None),
            P(("rep", "dec"), "tp", None, None),
            P(("rep", "dec"), "tp", None, None),
        ),
        check_vma=False,
    )
```

```python
import functools

import jax
import jax.numpy as jnp
from jax import lax
from jax.experimental import pallas as pl
from jax.experimental.pallas import tpu as pltpu
from jax.sharding import PartitionSpec as P

F32 = jnp.float32
BF16 = jnp.bfloat16
SMEM = pl.BlockSpec(memory_space=pltpu.SMEM)
HBM = pl.BlockSpec(memory_space=pltpu.HBM)
ANY = pl.BlockSpec(memory_space=pl.ANY)
VMEM = pl.BlockSpec(memory_space=pltpu.VMEM)


def shifted(count, by):
    return [(i, (i + by) % count) for i in range(count)]


def outgoing(mig, me, groups):
    half = groups // 2
    near = far = jnp.int32(-1)
    for m in range(mig.shape[0]):
        mine = mig[m, 0] == me
        gap = lax.rem(mig[m, 2] - me + groups, groups)
        near = jnp.where(mine & (gap == half), mig[m, 1], near)
        far = jnp.where(mine & (gap != half), mig[m, 1], far)
    return near, far


def incoming(mig, lens, me, groups):
    half = groups // 2
    near = far = jnp.int32(-1)
    near_len = far_len = far_gap = jnp.int32(0)
    for m in range(mig.shape[0]):
        mine = mig[m, 2] == me
        gap = lax.rem(me - mig[m, 0] + groups, groups)
        length = lens[mig[m, 0], mig[m, 1]]
        is_near = mine & (gap == half)
        is_far = mine & (gap != half)
        near = jnp.where(is_near, mig[m, 3], near)
        near_len = jnp.where(is_near, length, near_len)
        far = jnp.where(is_far, mig[m, 3], far)
        far_len = jnp.where(is_far, length, far_len)
        far_gap = jnp.where(is_far, gap, far_gap)
    return (near, near_len), (far, far_len), far_gap


def pack_kernel(groups, mig, table, key_pool, value_pool, near_out, far_out, token, sems):
    me = lax.axis_index("dec")
    pages = table.shape[1]
    outs = (near_out, far_out)
    slots = outgoing(mig, me, groups)

    def load(n, which, p):
        page = table[0, p, slots[n]]
        pool = (key_pool, value_pool)[which]
        return pltpu.make_async_copy(pool.at[page], outs[n].at[which * pages + p], sems.at[n, which, p])

    def each(do):
        for n in range(2):

            @pl.when(slots[n] >= 0)
            def _():
                for p in range(pages):
                    for which in range(2):
                        do(load(n, which, p))

    each(lambda copy: copy.start())
    token[0] = me
    each(lambda copy: copy.wait())


def attend_kernel(
    groups,
    token,
    mig,
    lens,
    table,
    states,
    query,
    key_weight,
    value_weight,
    out_weight,
    key_pool,
    value_pool,
    key_out,
    value_out,
    partial,
    new_rows,
    wkv,
    wo,
    kp,
    vp,
    q_scr,
    a_scr,
    n_scr,
    sems,
):
    del token
    me = lax.axis_index("dec")
    slot_count, steps, _ = states.shape
    rows = slot_count * steps
    pages = table.shape[1]
    page_len, head_dim = kp.shape[1:]
    heads = query.shape[2] // head_dim
    span = pages * page_len
    load_keys = pltpu.make_async_copy(key_pool, kp, sems.at[0])
    load_values = pltpu.make_async_copy(value_pool, vp, sems.at[1])
    load_wk = pltpu.make_async_copy(key_weight, wkv.at[:, :head_dim], sems.at[2])
    load_wv = pltpu.make_async_copy(value_weight, wkv.at[:, head_dim:], sems.at[3])
    load_wo = pltpu.make_async_copy(out_weight, wo, sems.at[4])
    for load in (load_keys, load_wk, load_wv, load_values, load_wo):
        load.start()
    near, far = outgoing(mig, me, groups)
    lengths = [lens[me, s] for s in range(slot_count)]

    for s in range(slot_count):
        qf = query[s].astype(F32)
        for h in range(heads):
            q_scr[pl.ds(h * rows + s * steps, steps), :] = qf[:, h * head_dim : (h + 1) * head_dim]
    x = jnp.concatenate([states[s].astype(F32) for s in range(slot_count)], 0).astype(BF16)
    queries = [
        jnp.concatenate(
            [q_scr[pl.ds(s * steps + t, heads, stride=rows), :] for t in range(steps)], 0
        ).astype(BF16)
        for s in range(slot_count)
    ]

    scaling = head_dim**-0.5
    count = steps * heads
    fresh_col = lax.broadcasted_iota(jnp.int32, (count, rows), 1)
    fresh_step = lax.broadcasted_iota(jnp.int32, (count, rows), 0) // heads
    position = lax.broadcasted_iota(jnp.int32, (count, span), 1)
    nt = (((1,), (1,)), ((), ()))
    numbers = [[table[0, p, s] for p in range(pages)] for s in range(slot_count)]
    load_keys.wait()
    scores = []
    for s in range(slot_count):
        keys = jnp.concatenate([kp[n] for n in numbers[s]], 0)
        cached = lax.dot_general(queries[s], keys, nt, preferred_element_type=F32) * scaling
        scores.append(jnp.where(position < lengths[s], cached, -jnp.inf))

    load_wk.wait()
    load_wv.wait()
    fresh_rows = jnp.dot(x, wkv[...], preferred_element_type=F32).astype(BF16)
    new_rows[...] = fresh_rows
    n_scr[...] = fresh_rows.astype(F32)
    new_k = fresh_rows[:, :head_dim]
    new_v = fresh_rows[:, head_dim:]

    load_values.wait()
    for s in range(slot_count):
        values = jnp.concatenate([vp[n] for n in numbers[s]], 0)
        cached = scores[s]
        fresh = lax.dot_general(queries[s], new_k, nt, preferred_element_type=F32) * scaling
        ok = (fresh_col >= s * steps) & (fresh_col <= s * steps + fresh_step)
        fresh = jnp.where(ok, fresh, -jnp.inf)
        peak = jnp.maximum(jnp.max(cached, 1, keepdims=True), jnp.max(fresh, 1, keepdims=True))
        cached = jnp.exp(cached - peak)
        fresh = jnp.exp(fresh - peak)
        total = jnp.sum(cached, 1, keepdims=True) + jnp.sum(fresh, 1, keepdims=True)
        cached_w = (cached / total).astype(BF16)
        fresh_w = (fresh / total).astype(BF16)
        out = jnp.dot(cached_w, values, preferred_element_type=F32)
        out = out + jnp.dot(fresh_w, new_v, preferred_element_type=F32)
        for t in range(steps):
            a_scr[pl.ds(s * steps + t, heads, stride=rows), :] = out[t * heads : (t + 1) * heads]

    tile = 16
    row = lax.broadcasted_iota(jnp.int32, (tile, head_dim), 0)
    tiles = []
    for s in range(slot_count):
        live = (lengths[s] > 0) & (s != near) & (s != far)
        first = jnp.where(live, lengths[s], -steps)
        for t in range(steps):
            at = lengths[s] + t
            page = table[0, at // page_len, s]
            low = at // tile * tile
            base = pl.multiple_of(lax.rem(low, page_len), tile)
            for pool, side in ((kp, 0), (vp, head_dim)):
                merged = pool[page, pl.ds(base, tile), :].astype(F32)
                for u in range(steps):
                    fresh_row = n_scr[s * steps + u : s * steps + u + 1, side : side + head_dim]
                    merged = jnp.where(row + low == first + u, fresh_row, merged)
                tiles.append((pool, page, base, merged.astype(BF16)))
    for pool, page, base, merged in tiles:
        pool[page, pl.ds(base, tile), :] = merged

    stores = [
        pltpu.make_async_copy(kp, key_out, sems.at[0]),
        pltpu.make_async_copy(vp, value_out, sems.at[1]),
    ]
    for store in stores:
        store.start()
    attention = jnp.concatenate([a_scr[h * rows : (h + 1) * rows, :].astype(BF16) for h in range(heads)], 1)
    load_wo.wait()
    partial[...] = jnp.dot(attention, wo[...], preferred_element_type=F32).astype(BF16)
    for store in stores:
        store.wait()


def finish_rows_kernel(groups, mig, lens, new_rows, *refs):
    *parts, mixed, near_out, far_out, scr = refs
    me = lax.axis_index("dec")
    slots = outgoing(mig, me, groups)
    width = parts[0].shape[1]
    terms = [part[...].astype(F32) for part in parts]
    level = 1
    while level < len(terms):
        terms = [terms[n] + terms[n ^ level] for n in range(len(terms))]
        level *= 2
    total = terms[0]
    slot_count, steps, _ = scr.shape
    for s in range(slot_count):
        live = (lens[me, s] > 0) & (s != slots[0]) & (s != slots[1])
        own = total[s * steps : (s + 1) * steps]
        scr[s, :, :width] = own
        scr[s, :, width:] = new_rows[s * steps : (s + 1) * steps, :].astype(F32)
        mixed[s] = jnp.where(live, own, 0.0).astype(BF16)
    for slot, out in zip(slots, (near_out, far_out)):
        out[...] = scr[jnp.maximum(slot, 0)].astype(BF16)


def place_kernel(groups, ways, mig, lens, table, *refs):
    near_pages, *far_pages = refs[: 1 + ways]
    near_rows, *far_rows = refs[1 + ways : 2 + 2 * ways]
    _, _, _, mixed, key_out, value_out, stage, lines, in_sems, line_sems, out_sems = refs[2 + 2 * ways :]
    me = lax.axis_index("dec")
    pages = table.shape[1]
    page_len, head_dim = stage.shape[2:]
    _, steps, width = mixed.shape
    *cases, far_gap = incoming(mig, lens, me, groups)
    row = lax.broadcasted_iota(jnp.int32, (page_len, head_dim), 0)

    def load(n, source):
        return pltpu.make_async_copy(source, stage.at[n], in_sems.at[n])

    def load_line(n, source):
        return pltpu.make_async_copy(source, lines.at[n], line_sems.at[n, 0])

    def store_line(n):
        return pltpu.make_async_copy(
            lines.at[n, :, pl.ds(0, width)], mixed.at[cases[n][0]], line_sems.at[n, 1]
        )

    def store(n, p, which):
        pool = (key_out, value_out)[which]
        page = table[0, p, cases[n][0]]
        return pltpu.make_async_copy(stage.at[n, which * pages + p], pool.at[page], out_sems.at[n, which, p])

    def each(do):
        for n in range(2):

            @pl.when(cases[n][0] >= 0)
            def _():
                do(n)

    def start(n):
        if n == 0 or ways == 1:
            load_line(n, (near_rows, far_rows[0])[n]).start()
            load(n, (near_pages, far_pages[0])[n]).start()
            return
        for way in range(ways):

            @pl.when((far_gap == 1) == (way == 0))
            def _():
                load_line(n, far_rows[way]).start()
                load(n, far_pages[way]).start()

    def patch(n):
        _, length = cases[n]
        load_line(n, near_rows).wait()
        store_line(n).start()
        fresh = lines[n, :, width:].astype(F32)
        load(n, near_pages).wait()
        for p in range(pages):
            at = row + p * page_len
            for which in range(2):
                page = stage[n, which * pages + p].astype(F32)
                page = jnp.where(at < length, page, 0.0)
                for t in range(steps):
                    page = jnp.where(
                        at == length + t, fresh[t : t + 1, which * head_dim : (which + 1) * head_dim], page
                    )
                stage[n, which * pages + p] = page.astype(BF16)
                store(n, p, which).start()

    def finish(n):
        store_line(n).wait()
        for p in range(pages):
            for which in range(2):
                store(n, p, which).wait()

    each(start)
    each(patch)
    each(finish)


def run(
    near_hops,
    far_hops,
    table,
    token_states,
    query_rows,
    key_weight,
    value_weight,
    out_weight,
    keys,
    values,
    cached_len,
    migrations,
):
    groups = lax.axis_size("dec")
    tp = lax.axis_size("tp")
    slot_count, steps, model = token_states.shape
    _, page_len, head_dim = keys.shape
    rows = slot_count * steps
    width = out_weight.shape[1]
    heads = query_rows.shape[2] // head_dim
    pages = table.shape[1]
    pool_shape = jax.ShapeDtypeStruct(keys.shape, BF16)
    moved_shape = jax.ShapeDtypeStruct((2 * pages, page_len, head_dim), BF16)
    limit = pltpu.CompilerParams(vmem_limit_bytes=63 * 2**20)

    near, far, token = pl.pallas_call(
        functools.partial(pack_kernel, groups),
        out_shape=(moved_shape, moved_shape, jax.ShapeDtypeStruct((1,), jnp.int32)),
        in_specs=[SMEM, SMEM, HBM, HBM],
        out_specs=(VMEM, VMEM, SMEM),
        scratch_shapes=[pltpu.SemaphoreType.DMA((2, 2, pages))],
        compiler_params=limit,
        name="pack",
    )(migrations, table, keys, values)
    pages_in = [lax.ppermute(near, "dec", near_hops)] + [lax.ppermute(far, "dec", hops) for hops in far_hops]

    key_mid, value_mid, partial, new_rows = pl.pallas_call(
        functools.partial(attend_kernel, groups),
        out_shape=(
            pool_shape,
            pool_shape,
            jax.ShapeDtypeStruct((rows, width), BF16),
            jax.ShapeDtypeStruct((rows, 2 * head_dim), BF16),
        ),
        in_specs=[SMEM, SMEM, SMEM, SMEM, VMEM, VMEM, HBM, HBM, HBM, HBM, HBM],
        out_specs=(HBM, HBM, VMEM, VMEM),
        scratch_shapes=[
            pltpu.VMEM((model, 2 * head_dim), BF16),
            pltpu.VMEM(out_weight.shape, BF16),
            pltpu.VMEM(keys.shape, BF16),
            pltpu.VMEM(values.shape, BF16),
            pltpu.VMEM((heads * rows, head_dim), F32),
            pltpu.VMEM((heads * rows, head_dim), F32),
            pltpu.VMEM((rows, 2 * head_dim), F32),
            pltpu.SemaphoreType.DMA((5,)),
        ],
        compiler_params=limit,
        cost_estimate=pl.CostEstimate(flops=1_000_000, bytes_accessed=1_000_000, transcendentals=0),
        name="attend",
    )(
        token,
        migrations,
        cached_len,
        table,
        token_states,
        query_rows,
        key_weight,
        value_weight,
        out_weight,
        keys,
        values,
    )

    others = [lax.ppermute(partial, "tp", [(i, i ^ n) for i in range(tp)]) for n in range(1, tp)]
    row_shape = jax.ShapeDtypeStruct((steps, width + 2 * head_dim), BF16)
    mixed, near_row, far_row = pl.pallas_call(
        functools.partial(finish_rows_kernel, groups),
        out_shape=(jax.ShapeDtypeStruct((slot_count, steps, width), BF16), row_shape, row_shape),
        in_specs=[SMEM, SMEM, VMEM] + [VMEM] * tp,
        out_specs=(VMEM, VMEM, VMEM),
        scratch_shapes=[pltpu.VMEM((slot_count, steps, width + 2 * head_dim), F32)],
        compiler_params=pltpu.CompilerParams(vmem_limit_bytes=8 * 2**20),
        name="rows",
    )(migrations, cached_len, new_rows, partial, *others)
    rows_in = [lax.ppermute(near_row, "dec", near_hops)] + [lax.ppermute(far_row, "dec", hops) for hops in far_hops]
    return pages_in, rows_in, mixed, key_mid, value_mid


def moved(table, inputs):
    groups = lax.axis_size("dec")
    half = groups // 2
    if half != 2:
        return run(shifted(groups, half), (shifted(groups, 1), shifted(groups, 1 + half)), table, *inputs)
    source_group = inputs[-1][:, 0]
    branches = []
    for case in range(2**half):
        senders = [pair + half * (case >> pair & 1) for pair in range(half)]
        receivers = [(sender + half) % groups for sender in senders]
        near_hops = [(senders[pair], receivers[pair]) for pair in range(half)]
        far_hops = [(senders[pair], receivers[(pair + 1) % half]) for pair in range(half)]
        near_hops += [(b, a) for a, b in near_hops]
        far_hops += [(b, a) for a, b in far_hops]
        branches.append(functools.partial(run, near_hops, (far_hops,)))
    number = jnp.sum(jnp.where(source_group >= half, 1 + (source_group & 1), 0)) // 2
    return lax.switch(number, branches, table, *inputs)


def local(
    token_states,
    query_rows,
    key_weight,
    value_weight,
    out_weight,
    key_pool,
    value_pool,
    cached_len,
    page_table,
    migrations,
):
    groups = lax.axis_size("dec")
    pool_pages, _, page_len, head_dim = key_pool.shape
    slot_count, steps, _ = token_states.shape
    keys = key_pool.reshape(pool_pages, page_len, head_dim)
    values = value_pool.reshape(pool_pages, page_len, head_dim)
    table = jnp.swapaxes(page_table, 1, 2)
    pages = table.shape[1]
    inputs = (
        token_states,
        query_rows,
        key_weight,
        value_weight,
        out_weight,
        keys,
        values,
        cached_len,
        migrations,
    )
    pages_in, rows_in, mixed_mid, key_mid, value_mid = moved(table, inputs)
    ways = len(pages_in) - 1
    pool_shape = jax.ShapeDtypeStruct(keys.shape, BF16)
    mixed_shape = jax.ShapeDtypeStruct((slot_count, steps, out_weight.shape[1]), BF16)
    mixed, key_out, value_out = pl.pallas_call(
        functools.partial(place_kernel, groups, ways),
        out_shape=(mixed_shape, pool_shape, pool_shape),
        in_specs=[SMEM] * 3 + [ANY] * (2 + 2 * ways) + [HBM] * 3,
        out_specs=(HBM, HBM, HBM),
        scratch_shapes=[
            pltpu.VMEM((2, 2 * pages, page_len, head_dim), BF16),
            pltpu.VMEM((2,) + rows_in[0].shape, BF16),
            pltpu.SemaphoreType.DMA((2,)),
            pltpu.SemaphoreType.DMA((2, 2)),
            pltpu.SemaphoreType.DMA((2, 2, pages)),
        ],
        input_output_aliases={5 + 2 * ways: 0, 6 + 2 * ways: 1, 7 + 2 * ways: 2},
        compiler_params=pltpu.CompilerParams(vmem_limit_bytes=255 * 2**18),
        name="place",
    )(migrations, cached_len, table, *pages_in, *rows_in, mixed_mid, key_mid, value_mid)
    return mixed, key_out.reshape(key_pool.shape), value_out.reshape(value_pool.shape)


def solution(mesh):
    placed = (
        P(("rep", "dec"), None, None),
        P(("rep", "dec"), None, "tp"),
        P(None, "tp"),
        P(None, "tp"),
        P("tp", None),
        P(("rep", "dec"), "tp", None, None),
        P(("rep", "dec"), "tp", None, None),
        P("rep", None),
        P(("rep", "dec"), None, None),
        P("rep", None),
    )
    return jax.shard_map(
        local,
        mesh=mesh,
        in_specs=placed,
        out_specs=(
            P(("rep", "dec"), None, None),
            P(("rep", "dec"), "tp", None, None),
            P(("rep", "dec"), "tp", None, None),
        ),
        check_vma=False,
    )
```

```python
import functools

import jax
import jax.numpy as jnp
from jax import lax
from jax.experimental import pallas as pl
from jax.experimental.pallas import tpu as pltpu
from jax.sharding import PartitionSpec as P

F32 = jnp.float32
BF16 = jnp.bfloat16
PARTS = 4
SMEM = pl.BlockSpec(memory_space=pltpu.SMEM)
HBM = pl.BlockSpec(memory_space=pltpu.HBM)
ANY = pl.BlockSpec(memory_space=pl.ANY)
VMEM = pl.BlockSpec(memory_space=pltpu.VMEM)


def shifted(count, by):
    return [(i, (i + by) % count) for i in range(count)]


def outgoing(mig, me, groups):
    half = groups // 2
    near = far = jnp.int32(-1)
    for m in range(mig.shape[0]):
        mine = mig[m, 0] == me
        gap = lax.rem(mig[m, 2] - me + groups, groups)
        near = jnp.where(mine & (gap == half), mig[m, 1], near)
        far = jnp.where(mine & (gap != half), mig[m, 1], far)
    return near, far


def incoming(mig, lens, me, groups):
    half = groups // 2
    near = far = jnp.int32(-1)
    near_len = far_len = far_gap = jnp.int32(0)
    for m in range(mig.shape[0]):
        mine = mig[m, 2] == me
        gap = lax.rem(me - mig[m, 0] + groups, groups)
        length = lens[mig[m, 0], mig[m, 1]]
        is_near = mine & (gap == half)
        is_far = mine & (gap != half)
        near = jnp.where(is_near, mig[m, 3], near)
        near_len = jnp.where(is_near, length, near_len)
        far = jnp.where(is_far, mig[m, 3], far)
        far_len = jnp.where(is_far, length, far_len)
        far_gap = jnp.where(is_far, gap, far_gap)
    return (near, near_len), (far, far_len), far_gap


def pack_kernel(groups, mig, table, key_pool, value_pool, near_out, far_out, token, sems):
    me = lax.axis_index("dec")
    pages = table.shape[1]
    outs = (near_out, far_out)
    slots = outgoing(mig, me, groups)

    def load(n, which, p):
        page = table[0, p, slots[n]]
        pool = (key_pool, value_pool)[which]
        return pltpu.make_async_copy(pool.at[page], outs[n].at[which * pages + p], sems.at[n, which, p])

    def each(do):
        for n in range(2):

            @pl.when(slots[n] >= 0)
            def _():
                for p in range(pages):
                    for which in range(2):
                        do(load(n, which, p))

    each(lambda copy: copy.start())
    token[0] = me
    each(lambda copy: copy.wait())


def attend_kernel(
    groups,
    token,
    mig,
    lens,
    table,
    states,
    query,
    key_weight,
    value_weight,
    out_weight,
    key_pool,
    value_pool,
    key_out,
    value_out,
    partial,
    new_rows,
    wk,
    wv,
    wo,
    kp,
    vp,
    q_scr,
    a_scr,
    n_scr,
    sems,
):
    del token
    me = lax.axis_index("dec")
    slot_count, steps, _ = states.shape
    rows = slot_count * steps
    pages = table.shape[1]
    page_len, head_dim = kp.shape[1:]
    heads = query.shape[2] // head_dim
    span = pages * page_len
    number = 0

    def split(source, target, parts):
        nonlocal number
        size = source.shape[0] // parts
        copies = []
        for part in range(parts):
            piece = pl.ds(part * size, size)
            copies.append(pltpu.make_async_copy(source.at[piece], target.at[piece], sems.at[number]))
            number += 1
        return copies

    load_keys = split(key_pool, kp, PARTS)
    load_wk = split(key_weight, wk, PARTS)
    load_wv = split(value_weight, wv, PARTS)
    load_values = split(value_pool, vp, PARTS)
    load_wo = split(out_weight, wo, PARTS)
    for load in load_keys + load_wk + load_wv + load_values + load_wo:
        load.start()
    near, far = outgoing(mig, me, groups)
    lengths = [lens[me, s] for s in range(slot_count)]

    for s in range(slot_count):
        qf = query[s].astype(F32)
        for h in range(heads):
            q_scr[pl.ds(h * rows + s * steps, steps), :] = qf[:, h * head_dim : (h + 1) * head_dim]
    x = jnp.concatenate([states[s].astype(F32) for s in range(slot_count)], 0).astype(BF16)
    queries = [
        jnp.concatenate(
            [q_scr[pl.ds(s * steps + t, heads, stride=rows), :] for t in range(steps)], 0
        ).astype(BF16)
        for s in range(slot_count)
    ]

    scaling = head_dim**-0.5
    count = steps * heads
    fresh_col = lax.broadcasted_iota(jnp.int32, (count, rows), 1)
    fresh_step = lax.broadcasted_iota(jnp.int32, (count, rows), 0) // heads
    position = lax.broadcasted_iota(jnp.int32, (count, span), 1)
    nt = (((1,), (1,)), ((), ()))
    numbers = [[table[0, p, s] for p in range(pages)] for s in range(slot_count)]
    for load in load_keys:
        load.wait()
    scores = []
    for s in range(slot_count):
        keys = jnp.concatenate([kp[n] for n in numbers[s]], 0)
        cached = lax.dot_general(queries[s], keys, nt, preferred_element_type=F32) * scaling
        scores.append(jnp.where(position < lengths[s], cached, -jnp.inf))

    fresh_k = jnp.zeros((rows, head_dim), F32)
    fresh_v = jnp.zeros((rows, head_dim), F32)
    size = wk.shape[0] // PARTS
    for part in range(PARTS):
        piece = slice(part * size, (part + 1) * size)
        load_wk[part].wait()
        fresh_k = fresh_k + jnp.dot(x[:, piece], wk[piece, :], preferred_element_type=F32)
        load_wv[part].wait()
        fresh_v = fresh_v + jnp.dot(x[:, piece], wv[piece, :], preferred_element_type=F32)
    fresh_rows = jnp.concatenate([fresh_k, fresh_v], 1).astype(BF16)
    new_rows[...] = fresh_rows
    n_scr[...] = fresh_rows.astype(F32)
    new_k = fresh_rows[:, :head_dim]
    new_v = fresh_rows[:, head_dim:]

    for load in load_values:
        load.wait()
    for s in range(slot_count):
        values = jnp.concatenate([vp[n] for n in numbers[s]], 0)
        cached = scores[s]
        fresh = lax.dot_general(queries[s], new_k, nt, preferred_element_type=F32) * scaling
        ok = (fresh_col >= s * steps) & (fresh_col <= s * steps + fresh_step)
        fresh = jnp.where(ok, fresh, -jnp.inf)
        peak = jnp.maximum(jnp.max(cached, 1, keepdims=True), jnp.max(fresh, 1, keepdims=True))
        cached = jnp.exp(cached - peak)
        fresh = jnp.exp(fresh - peak)
        total = jnp.sum(cached, 1, keepdims=True) + jnp.sum(fresh, 1, keepdims=True)
        cached_w = (cached / total).astype(BF16)
        fresh_w = (fresh / total).astype(BF16)
        out = jnp.dot(cached_w, values, preferred_element_type=F32)
        out = out + jnp.dot(fresh_w, new_v, preferred_element_type=F32)
        for t in range(steps):
            a_scr[pl.ds(s * steps + t, heads, stride=rows), :] = out[t * heads : (t + 1) * heads]

    tile = 16
    row = lax.broadcasted_iota(jnp.int32, (tile, head_dim), 0)
    tiles = []
    for s in range(slot_count):
        live = (lengths[s] > 0) & (s != near) & (s != far)
        first = jnp.where(live, lengths[s], -steps)
        for t in range(steps):
            at = lengths[s] + t
            page = table[0, at // page_len, s]
            low = at // tile * tile
            base = pl.multiple_of(lax.rem(low, page_len), tile)
            for pool, side in ((kp, 0), (vp, head_dim)):
                merged = pool[page, pl.ds(base, tile), :].astype(F32)
                for u in range(steps):
                    fresh_row = n_scr[s * steps + u : s * steps + u + 1, side : side + head_dim]
                    merged = jnp.where(row + low == first + u, fresh_row, merged)
                tiles.append((pool, page, base, merged.astype(BF16)))
    for pool, page, base, merged in tiles:
        pool[page, pl.ds(base, tile), :] = merged

    stores = [
        pltpu.make_async_copy(kp, key_out, sems.at[0]),
        pltpu.make_async_copy(vp, value_out, sems.at[1]),
    ]
    for store in stores:
        store.start()
    attention = jnp.concatenate([a_scr[h * rows : (h + 1) * rows, :].astype(BF16) for h in range(heads)], 1)
    result = jnp.zeros((rows, wo.shape[1]), F32)
    size = wo.shape[0] // PARTS
    for part in range(PARTS):
        piece = slice(part * size, (part + 1) * size)
        load_wo[part].wait()
        result = result + jnp.dot(attention[:, piece], wo[piece, :], preferred_element_type=F32)
    partial[...] = result.astype(BF16)
    for store in stores:
        store.wait()


def finish_rows_kernel(groups, mig, lens, new_rows, *refs):
    *parts, mixed, near_out, far_out, scr = refs
    me = lax.axis_index("dec")
    slots = outgoing(mig, me, groups)
    width = parts[0].shape[1]
    terms = [part[...].astype(F32) for part in parts]
    level = 1
    while level < len(terms):
        terms = [terms[n] + terms[n ^ level] for n in range(len(terms))]
        level *= 2
    total = terms[0]
    slot_count, steps, _ = scr.shape
    for s in range(slot_count):
        live = (lens[me, s] > 0) & (s != slots[0]) & (s != slots[1])
        own = total[s * steps : (s + 1) * steps]
        scr[s, :, :width] = own
        scr[s, :, width:] = new_rows[s * steps : (s + 1) * steps, :].astype(F32)
        mixed[s] = jnp.where(live, own, 0.0).astype(BF16)
    for slot, out in zip(slots, (near_out, far_out)):
        out[...] = scr[jnp.maximum(slot, 0)].astype(BF16)


def place_kernel(groups, ways, mig, lens, table, *refs):
    near_pages, *far_pages = refs[: 1 + ways]
    near_rows, *far_rows = refs[1 + ways : 2 + 2 * ways]
    mixed_in, _, _, mixed, key_out, value_out, stage, lines, in_sems, line_sems, out_sems, own_sem = refs[
        2 + 2 * ways :
    ]
    me = lax.axis_index("dec")
    pages = table.shape[1]
    page_len, head_dim = stage.shape[2:]
    _, steps, width = mixed.shape
    *cases, far_gap = incoming(mig, lens, me, groups)
    row = lax.broadcasted_iota(jnp.int32, (page_len, head_dim), 0)

    def load(n, source):
        return pltpu.make_async_copy(source, stage.at[n], in_sems.at[n])

    def load_line(n, source):
        return pltpu.make_async_copy(source, lines.at[n], line_sems.at[n, 0])

    def store_line(n):
        return pltpu.make_async_copy(
            lines.at[n, :, pl.ds(0, width)], mixed.at[cases[n][0]], line_sems.at[n, 1]
        )

    def store(n, p, which):
        pool = (key_out, value_out)[which]
        page = table[0, p, cases[n][0]]
        return pltpu.make_async_copy(stage.at[n, which * pages + p], pool.at[page], out_sems.at[n, which, p])

    def each(do):
        for n in range(2):

            @pl.when(cases[n][0] >= 0)
            def _():
                do(n)

    def start(n):
        if n == 0 or ways == 1:
            load_line(n, (near_rows, far_rows[0])[n]).start()
            load(n, (near_pages, far_pages[0])[n]).start()
            return
        for way in range(ways):

            @pl.when((far_gap == 1) == (way == 0))
            def _():
                load_line(n, far_rows[way]).start()
                load(n, far_pages[way]).start()

    def patch(n):
        _, length = cases[n]
        load_line(n, near_rows).wait()
        store_line(n).start()
        fresh = lines[n, :, width:].astype(F32)
        load(n, near_pages).wait()
        for p in range(pages):
            at = row + p * page_len
            for which in range(2):
                page = stage[n, which * pages + p].astype(F32)
                page = jnp.where(at < length, page, 0.0)
                for t in range(steps):
                    page = jnp.where(
                        at == length + t, fresh[t : t + 1, which * head_dim : (which + 1) * head_dim], page
                    )
                stage[n, which * pages + p] = page.astype(BF16)
                store(n, p, which).start()

    def finish(n):
        store_line(n).wait()
        for p in range(pages):
            for which in range(2):
                store(n, p, which).wait()

    own = pltpu.make_async_copy(mixed_in, mixed, own_sem)
    own.start()
    each(start)
    own.wait()
    each(patch)
    each(finish)


def run(
    near_hops,
    far_hops,
    table,
    token_states,
    query_rows,
    key_weight,
    value_weight,
    out_weight,
    keys,
    values,
    cached_len,
    migrations,
):
    groups = lax.axis_size("dec")
    tp = lax.axis_size("tp")
    slot_count, steps, model = token_states.shape
    _, page_len, head_dim = keys.shape
    rows = slot_count * steps
    width = out_weight.shape[1]
    heads = query_rows.shape[2] // head_dim
    pages = table.shape[1]
    pool_shape = jax.ShapeDtypeStruct(keys.shape, BF16)
    moved_shape = jax.ShapeDtypeStruct((2 * pages, page_len, head_dim), BF16)
    limit = pltpu.CompilerParams(vmem_limit_bytes=63 * 2**20)

    near, far, token = pl.pallas_call(
        functools.partial(pack_kernel, groups),
        out_shape=(moved_shape, moved_shape, jax.ShapeDtypeStruct((1,), jnp.int32)),
        in_specs=[SMEM, SMEM, HBM, HBM],
        out_specs=(VMEM, VMEM, SMEM),
        scratch_shapes=[pltpu.SemaphoreType.DMA((2, 2, pages))],
        compiler_params=limit,
        name="pack",
    )(migrations, table, keys, values)
    pages_in = [lax.ppermute(near, "dec", near_hops)] + [lax.ppermute(far, "dec", hops) for hops in far_hops]

    key_mid, value_mid, partial, new_rows = pl.pallas_call(
        functools.partial(attend_kernel, groups),
        out_shape=(
            pool_shape,
            pool_shape,
            jax.ShapeDtypeStruct((rows, width), BF16),
            jax.ShapeDtypeStruct((rows, 2 * head_dim), BF16),
        ),
        in_specs=[SMEM, SMEM, SMEM, SMEM, VMEM, VMEM, HBM, HBM, HBM, HBM, HBM],
        out_specs=(HBM, HBM, VMEM, VMEM),
        scratch_shapes=[
            pltpu.VMEM(key_weight.shape, BF16),
            pltpu.VMEM(value_weight.shape, BF16),
            pltpu.VMEM(out_weight.shape, BF16),
            pltpu.VMEM(keys.shape, BF16),
            pltpu.VMEM(values.shape, BF16),
            pltpu.VMEM((heads * rows, head_dim), F32),
            pltpu.VMEM((heads * rows, head_dim), F32),
            pltpu.VMEM((rows, 2 * head_dim), F32),
            pltpu.SemaphoreType.DMA((5 * PARTS,)),
        ],
        compiler_params=pltpu.CompilerParams(vmem_limit_bytes=40 * 2**20),
        cost_estimate=pl.CostEstimate(flops=1_000_000, bytes_accessed=1_000_000, transcendentals=0),
        name="attend",
    )(
        token,
        migrations,
        cached_len,
        table,
        token_states,
        query_rows,
        key_weight,
        value_weight,
        out_weight,
        keys,
        values,
    )

    others = [lax.ppermute(partial, "tp", [(i, i ^ n) for i in range(tp)]) for n in range(1, tp)]
    row_shape = jax.ShapeDtypeStruct((steps, width + 2 * head_dim), BF16)
    mixed, near_row, far_row = pl.pallas_call(
        functools.partial(finish_rows_kernel, groups),
        out_shape=(jax.ShapeDtypeStruct((slot_count, steps, width), BF16), row_shape, row_shape),
        in_specs=[SMEM, SMEM, VMEM] + [VMEM] * tp,
        out_specs=(VMEM, VMEM, VMEM),
        scratch_shapes=[pltpu.VMEM((slot_count, steps, width + 2 * head_dim), F32)],
        compiler_params=pltpu.CompilerParams(vmem_limit_bytes=8 * 2**20),
        name="rows",
    )(migrations, cached_len, new_rows, partial, *others)
    rows_in = [lax.ppermute(near_row, "dec", near_hops)] + [lax.ppermute(far_row, "dec", hops) for hops in far_hops]
    return pages_in, rows_in, mixed, key_mid, value_mid


def moved(table, inputs):
    groups = lax.axis_size("dec")
    half = groups // 2
    if half != 2:
        return run(shifted(groups, half), (shifted(groups, 1), shifted(groups, 1 + half)), table, *inputs)
    source_group = inputs[-1][:, 0]
    branches = []
    for case in range(2**half):
        senders = [pair + half * (case >> pair & 1) for pair in range(half)]
        receivers = [(sender + half) % groups for sender in senders]
        near_hops = [(senders[pair], receivers[pair]) for pair in range(half)]
        far_hops = [(senders[pair], receivers[(pair + 1) % half]) for pair in range(half)]
        near_hops += [(b, a) for a, b in near_hops]
        far_hops += [(b, a) for a, b in far_hops]
        branches.append(functools.partial(run, near_hops, (far_hops,)))
    bits = jnp.where(source_group >= half, source_group - half + 1, 0)
    number = lax.reduce(bits, jnp.int32(0), lax.bitwise_or, (0,))
    return lax.switch(number, branches, table, *inputs)


def local(
    token_states,
    query_rows,
    key_weight,
    value_weight,
    out_weight,
    key_pool,
    value_pool,
    cached_len,
    page_table,
    migrations,
):
    groups = lax.axis_size("dec")
    pool_pages, _, page_len, head_dim = key_pool.shape
    slot_count, steps, _ = token_states.shape
    keys = key_pool.reshape(pool_pages, page_len, head_dim)
    values = value_pool.reshape(pool_pages, page_len, head_dim)
    table = jnp.swapaxes(page_table, 1, 2)
    pages = table.shape[1]
    inputs = (
        token_states,
        query_rows,
        key_weight,
        value_weight,
        out_weight,
        keys,
        values,
        cached_len,
        migrations,
    )
    pages_in, rows_in, mixed_mid, key_mid, value_mid = moved(table, inputs)
    ways = len(pages_in) - 1
    pool_shape = jax.ShapeDtypeStruct(keys.shape, BF16)
    mixed_shape = jax.ShapeDtypeStruct((slot_count, steps, out_weight.shape[1]), BF16)
    mixed, key_out, value_out = pl.pallas_call(
        functools.partial(place_kernel, groups, ways),
        out_shape=(mixed_shape, pool_shape, pool_shape),
        in_specs=[SMEM] * 3 + [ANY] * (2 + 2 * ways) + [VMEM] + [HBM] * 2,
        out_specs=(HBM, HBM, HBM),
        scratch_shapes=[
            pltpu.VMEM((2, 2 * pages, page_len, head_dim), BF16),
            pltpu.VMEM((2,) + rows_in[0].shape, BF16),
            pltpu.SemaphoreType.DMA((2,)),
            pltpu.SemaphoreType.DMA((2, 2)),
            pltpu.SemaphoreType.DMA((2, 2, pages)),
            pltpu.SemaphoreType.DMA,
        ],
        input_output_aliases={6 + 2 * ways: 1, 7 + 2 * ways: 2},
        compiler_params=pltpu.CompilerParams(vmem_limit_bytes=63 * 2**20),
        name="place",
    )(migrations, cached_len, table, *pages_in, *rows_in, mixed_mid, key_mid, value_mid)
    return mixed, key_out.reshape(key_pool.shape), value_out.reshape(value_pool.shape)


def solution(mesh):
    placed = (
        P(("rep", "dec"), None, None),
        P(("rep", "dec"), None, "tp"),
        P(None, "tp"),
        P(None, "tp"),
        P("tp", None),
        P(("rep", "dec"), "tp", None, None),
        P(("rep", "dec"), "tp", None, None),
        P("rep", None),
        P(("rep", "dec"), None, None),
        P("rep", None),
    )
    return jax.shard_map(
        local,
        mesh=mesh,
        in_specs=placed,
        out_specs=(
            P(("rep", "dec"), None, None),
            P(("rep", "dec"), "tp", None, None),
            P(("rep", "dec"), "tp", None, None),
        ),
        check_vma=False,
    )
```

```python
import functools

import jax
import jax.numpy as jnp
from jax import lax
from jax.experimental import pallas as pl
from jax.experimental.pallas import tpu as pltpu
from jax.sharding import PartitionSpec as P

F32 = jnp.float32
BF16 = jnp.bfloat16
PARTS = 4
SMEM = pl.BlockSpec(memory_space=pltpu.SMEM)
HBM = pl.BlockSpec(memory_space=pltpu.HBM)
ANY = pl.BlockSpec(memory_space=pl.ANY)
VMEM = pl.BlockSpec(memory_space=pltpu.VMEM)


def shifted(count, by):
    return [(i, (i + by) % count) for i in range(count)]


def outgoing(mig, me, groups):
    half = groups // 2
    near = far = jnp.int32(-1)
    for m in range(mig.shape[0]):
        mine = mig[m, 0] == me
        gap = lax.rem(mig[m, 2] - me + groups, groups)
        near = jnp.where(mine & (gap == half), mig[m, 1], near)
        far = jnp.where(mine & (gap != half), mig[m, 1], far)
    return near, far


def incoming(mig, lens, me, groups):
    half = groups // 2
    near = far = jnp.int32(-1)
    near_len = far_len = far_gap = jnp.int32(0)
    for m in range(mig.shape[0]):
        mine = mig[m, 2] == me
        gap = lax.rem(me - mig[m, 0] + groups, groups)
        length = lens[mig[m, 0], mig[m, 1]]
        is_near = mine & (gap == half)
        is_far = mine & (gap != half)
        near = jnp.where(is_near, mig[m, 3], near)
        near_len = jnp.where(is_near, length, near_len)
        far = jnp.where(is_far, mig[m, 3], far)
        far_len = jnp.where(is_far, length, far_len)
        far_gap = jnp.where(is_far, gap, far_gap)
    return (near, near_len), (far, far_len), far_gap


def pack_kernel(groups, mig, table, key_pool, value_pool, near_out, far_out, token, sems):
    me = lax.axis_index("dec")
    pages = table.shape[1]
    outs = (near_out, far_out)
    slots = outgoing(mig, me, groups)

    def load(n, which, p):
        page = table[0, p, slots[n]]
        pool = (key_pool, value_pool)[which]
        return pltpu.make_async_copy(pool.at[page], outs[n].at[which * pages + p], sems.at[n, which, p])

    def each(do):
        for n in range(2):

            @pl.when(slots[n] >= 0)
            def _():
                for p in range(pages):
                    for which in range(2):
                        do(load(n, which, p))

    each(lambda copy: copy.start())
    token[0] = me
    each(lambda copy: copy.wait())


def attend_kernel(
    groups,
    token,
    mig,
    lens,
    table,
    states_hbm,
    query_hbm,
    key_weight,
    value_weight,
    out_weight,
    kp,
    vp,
    key_out,
    value_out,
    partial,
    new_rows,
    states,
    query,
    wk,
    wv,
    wo,
    q_scr,
    a_scr,
    tiles,
    load_sems,
    store_sems,
    tile_sems,
):
    del token
    me = lax.axis_index("dec")
    slot_count, steps, _ = states.shape
    rows = slot_count * steps
    pages = table.shape[1]
    page_len, head_dim = kp.shape[1:]
    heads = query.shape[2] // head_dim
    span = pages * page_len
    pools = ((kp, key_out, 0), (vp, value_out, head_dim))
    number = 0

    def split(source, target, parts):
        nonlocal number
        size = source.shape[0] // parts
        copies = []
        for part in range(parts):
            piece = pl.ds(part * size, size)
            copies.append(pltpu.make_async_copy(source.at[piece], target.at[piece], load_sems.at[number]))
            number += 1
        return copies

    (load_query,) = split(query_hbm, query, 1)
    (load_states,) = split(states_hbm, states, 1)
    load_wk = split(key_weight, wk, PARTS)
    load_wv = split(value_weight, wv, PARTS)
    loads = split(out_weight, wo, PARTS)
    stores = [pltpu.make_async_copy(pool, out, store_sems.at[n]) for n, (pool, out, _) in enumerate(pools)]
    for copy in [load_query, load_states] + load_wk + load_wv + loads + stores:
        copy.start()
    near, far = outgoing(mig, me, groups)
    lengths = [lens[me, s] for s in range(slot_count)]
    numbers = [[table[0, p, s] for p in range(pages)] for s in range(slot_count)]

    load_query.wait()
    for s in range(slot_count):
        qf = query[s].astype(F32)
        for h in range(heads):
            q_scr[pl.ds(h * rows + s * steps, steps), :] = qf[:, h * head_dim : (h + 1) * head_dim]

    count = steps * heads
    nt = (((1,), (1,)), ((), ()))
    queries = jnp.concatenate(
        [q_scr[pl.ds(r, heads, stride=rows), :] for r in range(rows)], 0
    ).astype(BF16)
    position = lax.broadcasted_iota(jnp.int32, (count, span), 1)
    scaling = head_dim**-0.5
    scores = []
    for s in range(slot_count):
        keys = jnp.concatenate([kp[n] for n in numbers[s]], 0)
        cached = lax.dot_general(
            queries[s * count : (s + 1) * count], keys, nt, preferred_element_type=F32
        )
        scores.append(jnp.where(position < lengths[s], cached * scaling, -jnp.inf))
    cached = jnp.concatenate(scores, 0)

    load_states.wait()
    x = jnp.concatenate([states[s].astype(F32) for s in range(slot_count)], 0).astype(BF16)
    fresh_k = jnp.zeros((rows, head_dim), F32)
    fresh_v = jnp.zeros((rows, head_dim), F32)
    size = wk.shape[0] // PARTS
    for part in range(PARTS):
        piece = slice(part * size, (part + 1) * size)
        load_wk[part].wait()
        fresh_k = fresh_k + jnp.dot(x[:, piece], wk[piece, :], preferred_element_type=F32)
        load_wv[part].wait()
        fresh_v = fresh_v + jnp.dot(x[:, piece], wv[piece, :], preferred_element_type=F32)
    fresh_k = fresh_k.astype(BF16)
    fresh_v = fresh_v.astype(BF16)
    new_rows[:, :head_dim] = fresh_k
    new_rows[:, head_dim:] = fresh_v

    fresh = lax.dot_general(queries, fresh_k, nt, preferred_element_type=F32) * scaling
    fresh_row = lax.broadcasted_iota(jnp.int32, fresh.shape, 0)
    fresh_col = lax.broadcasted_iota(jnp.int32, fresh.shape, 1)
    first = fresh_row // count * steps
    allowed = (fresh_col >= first) & (fresh_col <= fresh_row // heads)
    fresh = jnp.where(allowed, fresh, -jnp.inf)
    peak = jnp.maximum(jnp.max(cached, 1, keepdims=True), jnp.max(fresh, 1, keepdims=True))
    cached = jnp.exp(cached - peak)
    fresh = jnp.exp(fresh - peak)
    share = 1.0 / (jnp.sum(cached, 1, keepdims=True) + jnp.sum(fresh, 1, keepdims=True))
    cached_w = (cached * share).astype(BF16)
    fresh_w = (fresh * share).astype(BF16)
    fresh_out = jnp.dot(fresh_w, fresh_v, preferred_element_type=F32)
    for s in range(slot_count):
        values = jnp.concatenate([vp[n] for n in numbers[s]], 0)
        piece = slice(s * count, (s + 1) * count)
        out = jnp.dot(cached_w[piece], values, preferred_element_type=F32) + fresh_out[piece]
        for t in range(steps):
            a_scr[pl.ds(s * steps + t, heads, stride=rows), :] = out[t * heads : (t + 1) * heads]

    tile = tiles.shape[3]
    row = lax.broadcasted_iota(jnp.int32, (tile, head_dim), 0)
    fresh_f = (fresh_k.astype(F32), fresh_v.astype(F32))
    places = []
    for s in range(slot_count):
        live = (lengths[s] > 0) & (s != near) & (s != far)
        for t in range(steps):
            at = lengths[s] + t
            page = table[0, at // page_len, s]
            low = at // tile * tile
            base = pl.multiple_of(lax.rem(low, page_len), tile)
            places.append((s, t, page, base, live & ((t == 0) | (lax.rem(at, tile) == 0))))
            for n, (pool, _, _) in enumerate(pools):
                merged = pool[page, pl.ds(base, tile), :].astype(F32)
                for u in range(steps):
                    line = fresh_f[n][s * steps + u : s * steps + u + 1]
                    merged = jnp.where(row + low == lengths[s] + u, line, merged)
                tiles[n, s, t] = merged.astype(BF16)
    for store in stores:
        store.wait()

    def put(n, s, t, page, base):
        return pltpu.make_async_copy(
            tiles.at[n, s, t], pools[n][1].at[page, pl.ds(base, tile), :], tile_sems.at[n, s, t]
        )

    for s, t, page, base, wanted in places:

        @pl.when(wanted)
        def _():
            for n in range(2):
                put(n, s, t, page, base).start()

    attention = jnp.concatenate([a_scr[h * rows : (h + 1) * rows, :].astype(BF16) for h in range(heads)], 1)
    result = jnp.zeros((rows, wo.shape[1]), F32)
    size = wo.shape[0] // PARTS
    for part in range(PARTS):
        piece = slice(part * size, (part + 1) * size)
        loads[part].wait()
        result = result + jnp.dot(attention[:, piece], wo[piece, :], preferred_element_type=F32)
    partial[...] = result.astype(BF16)
    for s, t, page, base, wanted in places:

        @pl.when(wanted)
        def _():
            for n in range(2):
                put(n, s, t, page, base).wait()


def finish_rows_kernel(groups, mig, lens, new_rows, *refs):
    *parts, mixed, near_out, far_out, scr = refs
    me = lax.axis_index("dec")
    slots = outgoing(mig, me, groups)
    width = parts[0].shape[1]
    terms = [part[...].astype(F32) for part in parts]
    level = 1
    while level < len(terms):
        terms = [terms[n] + terms[n ^ level] for n in range(len(terms))]
        level *= 2
    total = terms[0]
    slot_count, steps, _ = scr.shape
    for s in range(slot_count):
        live = (lens[me, s] > 0) & (s != slots[0]) & (s != slots[1])
        own = total[s * steps : (s + 1) * steps]
        scr[s, :, :width] = own
        scr[s, :, width:] = new_rows[s * steps : (s + 1) * steps, :].astype(F32)
        mixed[s] = jnp.where(live, own, 0.0).astype(BF16)
    for slot, out in zip(slots, (near_out, far_out)):
        out[...] = scr[jnp.maximum(slot, 0)].astype(BF16)


def place_kernel(groups, ways, mig, lens, table, *refs):
    near_pages, *far_pages = refs[: 1 + ways]
    near_rows, *far_rows = refs[1 + ways : 2 + 2 * ways]
    mixed_in, _, _, mixed, key_out, value_out, stage, lines, in_sems, line_sems, out_sems, own_sem = refs[
        2 + 2 * ways :
    ]
    me = lax.axis_index("dec")
    pages = table.shape[1]
    page_len, head_dim = stage.shape[2:]
    _, steps, width = mixed.shape
    *cases, far_gap = incoming(mig, lens, me, groups)
    row = lax.broadcasted_iota(jnp.int32, (page_len, head_dim), 0)

    def load(n, source):
        return pltpu.make_async_copy(source, stage.at[n], in_sems.at[n])

    def load_line(n, source):
        return pltpu.make_async_copy(source, lines.at[n], line_sems.at[n, 0])

    def store_line(n):
        return pltpu.make_async_copy(
            lines.at[n, :, pl.ds(0, width)], mixed.at[cases[n][0]], line_sems.at[n, 1]
        )

    def store(n, p, which):
        pool = (key_out, value_out)[which]
        page = table[0, p, cases[n][0]]
        return pltpu.make_async_copy(stage.at[n, which * pages + p], pool.at[page], out_sems.at[n, which, p])

    def each(do):
        for n in range(2):

            @pl.when(cases[n][0] >= 0)
            def _():
                do(n)

    def start(n):
        if n == 0 or ways == 1:
            load_line(n, (near_rows, far_rows[0])[n]).start()
            load(n, (near_pages, far_pages[0])[n]).start()
            return
        for way in range(ways):

            @pl.when((far_gap == 1) == (way == 0))
            def _():
                load_line(n, far_rows[way]).start()
                load(n, far_pages[way]).start()

    def patch(n):
        _, length = cases[n]
        load_line(n, near_rows).wait()
        store_line(n).start()
        fresh = lines[n, :, width:].astype(F32)
        load(n, near_pages).wait()
        for p in range(pages):
            at = row + p * page_len
            for which in range(2):
                page = stage[n, which * pages + p].astype(F32)
                page = jnp.where(at < length, page, 0.0)
                for t in range(steps):
                    page = jnp.where(
                        at == length + t, fresh[t : t + 1, which * head_dim : (which + 1) * head_dim], page
                    )
                stage[n, which * pages + p] = page.astype(BF16)
                store(n, p, which).start()

    def finish(n):
        store_line(n).wait()
        for p in range(pages):
            for which in range(2):
                store(n, p, which).wait()

    own = pltpu.make_async_copy(mixed_in, mixed, own_sem)
    own.start()
    each(start)
    own.wait()
    each(patch)
    each(finish)


def run(
    near_hops,
    far_hops,
    table,
    token_states,
    query_rows,
    key_weight,
    value_weight,
    out_weight,
    keys,
    values,
    cached_len,
    migrations,
):
    groups = lax.axis_size("dec")
    tp = lax.axis_size("tp")
    slot_count, steps, model = token_states.shape
    _, page_len, head_dim = keys.shape
    rows = slot_count * steps
    width = out_weight.shape[1]
    heads = query_rows.shape[2] // head_dim
    pages = table.shape[1]
    pool_shape = jax.ShapeDtypeStruct(keys.shape, BF16)
    moved_shape = jax.ShapeDtypeStruct((2 * pages, page_len, head_dim), BF16)
    limit = pltpu.CompilerParams(vmem_limit_bytes=63 * 2**20)

    near, far, token = pl.pallas_call(
        functools.partial(pack_kernel, groups),
        out_shape=(moved_shape, moved_shape, jax.ShapeDtypeStruct((1,), jnp.int32)),
        in_specs=[SMEM, SMEM, HBM, HBM],
        out_specs=(VMEM, VMEM, SMEM),
        scratch_shapes=[pltpu.SemaphoreType.DMA((2, 2, pages))],
        compiler_params=pltpu.CompilerParams(vmem_limit_bytes=40 * 2**20),
        cost_estimate=pl.CostEstimate(flops=0, bytes_accessed=1_000_000, transcendentals=0),
        name="pack",
    )(migrations, table, keys, values)
    pages_in = [lax.ppermute(near, "dec", near_hops)] + [lax.ppermute(far, "dec", hops) for hops in far_hops]

    key_mid, value_mid, partial, new_rows = pl.pallas_call(
        functools.partial(attend_kernel, groups),
        out_shape=(
            pool_shape,
            pool_shape,
            jax.ShapeDtypeStruct((rows, width), BF16),
            jax.ShapeDtypeStruct((rows, 2 * head_dim), BF16),
        ),
        in_specs=[SMEM] * 4 + [ANY] * 5 + [VMEM] * 2,
        out_specs=(HBM, HBM, VMEM, VMEM),
        scratch_shapes=[
            pltpu.VMEM(token_states.shape, BF16),
            pltpu.VMEM(query_rows.shape, BF16),
            pltpu.VMEM(key_weight.shape, BF16),
            pltpu.VMEM(value_weight.shape, BF16),
            pltpu.VMEM(out_weight.shape, BF16),
            pltpu.VMEM((heads * rows, head_dim), F32),
            pltpu.VMEM((heads * rows, head_dim), F32),
            pltpu.VMEM((2, slot_count, steps, 16, head_dim), BF16),
            pltpu.SemaphoreType.DMA((2 + 3 * PARTS,)),
            pltpu.SemaphoreType.DMA((2,)),
            pltpu.SemaphoreType.DMA((2, slot_count, steps)),
        ],
        compiler_params=pltpu.CompilerParams(vmem_limit_bytes=40 * 2**20),
        cost_estimate=pl.CostEstimate(flops=1_000_000, bytes_accessed=1_000_000, transcendentals=0),
        name="attend",
    )(
        token,
        migrations,
        cached_len,
        table,
        token_states,
        query_rows,
        key_weight,
        value_weight,
        out_weight,
        keys,
        values,
    )

    others = [lax.ppermute(partial, "tp", [(i, i ^ n) for i in range(tp)]) for n in range(1, tp)]
    row_shape = jax.ShapeDtypeStruct((steps, width + 2 * head_dim), BF16)
    mixed, near_row, far_row = pl.pallas_call(
        functools.partial(finish_rows_kernel, groups),
        out_shape=(jax.ShapeDtypeStruct((slot_count, steps, width), BF16), row_shape, row_shape),
        in_specs=[SMEM, SMEM, VMEM] + [VMEM] * tp,
        out_specs=(VMEM, VMEM, VMEM),
        scratch_shapes=[pltpu.VMEM((slot_count, steps, width + 2 * head_dim), F32)],
        compiler_params=pltpu.CompilerParams(vmem_limit_bytes=8 * 2**20),
        name="rows",
    )(migrations, cached_len, new_rows, partial, *others)
    rows_in = [lax.ppermute(near_row, "dec", near_hops)] + [lax.ppermute(far_row, "dec", hops) for hops in far_hops]
    return pages_in, rows_in, mixed, key_mid, value_mid


def moved(table, inputs):
    groups = lax.axis_size("dec")
    half = groups // 2
    if half != 2:
        return run(shifted(groups, half), (shifted(groups, 1), shifted(groups, 1 + half)), table, *inputs)
    source_group = inputs[-1][:, 0]
    branches = []
    for case in range(2**half):
        senders = [pair + half * (case >> pair & 1) for pair in range(half)]
        receivers = [(sender + half) % groups for sender in senders]
        near_hops = [(senders[pair], receivers[pair]) for pair in range(half)]
        far_hops = [(senders[pair], receivers[(pair + 1) % half]) for pair in range(half)]
        near_hops += [(b, a) for a, b in near_hops]
        far_hops += [(b, a) for a, b in far_hops]
        branches.append(functools.partial(run, near_hops, (far_hops,)))
    bits = jnp.where(source_group >= half, source_group - half + 1, 0)
    number = lax.reduce(bits, jnp.int32(0), lax.bitwise_or, (0,))
    return lax.switch(number, branches, table, *inputs)


def local(
    token_states,
    query_rows,
    key_weight,
    value_weight,
    out_weight,
    key_pool,
    value_pool,
    cached_len,
    page_table,
    migrations,
):
    groups = lax.axis_size("dec")
    pool_pages, _, page_len, head_dim = key_pool.shape
    slot_count, steps, _ = token_states.shape
    keys = key_pool.reshape(pool_pages, page_len, head_dim)
    values = value_pool.reshape(pool_pages, page_len, head_dim)
    table = jnp.swapaxes(page_table, 1, 2)
    pages = table.shape[1]
    inputs = (
        token_states,
        query_rows,
        key_weight,
        value_weight,
        out_weight,
        keys,
        values,
        cached_len,
        migrations,
    )
    pages_in, rows_in, mixed_mid, key_mid, value_mid = moved(table, inputs)
    ways = len(pages_in) - 1
    pool_shape = jax.ShapeDtypeStruct(keys.shape, BF16)
    mixed_shape = jax.ShapeDtypeStruct((slot_count, steps, out_weight.shape[1]), BF16)
    mixed, key_out, value_out = pl.pallas_call(
        functools.partial(place_kernel, groups, ways),
        out_shape=(mixed_shape, pool_shape, pool_shape),
        in_specs=[SMEM] * 3 + [ANY] * (2 + 2 * ways) + [VMEM] + [HBM] * 2,
        out_specs=(HBM, HBM, HBM),
        scratch_shapes=[
            pltpu.VMEM((2, 2 * pages, page_len, head_dim), BF16),
            pltpu.VMEM((2,) + rows_in[0].shape, BF16),
            pltpu.SemaphoreType.DMA((2,)),
            pltpu.SemaphoreType.DMA((2, 2)),
            pltpu.SemaphoreType.DMA((2, 2, pages)),
            pltpu.SemaphoreType.DMA,
        ],
        input_output_aliases={6 + 2 * ways: 1, 7 + 2 * ways: 2},
        compiler_params=pltpu.CompilerParams(vmem_limit_bytes=63 * 2**20),
        name="place",
    )(migrations, cached_len, table, *pages_in, *rows_in, mixed_mid, key_mid, value_mid)
    return mixed, key_out.reshape(key_pool.shape), value_out.reshape(value_pool.shape)


def solution(mesh):
    placed = (
        P(("rep", "dec"), None, None),
        P(("rep", "dec"), None, "tp"),
        P(None, "tp"),
        P(None, "tp"),
        P("tp", None),
        P(("rep", "dec"), "tp", None, None),
        P(("rep", "dec"), "tp", None, None),
        P("rep", None),
        P(("rep", "dec"), None, None),
        P("rep", None),
    )
    return jax.shard_map(
        local,
        mesh=mesh,
        in_specs=placed,
        out_specs=(
            P(("rep", "dec"), None, None),
            P(("rep", "dec"), "tp", None, None),
            P(("rep", "dec"), "tp", None, None),
        ),
        check_vma=False,
    )
```

```python
import functools

import jax
import jax.numpy as jnp
from jax import lax
from jax.experimental import pallas as pl
from jax.experimental.pallas import tpu as pltpu
from jax.sharding import PartitionSpec as P

F32 = jnp.float32
BF16 = jnp.bfloat16
PARTS = 4
SMEM = pl.BlockSpec(memory_space=pltpu.SMEM)
HBM = pl.BlockSpec(memory_space=pltpu.HBM)
ANY = pl.BlockSpec(memory_space=pl.ANY)
VMEM = pl.BlockSpec(memory_space=pltpu.VMEM)


def shifted(count, by):
    return [(i, (i + by) % count) for i in range(count)]


def outgoing(mig, me, groups):
    half = groups // 2
    near = far = jnp.int32(-1)
    for m in range(mig.shape[0]):
        mine = mig[m, 0] == me
        gap = lax.rem(mig[m, 2] - me + groups, groups)
        near = jnp.where(mine & (gap == half), mig[m, 1], near)
        far = jnp.where(mine & (gap != half), mig[m, 1], far)
    return near, far


def incoming(mig, lens, me, groups):
    half = groups // 2
    near = far = jnp.int32(-1)
    near_len = far_len = far_gap = jnp.int32(0)
    for m in range(mig.shape[0]):
        mine = mig[m, 2] == me
        gap = lax.rem(me - mig[m, 0] + groups, groups)
        length = lens[mig[m, 0], mig[m, 1]]
        is_near = mine & (gap == half)
        is_far = mine & (gap != half)
        near = jnp.where(is_near, mig[m, 3], near)
        near_len = jnp.where(is_near, length, near_len)
        far = jnp.where(is_far, mig[m, 3], far)
        far_len = jnp.where(is_far, length, far_len)
        far_gap = jnp.where(is_far, gap, far_gap)
    return (near, near_len), (far, far_len), far_gap


def pack_kernel(groups, mig, table, key_pool, value_pool, near_out, far_out, token, sems):
    me = lax.axis_index("dec")
    pages = table.shape[1]
    outs = (near_out, far_out)
    slots = outgoing(mig, me, groups)

    def load(n, which, p):
        page = table[0, p, slots[n]]
        pool = (key_pool, value_pool)[which]
        return pltpu.make_async_copy(pool.at[page], outs[n].at[which * pages + p], sems.at[n, which, p])

    def each(do):
        for n in range(2):

            @pl.when(slots[n] >= 0)
            def _():
                for p in range(pages):
                    for which in range(2):
                        do(load(n, which, p))

    each(lambda copy: copy.start())
    half = groups // 2
    number = jnp.int32(0)
    if half == 2:
        for m in range(mig.shape[0]):
            number = number | jnp.where(mig[m, 0] >= half, mig[m, 0] - half + 1, 0)
    token[0] = number
    each(lambda copy: copy.wait())


def attend_kernel(
    groups,
    token,
    mig,
    lens,
    table,
    states_hbm,
    query_hbm,
    key_weight,
    value_weight,
    out_weight,
    kp,
    vp,
    key_out,
    value_out,
    partial,
    new_rows,
    states,
    query,
    wk,
    wv,
    wo,
    q_scr,
    a_scr,
    tiles,
    load_sems,
    store_sems,
    tile_sems,
):
    del token
    me = lax.axis_index("dec")
    slot_count, steps, _ = states.shape
    rows = slot_count * steps
    pages = table.shape[1]
    page_len, head_dim = kp.shape[1:]
    heads = query.shape[2] // head_dim
    span = pages * page_len
    pools = ((kp, key_out, 0), (vp, value_out, head_dim))
    number = 0

    def split(source, target, parts):
        nonlocal number
        size = source.shape[0] // parts
        copies = []
        for part in range(parts):
            piece = pl.ds(part * size, size)
            copies.append(pltpu.make_async_copy(source.at[piece], target.at[piece], load_sems.at[number]))
            number += 1
        return copies

    (load_query,) = split(query_hbm, query, 1)
    (load_states,) = split(states_hbm, states, 1)
    load_wk = split(key_weight, wk, PARTS)
    load_wv = split(value_weight, wv, PARTS)
    loads = split(out_weight, wo, PARTS)
    stores = [pltpu.make_async_copy(pool, out, store_sems.at[n]) for n, (pool, out, _) in enumerate(pools)]
    for copy in [load_query, load_states] + load_wk + load_wv + loads + stores:
        copy.start()
    near, far = outgoing(mig, me, groups)
    lengths = [lens[me, s] for s in range(slot_count)]
    numbers = [[table[0, p, s] for p in range(pages)] for s in range(slot_count)]

    load_query.wait()
    for s in range(slot_count):
        qf = query[s].astype(F32)
        for h in range(heads):
            q_scr[pl.ds(h * rows + s * steps, steps), :] = qf[:, h * head_dim : (h + 1) * head_dim]

    count = steps * heads
    nt = (((1,), (1,)), ((), ()))
    queries = jnp.concatenate(
        [q_scr[pl.ds(r, heads, stride=rows), :] for r in range(rows)], 0
    ).astype(BF16)
    position = lax.broadcasted_iota(jnp.int32, (count, span), 1)
    scaling = head_dim**-0.5
    scores = []
    for s in range(slot_count):
        keys = jnp.concatenate([kp[n] for n in numbers[s]], 0)
        cached = lax.dot_general(
            queries[s * count : (s + 1) * count], keys, nt, preferred_element_type=F32
        )
        scores.append(jnp.where(position < lengths[s], cached * scaling, -jnp.inf))
    cached = jnp.concatenate(scores, 0)

    load_states.wait()
    x = jnp.concatenate([states[s].astype(F32) for s in range(slot_count)], 0).astype(BF16)
    fresh_k = jnp.zeros((rows, head_dim), F32)
    fresh_v = jnp.zeros((rows, head_dim), F32)
    size = wk.shape[0] // PARTS
    for part in range(PARTS):
        piece = slice(part * size, (part + 1) * size)
        load_wk[part].wait()
        fresh_k = fresh_k + jnp.dot(x[:, piece], wk[piece, :], preferred_element_type=F32)
        load_wv[part].wait()
        fresh_v = fresh_v + jnp.dot(x[:, piece], wv[piece, :], preferred_element_type=F32)
    fresh_k = fresh_k.astype(BF16)
    fresh_v = fresh_v.astype(BF16)
    new_rows[:, :head_dim] = fresh_k
    new_rows[:, head_dim:] = fresh_v

    fresh = lax.dot_general(queries, fresh_k, nt, preferred_element_type=F32) * scaling
    fresh_row = lax.broadcasted_iota(jnp.int32, fresh.shape, 0)
    fresh_col = lax.broadcasted_iota(jnp.int32, fresh.shape, 1)
    first = fresh_row // count * steps
    allowed = (fresh_col >= first) & (fresh_col <= fresh_row // heads)
    fresh = jnp.where(allowed, fresh, -jnp.inf)
    peak = jnp.maximum(jnp.max(cached, 1, keepdims=True), jnp.max(fresh, 1, keepdims=True))
    cached = jnp.exp(cached - peak)
    fresh = jnp.exp(fresh - peak)
    share = 1.0 / (jnp.sum(cached, 1, keepdims=True) + jnp.sum(fresh, 1, keepdims=True))
    cached_w = (cached * share).astype(BF16)
    fresh_w = (fresh * share).astype(BF16)
    fresh_out = jnp.dot(fresh_w, fresh_v, preferred_element_type=F32)
    for s in range(slot_count):
        values = jnp.concatenate([vp[n] for n in numbers[s]], 0)
        piece = slice(s * count, (s + 1) * count)
        out = jnp.dot(cached_w[piece], values, preferred_element_type=F32) + fresh_out[piece]
        for t in range(steps):
            a_scr[pl.ds(s * steps + t, heads, stride=rows), :] = out[t * heads : (t + 1) * heads]

    tile = tiles.shape[3]
    row = lax.broadcasted_iota(jnp.int32, (tile, head_dim), 0)
    fresh_f = (fresh_k.astype(F32), fresh_v.astype(F32))
    places = []
    for s in range(slot_count):
        live = (lengths[s] > 0) & (s != near) & (s != far)
        for t in range(steps):
            at = lengths[s] + t
            page = table[0, at // page_len, s]
            low = at // tile * tile
            base = pl.multiple_of(lax.rem(low, page_len), tile)
            places.append((s, t, page, base, live & ((t == 0) | (lax.rem(at, tile) == 0))))
            for n, (pool, _, _) in enumerate(pools):
                merged = pool[page, pl.ds(base, tile), :].astype(F32)
                for u in range(steps):
                    line = fresh_f[n][s * steps + u : s * steps + u + 1]
                    merged = jnp.where(row + low == lengths[s] + u, line, merged)
                tiles[n, s, t] = merged.astype(BF16)
    for store in stores:
        store.wait()

    def put(n, s, t, page, base):
        return pltpu.make_async_copy(
            tiles.at[n, s, t], pools[n][1].at[page, pl.ds(base, tile), :], tile_sems.at[n, s, t]
        )

    for s, t, page, base, wanted in places:

        @pl.when(wanted)
        def _():
            for n in range(2):
                put(n, s, t, page, base).start()

    attention = jnp.concatenate([a_scr[h * rows : (h + 1) * rows, :].astype(BF16) for h in range(heads)], 1)
    result = jnp.zeros((rows, wo.shape[1]), F32)
    size = wo.shape[0] // PARTS
    for part in range(PARTS):
        piece = slice(part * size, (part + 1) * size)
        loads[part].wait()
        result = result + jnp.dot(attention[:, piece], wo[piece, :], preferred_element_type=F32)
    partial[...] = result.astype(BF16)
    for s, t, page, base, wanted in places:

        @pl.when(wanted)
        def _():
            for n in range(2):
                put(n, s, t, page, base).wait()


def finish_rows_kernel(groups, mig, lens, new_rows, *refs):
    *parts, mixed, near_out, far_out, scr = refs
    me = lax.axis_index("dec")
    slots = outgoing(mig, me, groups)
    width = parts[0].shape[1]
    terms = [part[...].astype(F32) for part in parts]
    level = 1
    while level < len(terms):
        terms = [terms[n] + terms[n ^ level] for n in range(len(terms))]
        level *= 2
    total = terms[0]
    slot_count, steps, _ = scr.shape
    for s in range(slot_count):
        live = (lens[me, s] > 0) & (s != slots[0]) & (s != slots[1])
        own = total[s * steps : (s + 1) * steps]
        scr[s, :, :width] = own
        scr[s, :, width:] = new_rows[s * steps : (s + 1) * steps, :].astype(F32)
        mixed[s] = jnp.where(live, own, 0.0).astype(BF16)
    for slot, out in zip(slots, (near_out, far_out)):
        out[...] = scr[jnp.maximum(slot, 0)].astype(BF16)


def place_kernel(groups, ways, mig, lens, table, *refs):
    near_pages, *far_pages = refs[: 1 + ways]
    near_rows, *far_rows = refs[1 + ways : 2 + 2 * ways]
    mixed_in, _, _, mixed, key_out, value_out, stage, lines, in_sems, line_sems, out_sems, own_sem = refs[
        2 + 2 * ways :
    ]
    me = lax.axis_index("dec")
    pages = table.shape[1]
    page_len, head_dim = stage.shape[2:]
    _, steps, width = mixed.shape
    *cases, far_gap = incoming(mig, lens, me, groups)
    row = lax.broadcasted_iota(jnp.int32, (page_len, head_dim), 0)

    def load(n, source):
        return pltpu.make_async_copy(source, stage.at[n], in_sems.at[n])

    def load_line(n, source):
        return pltpu.make_async_copy(source, lines.at[n], line_sems.at[n, 0])

    def store_line(n):
        return pltpu.make_async_copy(
            lines.at[n, :, pl.ds(0, width)], mixed.at[cases[n][0]], line_sems.at[n, 1]
        )

    def store(n, p, which):
        pool = (key_out, value_out)[which]
        page = table[0, p, cases[n][0]]
        return pltpu.make_async_copy(stage.at[n, which * pages + p], pool.at[page], out_sems.at[n, which, p])

    def each(do):
        for n in range(2):

            @pl.when(cases[n][0] >= 0)
            def _():
                do(n)

    def start(n):
        if n == 0 or ways == 1:
            load_line(n, (near_rows, far_rows[0])[n]).start()
            load(n, (near_pages, far_pages[0])[n]).start()
            return
        for way in range(ways):

            @pl.when((far_gap == 1) == (way == 0))
            def _():
                load_line(n, far_rows[way]).start()
                load(n, far_pages[way]).start()

    def patch(n):
        _, length = cases[n]
        load_line(n, near_rows).wait()
        store_line(n).start()
        fresh = lines[n, :, width:].astype(F32)
        load(n, near_pages).wait()
        for p in range(pages):
            at = row + p * page_len
            for which in range(2):
                page = stage[n, which * pages + p].astype(F32)
                page = jnp.where(at < length, page, 0.0)
                for t in range(steps):
                    page = jnp.where(
                        at == length + t, fresh[t : t + 1, which * head_dim : (which + 1) * head_dim], page
                    )
                stage[n, which * pages + p] = page.astype(BF16)
                store(n, p, which).start()

    def finish(n):
        store_line(n).wait()
        for p in range(pages):
            for which in range(2):
                store(n, p, which).wait()

    own = pltpu.make_async_copy(mixed_in, mixed, own_sem)
    own.start()
    each(start)
    own.wait()
    each(patch)
    each(finish)


def run(
    near_hops,
    far_hops,
    near,
    far,
    token,
    table,
    token_states,
    query_rows,
    key_weight,
    value_weight,
    out_weight,
    keys,
    values,
    cached_len,
    migrations,
):
    groups = lax.axis_size("dec")
    tp = lax.axis_size("tp")
    slot_count, steps, model = token_states.shape
    _, page_len, head_dim = keys.shape
    rows = slot_count * steps
    width = out_weight.shape[1]
    heads = query_rows.shape[2] // head_dim
    pages = table.shape[1]
    pool_shape = jax.ShapeDtypeStruct(keys.shape, BF16)
    limit = pltpu.CompilerParams(vmem_limit_bytes=63 * 2**20)

    pages_in = [lax.ppermute(near, "dec", near_hops)] + [lax.ppermute(far, "dec", hops) for hops in far_hops]

    key_mid, value_mid, partial, new_rows = pl.pallas_call(
        functools.partial(attend_kernel, groups),
        out_shape=(
            pool_shape,
            pool_shape,
            jax.ShapeDtypeStruct((rows, width), BF16),
            jax.ShapeDtypeStruct((rows, 2 * head_dim), BF16),
        ),
        in_specs=[SMEM] * 4 + [ANY] * 5 + [VMEM] * 2,
        out_specs=(HBM, HBM, VMEM, VMEM),
        scratch_shapes=[
            pltpu.VMEM(token_states.shape, BF16),
            pltpu.VMEM(query_rows.shape, BF16),
            pltpu.VMEM(key_weight.shape, BF16),
            pltpu.VMEM(value_weight.shape, BF16),
            pltpu.VMEM(out_weight.shape, BF16),
            pltpu.VMEM((heads * rows, head_dim), F32),
            pltpu.VMEM((heads * rows, head_dim), F32),
            pltpu.VMEM((2, slot_count, steps, 16, head_dim), BF16),
            pltpu.SemaphoreType.DMA((2 + 3 * PARTS,)),
            pltpu.SemaphoreType.DMA((2,)),
            pltpu.SemaphoreType.DMA((2, slot_count, steps)),
        ],
        compiler_params=pltpu.CompilerParams(vmem_limit_bytes=40 * 2**20),
        cost_estimate=pl.CostEstimate(flops=1_000_000, bytes_accessed=1_000_000, transcendentals=0),
        name="attend",
    )(
        token,
        migrations,
        cached_len,
        table,
        token_states,
        query_rows,
        key_weight,
        value_weight,
        out_weight,
        keys,
        values,
    )

    others = [lax.ppermute(partial, "tp", [(i, i ^ n) for i in range(tp)]) for n in range(1, tp)]
    row_shape = jax.ShapeDtypeStruct((steps, width + 2 * head_dim), BF16)
    mixed, near_row, far_row = pl.pallas_call(
        functools.partial(finish_rows_kernel, groups),
        out_shape=(jax.ShapeDtypeStruct((slot_count, steps, width), BF16), row_shape, row_shape),
        in_specs=[SMEM, SMEM, VMEM] + [VMEM] * tp,
        out_specs=(VMEM, VMEM, VMEM),
        scratch_shapes=[pltpu.VMEM((slot_count, steps, width + 2 * head_dim), F32)],
        compiler_params=pltpu.CompilerParams(vmem_limit_bytes=8 * 2**20),
        name="rows",
    )(migrations, cached_len, new_rows, partial, *others)
    rows_in = [lax.ppermute(near_row, "dec", near_hops)] + [lax.ppermute(far_row, "dec", hops) for hops in far_hops]
    return pages_in, rows_in, mixed, key_mid, value_mid


def moved(table, inputs):
    groups = lax.axis_size("dec")
    half = groups // 2
    keys, values, _, migrations = inputs[-4:]
    _, page_len, head_dim = keys.shape
    pages = table.shape[1]
    moved_shape = jax.ShapeDtypeStruct((2 * pages, page_len, head_dim), BF16)
    near, far, token = pl.pallas_call(
        functools.partial(pack_kernel, groups),
        out_shape=(moved_shape, moved_shape, jax.ShapeDtypeStruct((1,), jnp.int32)),
        in_specs=[SMEM, SMEM, HBM, HBM],
        out_specs=(VMEM, VMEM, SMEM),
        scratch_shapes=[pltpu.SemaphoreType.DMA((2, 2, pages))],
        compiler_params=pltpu.CompilerParams(vmem_limit_bytes=40 * 2**20),
        cost_estimate=pl.CostEstimate(flops=0, bytes_accessed=1_000_000, transcendentals=0),
        name="pack",
    )(migrations, table, keys, values)
    if half != 2:
        far_hops = (shifted(groups, 1), shifted(groups, 1 + half))
        return run(shifted(groups, half), far_hops, near, far, token, table, *inputs)
    branches = []
    for case in range(2**half):
        senders = [pair + half * (case >> pair & 1) for pair in range(half)]
        receivers = [(sender + half) % groups for sender in senders]
        near_hops = [(senders[pair], receivers[pair]) for pair in range(half)]
        far_hops = [(senders[pair], receivers[(pair + 1) % half]) for pair in range(half)]
        near_hops += [(b, a) for a, b in near_hops]
        far_hops += [(b, a) for a, b in far_hops]
        branches.append(functools.partial(run, near_hops, (far_hops,)))
    return lax.switch(token[0], branches, near, far, token, table, *inputs)


def local(
    token_states,
    query_rows,
    key_weight,
    value_weight,
    out_weight,
    key_pool,
    value_pool,
    cached_len,
    page_table,
    migrations,
):
    groups = lax.axis_size("dec")
    pool_pages, _, page_len, head_dim = key_pool.shape
    slot_count, steps, _ = token_states.shape
    keys = key_pool.reshape(pool_pages, page_len, head_dim)
    values = value_pool.reshape(pool_pages, page_len, head_dim)
    table = jnp.swapaxes(page_table, 1, 2)
    pages = table.shape[1]
    inputs = (
        token_states,
        query_rows,
        key_weight,
        value_weight,
        out_weight,
        keys,
        values,
        cached_len,
        migrations,
    )
    pages_in, rows_in, mixed_mid, key_mid, value_mid = moved(table, inputs)
    ways = len(pages_in) - 1
    pool_shape = jax.ShapeDtypeStruct(keys.shape, BF16)
    mixed_shape = jax.ShapeDtypeStruct((slot_count, steps, out_weight.shape[1]), BF16)
    mixed, key_out, value_out = pl.pallas_call(
        functools.partial(place_kernel, groups, ways),
        out_shape=(mixed_shape, pool_shape, pool_shape),
        in_specs=[SMEM] * 3 + [ANY] * (2 + 2 * ways) + [VMEM] + [HBM] * 2,
        out_specs=(HBM, HBM, HBM),
        scratch_shapes=[
            pltpu.VMEM((2, 2 * pages, page_len, head_dim), BF16),
            pltpu.VMEM((2,) + rows_in[0].shape, BF16),
            pltpu.SemaphoreType.DMA((2,)),
            pltpu.SemaphoreType.DMA((2, 2)),
            pltpu.SemaphoreType.DMA((2, 2, pages)),
            pltpu.SemaphoreType.DMA,
        ],
        input_output_aliases={6 + 2 * ways: 1, 7 + 2 * ways: 2},
        compiler_params=pltpu.CompilerParams(vmem_limit_bytes=63 * 2**20),
        name="place",
    )(migrations, cached_len, table, *pages_in, *rows_in, mixed_mid, key_mid, value_mid)
    return mixed, key_out.reshape(key_pool.shape), value_out.reshape(value_pool.shape)


def solution(mesh):
    placed = (
        P(("rep", "dec"), None, None),
        P(("rep", "dec"), None, "tp"),
        P(None, "tp"),
        P(None, "tp"),
        P("tp", None),
        P(("rep", "dec"), "tp", None, None),
        P(("rep", "dec"), "tp", None, None),
        P("rep", None),
        P(("rep", "dec"), None, None),
        P("rep", None),
    )
    return jax.shard_map(
        local,
        mesh=mesh,
        in_specs=placed,
        out_specs=(
            P(("rep", "dec"), None, None),
            P(("rep", "dec"), "tp", None, None),
            P(("rep", "dec"), "tp", None, None),
        ),
        check_vma=False,
    )
```

```python
import functools

import jax
import jax.numpy as jnp
from jax import lax
from jax.experimental import pallas as pl
from jax.experimental.pallas import tpu as pltpu
from jax.sharding import PartitionSpec as P

F32 = jnp.float32
BF16 = jnp.bfloat16
PARTS = 4
SMEM = pl.BlockSpec(memory_space=pltpu.SMEM)
HBM = pl.BlockSpec(memory_space=pltpu.HBM)
ANY = pl.BlockSpec(memory_space=pl.ANY)
VMEM = pl.BlockSpec(memory_space=pltpu.VMEM)


def shifted(count, by):
    return [(i, (i + by) % count) for i in range(count)]


def outgoing(mig, me, groups):
    half = groups // 2
    near = far = jnp.int32(-1)
    for m in range(mig.shape[0]):
        mine = mig[m, 0] == me
        gap = lax.rem(mig[m, 2] - me + groups, groups)
        near = jnp.where(mine & (gap == half), mig[m, 1], near)
        far = jnp.where(mine & (gap != half), mig[m, 1], far)
    return near, far


def incoming(mig, lens, me, groups):
    half = groups // 2
    near = far = jnp.int32(-1)
    near_len = far_len = far_gap = jnp.int32(0)
    for m in range(mig.shape[0]):
        mine = mig[m, 2] == me
        gap = lax.rem(me - mig[m, 0] + groups, groups)
        length = lens[mig[m, 0], mig[m, 1]]
        is_near = mine & (gap == half)
        is_far = mine & (gap != half)
        near = jnp.where(is_near, mig[m, 3], near)
        near_len = jnp.where(is_near, length, near_len)
        far = jnp.where(is_far, mig[m, 3], far)
        far_len = jnp.where(is_far, length, far_len)
        far_gap = jnp.where(is_far, gap, far_gap)
    return (near, near_len), (far, far_len), far_gap


def pack_kernel(groups, mig, table, key_pool, value_pool, near_out, far_out, token, sems):
    me = lax.axis_index("dec")
    pages = table.shape[1]
    outs = (near_out, far_out)
    slots = outgoing(mig, me, groups)

    def load(n, which, p):
        page = table[0, p, slots[n]]
        pool = (key_pool, value_pool)[which]
        return pltpu.make_async_copy(pool.at[page], outs[n].at[which * pages + p], sems.at[n, which, p])

    def each(do):
        for n in range(2):

            @pl.when(slots[n] >= 0)
            def _():
                for p in range(pages):
                    for which in range(2):
                        do(load(n, which, p))

    each(lambda copy: copy.start())
    half = groups // 2
    number = jnp.int32(0)
    if half == 2:
        for m in range(mig.shape[0]):
            number = number | jnp.where(mig[m, 0] >= half, mig[m, 0] - half + 1, 0)
    token[0] = number
    each(lambda copy: copy.wait())


def attend_kernel(
    groups,
    token,
    mig,
    lens,
    table,
    states_hbm,
    query_hbm,
    key_weight,
    value_weight,
    out_weight,
    kp,
    vp,
    key_out,
    value_out,
    partial,
    new_rows,
    states,
    query,
    wk,
    wv,
    wo,
    q_scr,
    a_scr,
    tiles,
    load_sems,
    store_sems,
    tile_sems,
):
    del token
    me = lax.axis_index("dec")
    slot_count, steps, _ = states.shape
    rows = slot_count * steps
    pages = table.shape[1]
    page_len, head_dim = kp.shape[1:]
    heads = query.shape[2] // head_dim
    span = pages * page_len
    pools = ((kp, key_out, 0), (vp, value_out, head_dim))
    number = 0

    def split(source, target, parts):
        nonlocal number
        size = source.shape[0] // parts
        copies = []
        for part in range(parts):
            piece = pl.ds(part * size, size)
            copies.append(pltpu.make_async_copy(source.at[piece], target.at[piece], load_sems.at[number]))
            number += 1
        return copies

    (load_query,) = split(query_hbm, query, 1)
    (load_states,) = split(states_hbm, states, 1)
    load_wk = split(key_weight, wk, PARTS)
    load_wv = split(value_weight, wv, PARTS)
    loads = split(out_weight, wo, PARTS)
    stores = [pltpu.make_async_copy(pool, out, store_sems.at[n]) for n, (pool, out, _) in enumerate(pools)]
    for copy in [load_query, load_states] + load_wk + load_wv + loads + stores:
        copy.start()
    near, far = outgoing(mig, me, groups)
    lengths = [lens[me, s] for s in range(slot_count)]
    numbers = [[table[0, p, s] for p in range(pages)] for s in range(slot_count)]

    load_query.wait()
    for s in range(slot_count):
        qf = query[s].astype(F32)
        for h in range(heads):
            q_scr[pl.ds(h * rows + s * steps, steps), :] = qf[:, h * head_dim : (h + 1) * head_dim]

    count = steps * heads
    nt = (((1,), (1,)), ((), ()))
    queries = jnp.concatenate(
        [q_scr[pl.ds(r, heads, stride=rows), :] for r in range(rows)], 0
    ).astype(BF16)
    position = lax.broadcasted_iota(jnp.int32, (count, span), 1)
    scaling = head_dim**-0.5
    blank = jnp.zeros((count, head_dim), BF16)
    scores = []
    for a in range(0, slot_count, 2):
        pair = (a, a + 1)
        keys = jnp.concatenate(
            [jnp.concatenate([kp[numbers[s][p]] for s in pair], 1) for p in range(pages)], 0
        )
        left = jnp.concatenate([queries[a * count : (a + 1) * count], blank], 1)
        right = jnp.concatenate([blank, queries[(a + 1) * count : (a + 2) * count]], 1)
        both = lax.dot_general(
            jnp.concatenate([left, right], 0), keys, nt, preferred_element_type=F32
        )
        for n, s in enumerate(pair):
            part = both[n * count : (n + 1) * count] * scaling
            scores.append(jnp.where(position < lengths[s], part, -jnp.inf))
    cached = jnp.concatenate(scores, 0)

    load_states.wait()
    x = jnp.concatenate([states[s].astype(F32) for s in range(slot_count)], 0).astype(BF16)
    fresh_rows = jnp.zeros((rows, 2 * head_dim), F32)
    size = wk.shape[0] // PARTS
    for part in range(PARTS):
        piece = slice(part * size, (part + 1) * size)
        load_wk[part].wait()
        load_wv[part].wait()
        weight = jnp.concatenate([wk[piece, :], wv[piece, :]], 1)
        fresh_rows = fresh_rows + jnp.dot(x[:, piece], weight, preferred_element_type=F32)
    fresh_k = fresh_rows[:, :head_dim].astype(BF16)
    fresh_v = fresh_rows[:, head_dim:].astype(BF16)
    new_rows[:, :head_dim] = fresh_k
    new_rows[:, head_dim:] = fresh_v

    fresh = lax.dot_general(queries, fresh_k, nt, preferred_element_type=F32) * scaling
    fresh_row = lax.broadcasted_iota(jnp.int32, fresh.shape, 0)
    fresh_col = lax.broadcasted_iota(jnp.int32, fresh.shape, 1)
    first = fresh_row // count * steps
    allowed = (fresh_col >= first) & (fresh_col <= fresh_row // heads)
    fresh = jnp.where(allowed, fresh, -jnp.inf)
    peak = jnp.maximum(jnp.max(cached, 1, keepdims=True), jnp.max(fresh, 1, keepdims=True))
    cached = jnp.exp(cached - peak)
    fresh = jnp.exp(fresh - peak)
    share = 1.0 / (jnp.sum(cached, 1, keepdims=True) + jnp.sum(fresh, 1, keepdims=True))
    cached_w = (cached * share).astype(BF16)
    fresh_w = (fresh * share).astype(BF16)
    fresh_out = jnp.dot(fresh_w, fresh_v, preferred_element_type=F32)
    for a in range(0, slot_count, 2):
        pair = (a, a + 1)
        values = jnp.concatenate(
            [jnp.concatenate([vp[numbers[s][p]] for s in pair], 1) for p in range(pages)], 0
        )
        both = jnp.dot(cached_w[a * count : (a + 2) * count], values, preferred_element_type=F32)
        for n, s in enumerate(pair):
            out = both[n * count : (n + 1) * count, n * head_dim : (n + 1) * head_dim]
            out = out + fresh_out[s * count : (s + 1) * count]
            for t in range(steps):
                a_scr[pl.ds(s * steps + t, heads, stride=rows), :] = out[t * heads : (t + 1) * heads]

    tile = tiles.shape[3]
    row = lax.broadcasted_iota(jnp.int32, (tile, head_dim), 0)
    fresh_f = (fresh_k.astype(F32), fresh_v.astype(F32))
    places = []
    for s in range(slot_count):
        live = (lengths[s] > 0) & (s != near) & (s != far)
        for t in range(steps):
            at = lengths[s] + t
            page = table[0, at // page_len, s]
            low = at // tile * tile
            base = pl.multiple_of(lax.rem(low, page_len), tile)
            places.append((s, t, page, base, live & ((t == 0) | (lax.rem(at, tile) == 0))))
            for n, (pool, _, _) in enumerate(pools):
                merged = pool[page, pl.ds(base, tile), :].astype(F32)
                for u in range(steps):
                    line = fresh_f[n][s * steps + u : s * steps + u + 1]
                    merged = jnp.where(row + low == lengths[s] + u, line, merged)
                tiles[n, s, t] = merged.astype(BF16)
    for store in stores:
        store.wait()

    def put(n, s, t, page, base):
        return pltpu.make_async_copy(
            tiles.at[n, s, t], pools[n][1].at[page, pl.ds(base, tile), :], tile_sems.at[n, s, t]
        )

    for s, t, page, base, wanted in places:

        @pl.when(wanted)
        def _():
            for n in range(2):
                put(n, s, t, page, base).start()

    attention = jnp.concatenate([a_scr[h * rows : (h + 1) * rows, :].astype(BF16) for h in range(heads)], 1)
    result = jnp.zeros((rows, wo.shape[1]), F32)
    size = wo.shape[0] // PARTS
    for part in range(PARTS):
        piece = slice(part * size, (part + 1) * size)
        loads[part].wait()
        result = result + jnp.dot(attention[:, piece], wo[piece, :], preferred_element_type=F32)
    partial[...] = result.astype(BF16)
    for s, t, page, base, wanted in places:

        @pl.when(wanted)
        def _():
            for n in range(2):
                put(n, s, t, page, base).wait()


def finish_rows_kernel(groups, mig, lens, new_rows, *refs):
    *parts, mixed, near_out, far_out, scr = refs
    me = lax.axis_index("dec")
    slots = outgoing(mig, me, groups)
    width = parts[0].shape[1]
    terms = [part[...].astype(F32) for part in parts]
    level = 1
    while level < len(terms):
        terms = [terms[n] + terms[n ^ level] for n in range(len(terms))]
        level *= 2
    total = terms[0]
    slot_count, steps, _ = scr.shape
    for s in range(slot_count):
        live = (lens[me, s] > 0) & (s != slots[0]) & (s != slots[1])
        own = total[s * steps : (s + 1) * steps]
        scr[s, :, :width] = own
        scr[s, :, width:] = new_rows[s * steps : (s + 1) * steps, :].astype(F32)
        mixed[s] = jnp.where(live, own, 0.0).astype(BF16)
    for slot, out in zip(slots, (near_out, far_out)):
        out[...] = scr[jnp.maximum(slot, 0)].astype(BF16)


def place_kernel(groups, ways, mig, lens, table, *refs):
    near_pages, *far_pages = refs[: 1 + ways]
    near_rows, *far_rows = refs[1 + ways : 2 + 2 * ways]
    mixed_in, _, _, mixed, key_out, value_out, stage, lines, in_sems, line_sems, out_sems, own_sem = refs[
        2 + 2 * ways :
    ]
    me = lax.axis_index("dec")
    pages = table.shape[1]
    page_len, head_dim = stage.shape[2:]
    _, steps, width = mixed.shape
    *cases, far_gap = incoming(mig, lens, me, groups)
    row = lax.broadcasted_iota(jnp.int32, (page_len, head_dim), 0)

    def load(n, p, which, source):
        at = which * pages + p
        return pltpu.make_async_copy(source.at[at], stage.at[n, at], in_sems.at[n, at])

    def load_line(n, source):
        return pltpu.make_async_copy(source, lines.at[n], line_sems.at[n, 0])

    def store_line(n):
        return pltpu.make_async_copy(
            lines.at[n, :, pl.ds(0, width)], mixed.at[cases[n][0]], line_sems.at[n, 1]
        )

    def store(n, p, which):
        pool = (key_out, value_out)[which]
        page = table[0, p, cases[n][0]]
        return pltpu.make_async_copy(stage.at[n, which * pages + p], pool.at[page], out_sems.at[n, which, p])

    def each(do):
        for n in range(2):

            @pl.when(cases[n][0] >= 0)
            def _():
                do(n)

    def start_from(n, page_source, line_source):
        load_line(n, line_source).start()
        for p in range(pages):
            for which in range(2):
                load(n, p, which, page_source).start()

    def start(n):
        if n == 0 or ways == 1:
            start_from(n, (near_pages, far_pages[0])[n], (near_rows, far_rows[0])[n])
            return
        for way in range(ways):

            @pl.when((far_gap == 1) == (way == 0))
            def _():
                start_from(n, far_pages[way], far_rows[way])

    def patch(n):
        _, length = cases[n]
        load_line(n, near_rows).wait()
        store_line(n).start()
        fresh = lines[n, :, width:].astype(F32)
        for p in range(pages):
            at = row + p * page_len
            for which in range(2):
                load(n, p, which, near_pages).wait()

            @pl.when(length < (p + 1) * page_len)
            def _():
                for which in range(2):
                    page = stage[n, which * pages + p].astype(F32)
                    page = jnp.where(at < length, page, 0.0)
                    for t in range(steps):
                        line = fresh[t : t + 1, which * head_dim : (which + 1) * head_dim]
                        page = jnp.where(at == length + t, line, page)
                    stage[n, which * pages + p] = page.astype(BF16)

            for which in range(2):
                store(n, p, which).start()

    def finish(n):
        store_line(n).wait()
        for p in range(pages):
            for which in range(2):
                store(n, p, which).wait()

    own = pltpu.make_async_copy(mixed_in, mixed, own_sem)
    own.start()
    each(start)
    own.wait()
    each(patch)
    each(finish)


def run(
    near_hops,
    far_hops,
    near,
    far,
    token,
    table,
    token_states,
    query_rows,
    key_weight,
    value_weight,
    out_weight,
    keys,
    values,
    cached_len,
    migrations,
):
    groups = lax.axis_size("dec")
    tp = lax.axis_size("tp")
    slot_count, steps, model = token_states.shape
    _, page_len, head_dim = keys.shape
    rows = slot_count * steps
    width = out_weight.shape[1]
    heads = query_rows.shape[2] // head_dim
    pages = table.shape[1]
    pool_shape = jax.ShapeDtypeStruct(keys.shape, BF16)
    limit = pltpu.CompilerParams(vmem_limit_bytes=63 * 2**20)

    pages_in = [lax.ppermute(near, "dec", near_hops)] + [lax.ppermute(far, "dec", hops) for hops in far_hops]

    key_mid, value_mid, partial, new_rows = pl.pallas_call(
        functools.partial(attend_kernel, groups),
        out_shape=(
            pool_shape,
            pool_shape,
            jax.ShapeDtypeStruct((rows, width), BF16),
            jax.ShapeDtypeStruct((rows, 2 * head_dim), BF16),
        ),
        in_specs=[SMEM] * 4 + [ANY] * 5 + [VMEM] * 2,
        out_specs=(HBM, HBM, VMEM, VMEM),
        scratch_shapes=[
            pltpu.VMEM(token_states.shape, BF16),
            pltpu.VMEM(query_rows.shape, BF16),
            pltpu.VMEM(key_weight.shape, BF16),
            pltpu.VMEM(value_weight.shape, BF16),
            pltpu.VMEM(out_weight.shape, BF16),
            pltpu.VMEM((heads * rows, head_dim), F32),
            pltpu.VMEM((heads * rows, head_dim), F32),
            pltpu.VMEM((2, slot_count, steps, 16, head_dim), BF16),
            pltpu.SemaphoreType.DMA((2 + 3 * PARTS,)),
            pltpu.SemaphoreType.DMA((2,)),
            pltpu.SemaphoreType.DMA((2, slot_count, steps)),
        ],
        compiler_params=pltpu.CompilerParams(vmem_limit_bytes=40 * 2**20),
        cost_estimate=pl.CostEstimate(flops=1_000_000, bytes_accessed=1_000_000, transcendentals=0),
        name="attend",
    )(
        token,
        migrations,
        cached_len,
        table,
        token_states,
        query_rows,
        key_weight,
        value_weight,
        out_weight,
        keys,
        values,
    )

    others = [lax.ppermute(partial, "tp", [(i, i ^ n) for i in range(tp)]) for n in range(1, tp)]
    row_shape = jax.ShapeDtypeStruct((steps, width + 2 * head_dim), BF16)
    mixed, near_row, far_row = pl.pallas_call(
        functools.partial(finish_rows_kernel, groups),
        out_shape=(jax.ShapeDtypeStruct((slot_count, steps, width), BF16), row_shape, row_shape),
        in_specs=[SMEM, SMEM, VMEM] + [VMEM] * tp,
        out_specs=(VMEM, VMEM, VMEM),
        scratch_shapes=[pltpu.VMEM((slot_count, steps, width + 2 * head_dim), F32)],
        compiler_params=pltpu.CompilerParams(vmem_limit_bytes=8 * 2**20),
        name="rows",
    )(migrations, cached_len, new_rows, partial, *others)
    rows_in = [lax.ppermute(near_row, "dec", near_hops)] + [lax.ppermute(far_row, "dec", hops) for hops in far_hops]
    return pages_in, rows_in, mixed, key_mid, value_mid


def moved(table, inputs):
    groups = lax.axis_size("dec")
    half = groups // 2
    keys, values, _, migrations = inputs[-4:]
    _, page_len, head_dim = keys.shape
    pages = table.shape[1]
    moved_shape = jax.ShapeDtypeStruct((2 * pages, page_len, head_dim), BF16)
    near, far, token = pl.pallas_call(
        functools.partial(pack_kernel, groups),
        out_shape=(moved_shape, moved_shape, jax.ShapeDtypeStruct((1,), jnp.int32)),
        in_specs=[SMEM, SMEM, HBM, HBM],
        out_specs=(VMEM, VMEM, SMEM),
        scratch_shapes=[pltpu.SemaphoreType.DMA((2, 2, pages))],
        compiler_params=pltpu.CompilerParams(vmem_limit_bytes=40 * 2**20),
        cost_estimate=pl.CostEstimate(flops=0, bytes_accessed=1_000_000, transcendentals=0),
        name="pack",
    )(migrations, table, keys, values)
    if half != 2:
        far_hops = (shifted(groups, 1), shifted(groups, 1 + half))
        return run(shifted(groups, half), far_hops, near, far, token, table, *inputs)
    branches = []
    for case in range(2**half):
        senders = [pair + half * (case >> pair & 1) for pair in range(half)]
        receivers = [(sender + half) % groups for sender in senders]
        near_hops = [(senders[pair], receivers[pair]) for pair in range(half)]
        far_hops = [(senders[pair], receivers[(pair + 1) % half]) for pair in range(half)]
        near_hops += [(b, a) for a, b in near_hops]
        far_hops += [(b, a) for a, b in far_hops]
        branches.append(functools.partial(run, near_hops, (far_hops,)))
    return lax.switch(token[0], branches, near, far, token, table, *inputs)


def local(
    token_states,
    query_rows,
    key_weight,
    value_weight,
    out_weight,
    key_pool,
    value_pool,
    cached_len,
    page_table,
    migrations,
):
    groups = lax.axis_size("dec")
    pool_pages, _, page_len, head_dim = key_pool.shape
    slot_count, steps, _ = token_states.shape
    keys = key_pool.reshape(pool_pages, page_len, head_dim)
    values = value_pool.reshape(pool_pages, page_len, head_dim)
    table = jnp.swapaxes(page_table, 1, 2)
    pages = table.shape[1]
    inputs = (
        token_states,
        query_rows,
        key_weight,
        value_weight,
        out_weight,
        keys,
        values,
        cached_len,
        migrations,
    )
    pages_in, rows_in, mixed_mid, key_mid, value_mid = moved(table, inputs)
    ways = len(pages_in) - 1
    pool_shape = jax.ShapeDtypeStruct(keys.shape, BF16)
    mixed_shape = jax.ShapeDtypeStruct((slot_count, steps, out_weight.shape[1]), BF16)
    mixed, key_out, value_out = pl.pallas_call(
        functools.partial(place_kernel, groups, ways),
        out_shape=(mixed_shape, pool_shape, pool_shape),
        in_specs=[SMEM] * 3 + [ANY] * (2 + 2 * ways) + [VMEM] + [HBM] * 2,
        out_specs=(HBM, HBM, HBM),
        scratch_shapes=[
            pltpu.VMEM((2, 2 * pages, page_len, head_dim), BF16),
            pltpu.VMEM((2,) + rows_in[0].shape, BF16),
            pltpu.SemaphoreType.DMA((2, 2 * pages)),
            pltpu.SemaphoreType.DMA((2, 2)),
            pltpu.SemaphoreType.DMA((2, 2, pages)),
            pltpu.SemaphoreType.DMA,
        ],
        input_output_aliases={6 + 2 * ways: 1, 7 + 2 * ways: 2},
        compiler_params=pltpu.CompilerParams(vmem_limit_bytes=63 * 2**20),
        name="place",
    )(migrations, cached_len, table, *pages_in, *rows_in, mixed_mid, key_mid, value_mid)
    return mixed, key_out.reshape(key_pool.shape), value_out.reshape(value_pool.shape)


def solution(mesh):
    placed = (
        P(("rep", "dec"), None, None),
        P(("rep", "dec"), None, "tp"),
        P(None, "tp"),
        P(None, "tp"),
        P("tp", None),
        P(("rep", "dec"), "tp", None, None),
        P(("rep", "dec"), "tp", None, None),
        P("rep", None),
        P(("rep", "dec"), None, None),
        P("rep", None),
    )
    return jax.shard_map(
        local,
        mesh=mesh,
        in_specs=placed,
        out_specs=(
            P(("rep", "dec"), None, None),
            P(("rep", "dec"), "tp", None, None),
            P(("rep", "dec"), "tp", None, None),
        ),
        check_vma=False,
    )
```

```python
import functools

import jax
import jax.numpy as jnp
from jax import lax
from jax.experimental import pallas as pl
from jax.experimental.pallas import tpu as pltpu
from jax.sharding import PartitionSpec as P

F32 = jnp.float32
BF16 = jnp.bfloat16
PARTS = 4
SMEM = pl.BlockSpec(memory_space=pltpu.SMEM)
HBM = pl.BlockSpec(memory_space=pltpu.HBM)
ANY = pl.BlockSpec(memory_space=pl.ANY)
VMEM = pl.BlockSpec(memory_space=pltpu.VMEM)


def shifted(count, by):
    return [(i, (i + by) % count) for i in range(count)]


def outgoing(mig, me, groups):
    half = groups // 2
    near = far = jnp.int32(-1)
    for m in range(mig.shape[0]):
        mine = mig[m, 0] == me
        gap = lax.rem(mig[m, 2] - me + groups, groups)
        near = jnp.where(mine & (gap == half), mig[m, 1], near)
        far = jnp.where(mine & (gap != half), mig[m, 1], far)
    return near, far


def incoming(mig, lens, me, groups):
    half = groups // 2
    near = far = jnp.int32(-1)
    near_len = far_len = far_gap = jnp.int32(0)
    for m in range(mig.shape[0]):
        mine = mig[m, 2] == me
        gap = lax.rem(me - mig[m, 0] + groups, groups)
        length = lens[mig[m, 0], mig[m, 1]]
        is_near = mine & (gap == half)
        is_far = mine & (gap != half)
        near = jnp.where(is_near, mig[m, 3], near)
        near_len = jnp.where(is_near, length, near_len)
        far = jnp.where(is_far, mig[m, 3], far)
        far_len = jnp.where(is_far, length, far_len)
        far_gap = jnp.where(is_far, gap, far_gap)
    return (near, near_len), (far, far_len), far_gap


NUMBER, OUT_NEAR, OUT_FAR, IN_NEAR, NEAR_LEN, IN_FAR, FAR_LEN, FAR_GAP, LENGTHS = range(9)


def pack_kernel(groups, mig, lens, table, key_pool, value_pool, near_out, far_out, facts, sems):
    me = lax.axis_index("dec")
    _, pages, slot_count = table.shape
    outs = (near_out, far_out)
    slots = outgoing(mig, me, groups)

    def load(n, which, p):
        page = table[0, p, slots[n]]
        pool = (key_pool, value_pool)[which]
        return pltpu.make_async_copy(pool.at[page], outs[n].at[which * pages + p], sems.at[n, which, p])

    def each(do):
        for n in range(2):

            @pl.when(slots[n] >= 0)
            def _():
                for p in range(pages):
                    for which in range(2):
                        do(load(n, which, p))

    each(lambda copy: copy.start())
    half = groups // 2
    number = jnp.int32(0)
    if half == 2:
        for m in range(mig.shape[0]):
            number = number | jnp.where(mig[m, 0] >= half, mig[m, 0] - half + 1, 0)
    facts[NUMBER] = number
    facts[OUT_NEAR], facts[OUT_FAR] = slots
    near, far, far_gap = incoming(mig, lens, me, groups)
    facts[IN_NEAR], facts[NEAR_LEN] = near
    facts[IN_FAR], facts[FAR_LEN] = far
    facts[FAR_GAP] = far_gap
    for s in range(slot_count):
        facts[LENGTHS + s] = lens[me, s]
        for p in range(pages):
            facts[LENGTHS + slot_count + s * pages + p] = table[0, p, s]
    each(lambda copy: copy.wait())


def attend_kernel(
    facts,
    states_hbm,
    query_hbm,
    key_weight,
    value_weight,
    out_weight,
    kp,
    vp,
    mig,
    lens,
    table,
    key_out,
    value_out,
    partial,
    new_rows,
    states,
    query,
    wk,
    wv,
    wo,
    q_scr,
    a_scr,
    tiles,
    load_sems,
    store_sems,
    tile_sems,
):
    del mig, lens, table
    slot_count, steps, _ = states.shape
    rows = slot_count * steps
    page_len, head_dim = kp.shape[1:]
    pages = kp.shape[0] // slot_count
    heads = query.shape[2] // head_dim
    span = pages * page_len
    pools = ((kp, key_out, 0), (vp, value_out, head_dim))
    number = 0

    def split(source, target, parts):
        nonlocal number
        size = source.shape[0] // parts
        copies = []
        for part in range(parts):
            piece = pl.ds(part * size, size)
            copies.append(pltpu.make_async_copy(source.at[piece], target.at[piece], load_sems.at[number]))
            number += 1
        return copies

    (load_query,) = split(query_hbm, query, 1)
    (load_states,) = split(states_hbm, states, 1)
    load_wk = split(key_weight, wk, PARTS)
    load_wv = split(value_weight, wv, PARTS)
    loads = split(out_weight, wo, PARTS)
    stores = [pltpu.make_async_copy(pool, out, store_sems.at[n]) for n, (pool, out, _) in enumerate(pools)]
    for copy in [load_query, load_states] + load_wk + load_wv + loads + stores:
        copy.start()
    near, far = facts[OUT_NEAR], facts[OUT_FAR]
    lengths = [facts[LENGTHS + s] for s in range(slot_count)]
    first_page = [LENGTHS + slot_count + s * pages for s in range(slot_count)]
    numbers = [[facts[first_page[s] + p] for p in range(pages)] for s in range(slot_count)]

    load_query.wait()
    for s in range(slot_count):
        qf = query[s].astype(F32)
        for h in range(heads):
            q_scr[pl.ds(h * rows + s * steps, steps), :] = qf[:, h * head_dim : (h + 1) * head_dim]

    count = steps * heads
    nt = (((1,), (1,)), ((), ()))
    queries = jnp.concatenate(
        [q_scr[pl.ds(r, heads, stride=rows), :] for r in range(rows)], 0
    ).astype(BF16)
    position = lax.broadcasted_iota(jnp.int32, (count, span), 1)
    scaling = head_dim**-0.5
    scores = []
    for s in range(slot_count):
        keys = jnp.concatenate([kp[n] for n in numbers[s]], 0)
        cached = lax.dot_general(
            queries[s * count : (s + 1) * count], keys, nt, preferred_element_type=F32
        )
        scores.append(jnp.where(position < lengths[s], cached * scaling, -jnp.inf))
    cached = jnp.concatenate(scores, 0)

    load_states.wait()
    x = jnp.concatenate([states[s].astype(F32) for s in range(slot_count)], 0).astype(BF16)
    fresh_k = jnp.zeros((rows, head_dim), F32)
    fresh_v = jnp.zeros((rows, head_dim), F32)
    size = wk.shape[0] // PARTS
    for part in range(PARTS):
        piece = slice(part * size, (part + 1) * size)
        load_wk[part].wait()
        fresh_k = fresh_k + jnp.dot(x[:, piece], wk[piece, :], preferred_element_type=F32)
        load_wv[part].wait()
        fresh_v = fresh_v + jnp.dot(x[:, piece], wv[piece, :], preferred_element_type=F32)
    fresh_k = fresh_k.astype(BF16)
    fresh_v = fresh_v.astype(BF16)
    new_rows[:, :head_dim] = fresh_k
    new_rows[:, head_dim:] = fresh_v

    fresh = lax.dot_general(queries, fresh_k, nt, preferred_element_type=F32) * scaling
    fresh_row = lax.broadcasted_iota(jnp.int32, fresh.shape, 0)
    fresh_col = lax.broadcasted_iota(jnp.int32, fresh.shape, 1)
    first = fresh_row // count * steps
    allowed = (fresh_col >= first) & (fresh_col <= fresh_row // heads)
    fresh = jnp.where(allowed, fresh, -jnp.inf)
    peak = jnp.maximum(jnp.max(cached, 1, keepdims=True), jnp.max(fresh, 1, keepdims=True))
    cached = jnp.exp(cached - peak)
    fresh = jnp.exp(fresh - peak)
    share = 1.0 / (jnp.sum(cached, 1, keepdims=True) + jnp.sum(fresh, 1, keepdims=True))
    cached_w = (cached * share).astype(BF16)
    fresh_w = (fresh * share).astype(BF16)
    fresh_out = jnp.dot(fresh_w, fresh_v, preferred_element_type=F32)
    for s in range(slot_count):
        values = jnp.concatenate([vp[n] for n in numbers[s]], 0)
        piece = slice(s * count, (s + 1) * count)
        out = jnp.dot(cached_w[piece], values, preferred_element_type=F32) + fresh_out[piece]
        for t in range(steps):
            a_scr[pl.ds(s * steps + t, heads, stride=rows), :] = out[t * heads : (t + 1) * heads]

    tile = tiles.shape[3]
    row = lax.broadcasted_iota(jnp.int32, (tile, head_dim), 0)
    fresh_f = (fresh_k.astype(F32), fresh_v.astype(F32))
    places = []
    for s in range(slot_count):
        live = (lengths[s] > 0) & (s != near) & (s != far)
        for t in range(steps):
            at = lengths[s] + t
            page = facts[first_page[s] + at // page_len]
            low = at // tile * tile
            base = pl.multiple_of(lax.rem(low, page_len), tile)
            places.append((s, t, page, base, live & ((t == 0) | (lax.rem(at, tile) == 0))))
            for n, (pool, _, _) in enumerate(pools):
                merged = pool[page, pl.ds(base, tile), :].astype(F32)
                for u in range(steps):
                    line = fresh_f[n][s * steps + u : s * steps + u + 1]
                    merged = jnp.where(row + low == lengths[s] + u, line, merged)
                tiles[n, s, t] = merged.astype(BF16)
    for store in stores:
        store.wait()

    def put(n, s, t, page, base):
        return pltpu.make_async_copy(
            tiles.at[n, s, t], pools[n][1].at[page, pl.ds(base, tile), :], tile_sems.at[n, s, t]
        )

    for s, t, page, base, wanted in places:

        @pl.when(wanted)
        def _():
            for n in range(2):
                put(n, s, t, page, base).start()

    attention = jnp.concatenate([a_scr[h * rows : (h + 1) * rows, :].astype(BF16) for h in range(heads)], 1)
    result = jnp.zeros((rows, wo.shape[1]), F32)
    size = wo.shape[0] // PARTS
    for part in range(PARTS):
        piece = slice(part * size, (part + 1) * size)
        loads[part].wait()
        result = result + jnp.dot(attention[:, piece], wo[piece, :], preferred_element_type=F32)
    partial[...] = result.astype(BF16)
    for s, t, page, base, wanted in places:

        @pl.when(wanted)
        def _():
            for n in range(2):
                put(n, s, t, page, base).wait()


def finish_rows_kernel(facts, new_rows, *refs):
    *parts, mixed, near_out, far_out, scr = refs
    slots = facts[OUT_NEAR], facts[OUT_FAR]
    width = parts[0].shape[1]
    terms = [part[...].astype(F32) for part in parts]
    level = 1
    while level < len(terms):
        terms = [terms[n] + terms[n ^ level] for n in range(len(terms))]
        level *= 2
    total = terms[0]
    slot_count, steps, _ = scr.shape
    for s in range(slot_count):
        live = (facts[LENGTHS + s] > 0) & (s != slots[0]) & (s != slots[1])
        own = total[s * steps : (s + 1) * steps]
        scr[s, :, :width] = own
        scr[s, :, width:] = new_rows[s * steps : (s + 1) * steps, :].astype(F32)
        mixed[s] = jnp.where(live, own, 0.0).astype(BF16)
    for slot, out in zip(slots, (near_out, far_out)):
        out[...] = scr[jnp.maximum(slot, 0)].astype(BF16)


def place_kernel(ways, facts, *refs):
    near_pages, *far_pages = refs[: 1 + ways]
    near_rows, *far_rows = refs[1 + ways : 2 + 2 * ways]
    mixed_in, _, _, mixed, key_out, value_out, stage, lines, in_sems, line_sems, out_sems, own_sem = refs[
        2 + 2 * ways :
    ]
    pages = stage.shape[1] // 2
    page_len, head_dim = stage.shape[2:]
    slot_count, steps, width = mixed.shape
    cases = ((facts[IN_NEAR], facts[NEAR_LEN]), (facts[IN_FAR], facts[FAR_LEN]))
    far_gap = facts[FAR_GAP]
    row = lax.broadcasted_iota(jnp.int32, (page_len, head_dim), 0)

    def load(n, source):
        return pltpu.make_async_copy(source, stage.at[n], in_sems.at[n])

    def load_line(n, source):
        return pltpu.make_async_copy(source, lines.at[n], line_sems.at[n, 0])

    def store_line(n):
        return pltpu.make_async_copy(
            lines.at[n, :, pl.ds(0, width)], mixed.at[cases[n][0]], line_sems.at[n, 1]
        )

    def store(n, p, which):
        pool = (key_out, value_out)[which]
        page = facts[LENGTHS + slot_count + cases[n][0] * pages + p]
        return pltpu.make_async_copy(stage.at[n, which * pages + p], pool.at[page], out_sems.at[n, which, p])

    def each(do):
        for n in range(2):

            @pl.when(cases[n][0] >= 0)
            def _():
                do(n)

    def start(n):
        if n == 0 or ways == 1:
            load_line(n, (near_rows, far_rows[0])[n]).start()
            load(n, (near_pages, far_pages[0])[n]).start()
            return
        for way in range(ways):

            @pl.when((far_gap == 1) == (way == 0))
            def _():
                load_line(n, far_rows[way]).start()
                load(n, far_pages[way]).start()

    def patch(n):
        _, length = cases[n]
        load_line(n, near_rows).wait()
        store_line(n).start()
        fresh = lines[n, :, width:].astype(F32)
        load(n, near_pages).wait()
        for p in range(pages):
            at = row + p * page_len
            for which in range(2):
                page = stage[n, which * pages + p].astype(F32)
                page = jnp.where(at < length, page, 0.0)
                for t in range(steps):
                    page = jnp.where(
                        at == length + t, fresh[t : t + 1, which * head_dim : (which + 1) * head_dim], page
                    )
                stage[n, which * pages + p] = page.astype(BF16)
                store(n, p, which).start()

    def finish(n):
        store_line(n).wait()
        for p in range(pages):
            for which in range(2):
                store(n, p, which).wait()

    own = pltpu.make_async_copy(mixed_in, mixed, own_sem)
    own.start()
    each(start)
    own.wait()
    each(patch)
    each(finish)


def run(
    near_hops,
    far_hops,
    near,
    far,
    facts,
    scalars,
    token_states,
    query_rows,
    key_weight,
    value_weight,
    out_weight,
    keys,
    values,
):
    groups = lax.axis_size("dec")
    tp = lax.axis_size("tp")
    slot_count, steps, model = token_states.shape
    _, page_len, head_dim = keys.shape
    rows = slot_count * steps
    width = out_weight.shape[1]
    heads = query_rows.shape[2] // head_dim
    pool_shape = jax.ShapeDtypeStruct(keys.shape, BF16)
    limit = pltpu.CompilerParams(vmem_limit_bytes=63 * 2**20)

    pages_in = [lax.ppermute(near, "dec", near_hops)] + [lax.ppermute(far, "dec", hops) for hops in far_hops]

    key_mid, value_mid, partial, new_rows = pl.pallas_call(
        attend_kernel,
        out_shape=(
            pool_shape,
            pool_shape,
            jax.ShapeDtypeStruct((rows, width), BF16),
            jax.ShapeDtypeStruct((rows, 2 * head_dim), BF16),
        ),
        in_specs=[SMEM] + [ANY] * 5 + [VMEM] * 2 + [ANY] * 3,
        out_specs=(HBM, HBM, VMEM, VMEM),
        scratch_shapes=[
            pltpu.VMEM(token_states.shape, BF16),
            pltpu.VMEM(query_rows.shape, BF16),
            pltpu.VMEM(key_weight.shape, BF16),
            pltpu.VMEM(value_weight.shape, BF16),
            pltpu.VMEM(out_weight.shape, BF16),
            pltpu.VMEM((heads * rows, head_dim), F32),
            pltpu.VMEM((heads * rows, head_dim), F32),
            pltpu.VMEM((2, slot_count, steps, 16, head_dim), BF16),
            pltpu.SemaphoreType.DMA((2 + 3 * PARTS,)),
            pltpu.SemaphoreType.DMA((2,)),
            pltpu.SemaphoreType.DMA((2, slot_count, steps)),
        ],
        compiler_params=pltpu.CompilerParams(vmem_limit_bytes=40 * 2**20),
        cost_estimate=pl.CostEstimate(flops=1_000_000, bytes_accessed=1_000_000, transcendentals=0),
        name="attend",
    )(
        facts,
        token_states,
        query_rows,
        key_weight,
        value_weight,
        out_weight,
        keys,
        values,
        *scalars,
    )

    others = [lax.ppermute(partial, "tp", [(i, i ^ n) for i in range(tp)]) for n in range(1, tp)]
    row_shape = jax.ShapeDtypeStruct((steps, width + 2 * head_dim), BF16)
    mixed, near_row, far_row = pl.pallas_call(
        finish_rows_kernel,
        out_shape=(jax.ShapeDtypeStruct((slot_count, steps, width), BF16), row_shape, row_shape),
        in_specs=[SMEM, VMEM] + [VMEM] * tp,
        out_specs=(VMEM, VMEM, VMEM),
        scratch_shapes=[pltpu.VMEM((slot_count, steps, width + 2 * head_dim), F32)],
        compiler_params=pltpu.CompilerParams(vmem_limit_bytes=8 * 2**20),
        name="rows",
    )(facts, new_rows, partial, *others)
    rows_in = [lax.ppermute(near_row, "dec", near_hops)] + [lax.ppermute(far_row, "dec", hops) for hops in far_hops]
    return pages_in, rows_in, mixed, key_mid, value_mid


def moved(migrations, cached_len, table, inputs):
    groups = lax.axis_size("dec")
    half = groups // 2
    keys, values = inputs[-2:]
    scalars = (migrations, cached_len, table)
    _, page_len, head_dim = keys.shape
    pages, slot_count = table.shape[1:]
    facts_shape = jax.ShapeDtypeStruct((LENGTHS + slot_count + slot_count * pages,), jnp.int32)
    moved_shape = jax.ShapeDtypeStruct((2 * pages, page_len, head_dim), BF16)
    near, far, facts = pl.pallas_call(
        functools.partial(pack_kernel, groups),
        out_shape=(moved_shape, moved_shape, facts_shape),
        in_specs=[SMEM, SMEM, SMEM, HBM, HBM],
        out_specs=(VMEM, VMEM, SMEM),
        scratch_shapes=[pltpu.SemaphoreType.DMA((2, 2, pages))],
        compiler_params=pltpu.CompilerParams(vmem_limit_bytes=40 * 2**20),
        cost_estimate=pl.CostEstimate(flops=0, bytes_accessed=1_000_000, transcendentals=0),
        name="pack",
    )(migrations, cached_len, table, keys, values)
    if half != 2:
        far_hops = (shifted(groups, 1), shifted(groups, 1 + half))
        return facts, run(shifted(groups, half), far_hops, near, far, facts, scalars, *inputs)
    branches = []
    for case in range(2**half):
        senders = [pair + half * (case >> pair & 1) for pair in range(half)]
        receivers = [(sender + half) % groups for sender in senders]
        near_hops = [(senders[pair], receivers[pair]) for pair in range(half)]
        far_hops = [(senders[pair], receivers[(pair + 1) % half]) for pair in range(half)]
        near_hops += [(b, a) for a, b in near_hops]
        far_hops += [(b, a) for a, b in far_hops]
        branches.append(functools.partial(run, near_hops, (far_hops,)))
    return facts, lax.switch(facts[NUMBER], branches, near, far, facts, scalars, *inputs)


def local(
    token_states,
    query_rows,
    key_weight,
    value_weight,
    out_weight,
    key_pool,
    value_pool,
    cached_len,
    page_table,
    migrations,
):
    groups = lax.axis_size("dec")
    pool_pages, _, page_len, head_dim = key_pool.shape
    slot_count, steps, _ = token_states.shape
    keys = key_pool.reshape(pool_pages, page_len, head_dim)
    values = value_pool.reshape(pool_pages, page_len, head_dim)
    table = jnp.swapaxes(page_table, 1, 2)
    pages = table.shape[1]
    inputs = (
        token_states,
        query_rows,
        key_weight,
        value_weight,
        out_weight,
        keys,
        values,
    )
    facts, (pages_in, rows_in, mixed_mid, key_mid, value_mid) = moved(
        migrations, cached_len, table, inputs
    )
    ways = len(pages_in) - 1
    pool_shape = jax.ShapeDtypeStruct(keys.shape, BF16)
    mixed_shape = jax.ShapeDtypeStruct((slot_count, steps, out_weight.shape[1]), BF16)
    mixed, key_out, value_out = pl.pallas_call(
        functools.partial(place_kernel, ways),
        out_shape=(mixed_shape, pool_shape, pool_shape),
        in_specs=[SMEM] + [ANY] * (2 + 2 * ways) + [VMEM] + [HBM] * 2,
        out_specs=(HBM, HBM, HBM),
        scratch_shapes=[
            pltpu.VMEM((2, 2 * pages, page_len, head_dim), BF16),
            pltpu.VMEM((2,) + rows_in[0].shape, BF16),
            pltpu.SemaphoreType.DMA((2,)),
            pltpu.SemaphoreType.DMA((2, 2)),
            pltpu.SemaphoreType.DMA((2, 2, pages)),
            pltpu.SemaphoreType.DMA,
        ],
        input_output_aliases={4 + 2 * ways: 1, 5 + 2 * ways: 2},
        compiler_params=pltpu.CompilerParams(vmem_limit_bytes=63 * 2**20),
        name="place",
    )(facts, *pages_in, *rows_in, mixed_mid, key_mid, value_mid)
    return mixed, key_out.reshape(key_pool.shape), value_out.reshape(value_pool.shape)


def solution(mesh):
    placed = (
        P(("rep", "dec"), None, None),
        P(("rep", "dec"), None, "tp"),
        P(None, "tp"),
        P(None, "tp"),
        P("tp", None),
        P(("rep", "dec"), "tp", None, None),
        P(("rep", "dec"), "tp", None, None),
        P("rep", None),
        P(("rep", "dec"), None, None),
        P("rep", None),
    )
    return jax.shard_map(
        local,
        mesh=mesh,
        in_specs=placed,
        out_specs=(
            P(("rep", "dec"), None, None),
            P(("rep", "dec"), "tp", None, None),
            P(("rep", "dec"), "tp", None, None),
        ),
        check_vma=False,
    )
```

```python
import functools

import jax
import jax.numpy as jnp
from jax import lax
from jax.experimental import pallas as pl
from jax.experimental.pallas import tpu as pltpu
from jax.sharding import PartitionSpec as P

F32 = jnp.float32
BF16 = jnp.bfloat16
PARTS = 4
SMEM = pl.BlockSpec(memory_space=pltpu.SMEM)
HBM = pl.BlockSpec(memory_space=pltpu.HBM)
ANY = pl.BlockSpec(memory_space=pl.ANY)
VMEM = pl.BlockSpec(memory_space=pltpu.VMEM)


def shifted(count, by):
    return [(i, (i + by) % count) for i in range(count)]


def outgoing(mig, me, groups):
    half = groups // 2
    near = far = jnp.int32(-1)
    for m in range(mig.shape[0]):
        mine = mig[m, 0] == me
        gap = lax.rem(mig[m, 2] - me + groups, groups)
        near = jnp.where(mine & (gap == half), mig[m, 1], near)
        far = jnp.where(mine & (gap != half), mig[m, 1], far)
    return near, far


def incoming(mig, lens, me, groups):
    half = groups // 2
    near = far = jnp.int32(-1)
    near_len = far_len = far_gap = jnp.int32(0)
    for m in range(mig.shape[0]):
        mine = mig[m, 2] == me
        gap = lax.rem(me - mig[m, 0] + groups, groups)
        length = lens[mig[m, 0], mig[m, 1]]
        is_near = mine & (gap == half)
        is_far = mine & (gap != half)
        near = jnp.where(is_near, mig[m, 3], near)
        near_len = jnp.where(is_near, length, near_len)
        far = jnp.where(is_far, mig[m, 3], far)
        far_len = jnp.where(is_far, length, far_len)
        far_gap = jnp.where(is_far, gap, far_gap)
    return (near, near_len), (far, far_len), far_gap


NUMBER, OUT_NEAR, OUT_FAR, IN_NEAR, NEAR_LEN, IN_FAR, FAR_LEN, FAR_GAP, LENGTHS = range(9)


def pack_kernel(groups, mig, lens, table, key_pool, value_pool, near_out, far_out, facts, sems):
    me = lax.axis_index("dec")
    _, pages, slot_count = table.shape
    outs = (near_out, far_out)
    slots = outgoing(mig, me, groups)

    def load(n, which, p):
        page = table[0, p, slots[n]]
        pool = (key_pool, value_pool)[which]
        return pltpu.make_async_copy(pool.at[page], outs[n].at[which * pages + p], sems.at[n, which, p])

    def each(do):
        for n in range(2):

            @pl.when(slots[n] >= 0)
            def _():
                for p in range(pages):
                    for which in range(2):
                        do(load(n, which, p))

    each(lambda copy: copy.start())
    half = groups // 2
    number = jnp.int32(0)
    if half == 2:
        for m in range(mig.shape[0]):
            number = number | jnp.where(mig[m, 0] >= half, mig[m, 0] - half + 1, 0)
    facts[NUMBER] = number
    facts[OUT_NEAR], facts[OUT_FAR] = slots
    near, far, far_gap = incoming(mig, lens, me, groups)
    facts[IN_NEAR], facts[NEAR_LEN] = near
    facts[IN_FAR], facts[FAR_LEN] = far
    facts[FAR_GAP] = far_gap
    for s in range(slot_count):
        facts[LENGTHS + s] = lens[me, s]
        for p in range(pages):
            facts[LENGTHS + slot_count + s * pages + p] = table[0, p, s]
    each(lambda copy: copy.wait())


def attend_kernel(
    facts,
    states_hbm,
    query_hbm,
    key_weight,
    value_weight,
    out_weight,
    kp,
    vp,
    mig,
    lens,
    table,
    key_out,
    value_out,
    partial,
    new_rows,
    states,
    query,
    wk,
    wv,
    wo,
    q_scr,
    a_scr,
    tiles,
    load_sems,
    store_sems,
    tile_sems,
):
    del mig, lens, table
    slot_count, steps, _ = states.shape
    rows = slot_count * steps
    page_len, head_dim = kp.shape[1:]
    pages = kp.shape[0] // slot_count
    heads = query.shape[2] // head_dim
    span = pages * page_len
    pools = ((kp, key_out, 0), (vp, value_out, head_dim))
    number = 0

    def split(source, target, parts):
        nonlocal number
        size = source.shape[0] // parts
        copies = []
        for part in range(parts):
            piece = pl.ds(part * size, size)
            copies.append(pltpu.make_async_copy(source.at[piece], target.at[piece], load_sems.at[number]))
            number += 1
        return copies

    (load_query,) = split(query_hbm, query, 1)
    (load_states,) = split(states_hbm, states, 1)
    load_wk = split(key_weight, wk, PARTS)
    load_wv = split(value_weight, wv, PARTS)
    loads = split(out_weight, wo, PARTS)
    stores = [pltpu.make_async_copy(pool, out, store_sems.at[n]) for n, (pool, out, _) in enumerate(pools)]
    for copy in [load_query, load_states] + load_wk + load_wv + loads + stores:
        copy.start()
    near, far = facts[OUT_NEAR], facts[OUT_FAR]
    lengths = [facts[LENGTHS + s] for s in range(slot_count)]
    first_page = [LENGTHS + slot_count + s * pages for s in range(slot_count)]
    numbers = [[facts[first_page[s] + p] for p in range(pages)] for s in range(slot_count)]

    load_query.wait()
    for s in range(slot_count):
        qf = query[s].astype(F32)
        for h in range(heads):
            q_scr[pl.ds(h * rows + s * steps, steps), :] = qf[:, h * head_dim : (h + 1) * head_dim]

    count = steps * heads
    nt = (((1,), (1,)), ((), ()))
    queries = jnp.concatenate(
        [q_scr[pl.ds(r, heads, stride=rows), :] for r in range(rows)], 0
    ).astype(BF16)
    position = lax.broadcasted_iota(jnp.int32, (count, span), 1)
    scaling = head_dim**-0.5
    scores = []
    for s in range(slot_count):
        keys = jnp.concatenate([kp[n] for n in numbers[s]], 0)
        cached = lax.dot_general(
            queries[s * count : (s + 1) * count], keys, nt, preferred_element_type=F32
        )
        scores.append(jnp.where(position < lengths[s], cached * scaling, -jnp.inf))
    cached = jnp.concatenate(scores, 0)

    load_states.wait()
    x = jnp.concatenate([states[s].astype(F32) for s in range(slot_count)], 0).astype(BF16)
    fresh_k = jnp.zeros((rows, head_dim), F32)
    fresh_v = jnp.zeros((rows, head_dim), F32)
    size = wk.shape[0] // PARTS
    for part in range(PARTS):
        piece = slice(part * size, (part + 1) * size)
        load_wk[part].wait()
        fresh_k = fresh_k + jnp.dot(x[:, piece], wk[piece, :], preferred_element_type=F32)
        load_wv[part].wait()
        fresh_v = fresh_v + jnp.dot(x[:, piece], wv[piece, :], preferred_element_type=F32)
    fresh_k = fresh_k.astype(BF16)
    fresh_v = fresh_v.astype(BF16)
    new_rows[:, :head_dim] = fresh_k
    new_rows[:, head_dim:] = fresh_v

    fresh = lax.dot_general(queries, fresh_k, nt, preferred_element_type=F32) * scaling
    fresh_row = lax.broadcasted_iota(jnp.int32, fresh.shape, 0)
    fresh_col = lax.broadcasted_iota(jnp.int32, fresh.shape, 1)
    first = fresh_row // count * steps
    allowed = (fresh_col >= first) & (fresh_col <= fresh_row // heads)
    fresh = jnp.where(allowed, fresh, -jnp.inf)
    peak = jnp.maximum(jnp.max(cached, 1, keepdims=True), jnp.max(fresh, 1, keepdims=True))
    cached = jnp.exp(cached - peak)
    fresh = jnp.exp(fresh - peak)
    share = 1.0 / (jnp.sum(cached, 1, keepdims=True) + jnp.sum(fresh, 1, keepdims=True))
    cached_w = (cached * share).astype(BF16)
    fresh_w = (fresh * share).astype(BF16)
    fresh_out = jnp.dot(fresh_w, fresh_v, preferred_element_type=F32)
    for s in range(slot_count):
        values = jnp.concatenate([vp[n] for n in numbers[s]], 0)
        piece = slice(s * count, (s + 1) * count)
        out = jnp.dot(cached_w[piece], values, preferred_element_type=F32) + fresh_out[piece]
        for t in range(steps):
            a_scr[pl.ds(s * steps + t, heads, stride=rows), :] = out[t * heads : (t + 1) * heads]

    tile = tiles.shape[3]
    row = lax.broadcasted_iota(jnp.int32, (tile, head_dim), 0)
    fresh_f = (fresh_k.astype(F32), fresh_v.astype(F32))
    places = []
    for s in range(slot_count):
        live = (lengths[s] > 0) & (s != near) & (s != far)
        for t in range(steps):
            at = lengths[s] + t
            page = facts[first_page[s] + at // page_len]
            low = at // tile * tile
            base = pl.multiple_of(lax.rem(low, page_len), tile)
            places.append((s, t, page, base, live & ((t == 0) | (lax.rem(at, tile) == 0))))
            for n, (pool, _, _) in enumerate(pools):
                merged = pool[page, pl.ds(base, tile), :].astype(F32)
                for u in range(steps):
                    line = fresh_f[n][s * steps + u : s * steps + u + 1]
                    merged = jnp.where(row + low == lengths[s] + u, line, merged)
                tiles[n, s, t] = merged.astype(BF16)
    for store in stores:
        store.wait()

    def put(n, s, t, page, base):
        return pltpu.make_async_copy(
            tiles.at[n, s, t], pools[n][1].at[page, pl.ds(base, tile), :], tile_sems.at[n, s, t]
        )

    for s, t, page, base, wanted in places:

        @pl.when(wanted)
        def _():
            for n in range(2):
                put(n, s, t, page, base).start()

    attention = jnp.concatenate([a_scr[h * rows : (h + 1) * rows, :].astype(BF16) for h in range(heads)], 1)
    result = jnp.zeros((rows, wo.shape[1]), F32)
    size = wo.shape[0] // PARTS
    for part in range(PARTS):
        piece = slice(part * size, (part + 1) * size)
        loads[part].wait()
        result = result + jnp.dot(attention[:, piece], wo[piece, :], preferred_element_type=F32)
    partial[...] = result.astype(BF16)
    for s, t, page, base, wanted in places:

        @pl.when(wanted)
        def _():
            for n in range(2):
                put(n, s, t, page, base).wait()


def finish_rows_kernel(facts, new_rows, *refs):
    *parts, mixed, near_out, far_out, scr = refs
    slots = facts[OUT_NEAR], facts[OUT_FAR]
    width = parts[0].shape[1]
    terms = [part[...].astype(F32) for part in parts]
    level = 1
    while level < len(terms):
        terms = [terms[n] + terms[n ^ level] for n in range(len(terms))]
        level *= 2
    total = terms[0]
    slot_count, steps, _ = scr.shape
    for s in range(slot_count):
        live = (facts[LENGTHS + s] > 0) & (s != slots[0]) & (s != slots[1])
        own = total[s * steps : (s + 1) * steps]
        scr[s, :, :width] = own
        scr[s, :, width:] = new_rows[s * steps : (s + 1) * steps, :].astype(F32)
        mixed[s] = jnp.where(live, own, 0.0).astype(BF16)
    for slot, out in zip(slots, (near_out, far_out)):
        out[...] = scr[jnp.maximum(slot, 0)].astype(BF16)


def place_kernel(ways, facts, *refs):
    near_pages, *far_pages = refs[: 1 + ways]
    near_rows, *far_rows = refs[1 + ways : 2 + 2 * ways]
    mixed_in, _, _, mixed, key_out, value_out, stage, out_sems, line_sems, own_sem = refs[2 + 2 * ways :]
    pages = stage.shape[1] // 2
    page_len, head_dim = stage.shape[2:]
    slot_count, steps, width = mixed.shape
    row = lax.broadcasted_iota(jnp.int32, (page_len, head_dim), 0)
    far_gap = facts[FAR_GAP]
    cases = [(0, facts[IN_NEAR], facts[NEAR_LEN], facts[IN_NEAR] >= 0, near_pages, near_rows)]
    for way in range(ways):
        came = facts[IN_FAR] >= 0
        if ways == 2:
            came = came & ((far_gap == 1) == (way == 0))
        cases.append((1, facts[IN_FAR], facts[FAR_LEN], came, far_pages[way], far_rows[way]))

    def store(n, slot, p, which, source):
        pool = (key_out, value_out)[which]
        page = facts[LENGTHS + slot_count + slot * pages + p]
        return pltpu.make_async_copy(source, pool.at[page], out_sems.at[n, which, p])

    def store_line(n, slot, rows):
        return pltpu.make_async_copy(rows.at[:, pl.ds(0, width)], mixed.at[slot], line_sems.at[n])

    own = pltpu.make_async_copy(mixed_in, mixed, own_sem)
    own.start()
    for n, slot, length, came, arrived, rows in cases:

        @pl.when(came)
        def _():
            fresh = rows[:, width:].astype(F32)
            for p in range(pages):
                whole = length >= (p + 1) * page_len

                @pl.when(whole)
                def _():
                    for which in range(2):
                        store(n, slot, p, which, arrived.at[which * pages + p]).start()

                @pl.when(jnp.logical_not(whole))
                def _():
                    at = row + p * page_len
                    for which in range(2):
                        page = jnp.where(at < length, arrived[which * pages + p].astype(F32), 0.0)
                        for t in range(steps):
                            line = fresh[t : t + 1, which * head_dim : (which + 1) * head_dim]
                            page = jnp.where(at == length + t, line, page)
                        stage[n, which * pages + p] = page.astype(BF16)
                        store(n, slot, p, which, stage.at[n, which * pages + p]).start()

    own.wait()
    for n, slot, _, came, _, rows in cases:

        @pl.when(came)
        def _():
            store_line(n, slot, rows).start()

    for n, slot, _, came, arrived, rows in cases:

        @pl.when(came)
        def _():
            for p in range(pages):
                for which in range(2):
                    store(n, slot, p, which, arrived.at[which * pages + p]).wait()
            store_line(n, slot, rows).wait()


def run(
    near_hops,
    far_hops,
    near,
    far,
    facts,
    scalars,
    token_states,
    query_rows,
    key_weight,
    value_weight,
    out_weight,
    keys,
    values,
):
    groups = lax.axis_size("dec")
    tp = lax.axis_size("tp")
    slot_count, steps, model = token_states.shape
    _, page_len, head_dim = keys.shape
    rows = slot_count * steps
    width = out_weight.shape[1]
    heads = query_rows.shape[2] // head_dim
    pool_shape = jax.ShapeDtypeStruct(keys.shape, BF16)
    limit = pltpu.CompilerParams(vmem_limit_bytes=63 * 2**20)

    pages_in = [lax.ppermute(near, "dec", near_hops)] + [lax.ppermute(far, "dec", hops) for hops in far_hops]

    key_mid, value_mid, partial, new_rows = pl.pallas_call(
        attend_kernel,
        out_shape=(
            pool_shape,
            pool_shape,
            jax.ShapeDtypeStruct((rows, width), BF16),
            jax.ShapeDtypeStruct((rows, 2 * head_dim), BF16),
        ),
        in_specs=[SMEM] + [ANY] * 5 + [VMEM] * 2 + [ANY] * 3,
        out_specs=(HBM, HBM, VMEM, VMEM),
        scratch_shapes=[
            pltpu.VMEM(token_states.shape, BF16),
            pltpu.VMEM(query_rows.shape, BF16),
            pltpu.VMEM(key_weight.shape, BF16),
            pltpu.VMEM(value_weight.shape, BF16),
            pltpu.VMEM(out_weight.shape, BF16),
            pltpu.VMEM((heads * rows, head_dim), F32),
            pltpu.VMEM((heads * rows, head_dim), F32),
            pltpu.VMEM((2, slot_count, steps, 16, head_dim), BF16),
            pltpu.SemaphoreType.DMA((2 + 3 * PARTS,)),
            pltpu.SemaphoreType.DMA((2,)),
            pltpu.SemaphoreType.DMA((2, slot_count, steps)),
        ],
        compiler_params=pltpu.CompilerParams(vmem_limit_bytes=40 * 2**20),
        cost_estimate=pl.CostEstimate(flops=1_000_000, bytes_accessed=1_000_000, transcendentals=0),
        name="attend",
    )(
        facts,
        token_states,
        query_rows,
        key_weight,
        value_weight,
        out_weight,
        keys,
        values,
        *scalars,
    )

    others = [lax.ppermute(partial, "tp", [(i, i ^ n) for i in range(tp)]) for n in range(1, tp)]
    row_shape = jax.ShapeDtypeStruct((steps, width + 2 * head_dim), BF16)
    mixed_mid, near_row, far_row = pl.pallas_call(
        finish_rows_kernel,
        out_shape=(jax.ShapeDtypeStruct((slot_count, steps, width), BF16), row_shape, row_shape),
        in_specs=[SMEM, VMEM] + [VMEM] * tp,
        out_specs=(VMEM, VMEM, VMEM),
        scratch_shapes=[pltpu.VMEM((slot_count, steps, width + 2 * head_dim), F32)],
        compiler_params=pltpu.CompilerParams(vmem_limit_bytes=8 * 2**20),
        name="rows",
    )(facts, new_rows, partial, *others)
    rows_in = [lax.ppermute(near_row, "dec", near_hops)] + [lax.ppermute(far_row, "dec", hops) for hops in far_hops]
    pages = keys.shape[0] // slot_count
    ways = len(pages_in) - 1
    mixed_shape = jax.ShapeDtypeStruct((slot_count, steps, width), BF16)
    mixed, key_out, value_out = pl.pallas_call(
        functools.partial(place_kernel, ways),
        out_shape=(mixed_shape, pool_shape, pool_shape),
        in_specs=[SMEM] + [VMEM] * (2 + 2 * ways) + [VMEM] + [HBM] * 2,
        out_specs=(HBM, HBM, HBM),
        scratch_shapes=[
            pltpu.VMEM((2, 2 * pages, page_len, head_dim), BF16),
            pltpu.SemaphoreType.DMA((2, 2, pages)),
            pltpu.SemaphoreType.DMA((2,)),
            pltpu.SemaphoreType.DMA,
        ],
        input_output_aliases={4 + 2 * ways: 1, 5 + 2 * ways: 2},
        compiler_params=pltpu.CompilerParams(vmem_limit_bytes=41943040),
        name="place",
    )(facts, *pages_in, *rows_in, mixed_mid, key_mid, value_mid)
    return mixed, key_out, value_out


def moved(migrations, cached_len, table, inputs):
    groups = lax.axis_size("dec")
    half = groups // 2
    keys, values = inputs[-2:]
    scalars = (migrations, cached_len, table)
    _, page_len, head_dim = keys.shape
    pages, slot_count = table.shape[1:]
    facts_shape = jax.ShapeDtypeStruct((LENGTHS + slot_count + slot_count * pages,), jnp.int32)
    moved_shape = jax.ShapeDtypeStruct((2 * pages, page_len, head_dim), BF16)
    near, far, facts = pl.pallas_call(
        functools.partial(pack_kernel, groups),
        out_shape=(moved_shape, moved_shape, facts_shape),
        in_specs=[SMEM, SMEM, SMEM, HBM, HBM],
        out_specs=(VMEM, VMEM, SMEM),
        scratch_shapes=[pltpu.SemaphoreType.DMA((2, 2, pages))],
        compiler_params=pltpu.CompilerParams(vmem_limit_bytes=40 * 2**20),
        cost_estimate=pl.CostEstimate(flops=0, bytes_accessed=1_000_000, transcendentals=0),
        name="pack",
    )(migrations, cached_len, table, keys, values)
    if half != 2:
        far_hops = (shifted(groups, 1), shifted(groups, 1 + half))
        return run(shifted(groups, half), far_hops, near, far, facts, scalars, *inputs)
    branches = []
    for case in range(2**half):
        senders = [pair + half * (case >> pair & 1) for pair in range(half)]
        receivers = [(sender + half) % groups for sender in senders]
        near_hops = [(senders[pair], receivers[pair]) for pair in range(half)]
        far_hops = [(senders[pair], receivers[(pair + 1) % half]) for pair in range(half)]
        near_hops += [(b, a) for a, b in near_hops]
        far_hops += [(b, a) for a, b in far_hops]
        branches.append(functools.partial(run, near_hops, (far_hops,)))
    outs = lax.switch(facts[NUMBER], branches, near, far, facts, scalars, *inputs)
    return pl.pallas_call(
        lambda *refs: None,
        out_shape=tuple(jax.ShapeDtypeStruct(out.shape, out.dtype) for out in outs),
        in_specs=[HBM] * 3,
        out_specs=(HBM,) * 3,
        input_output_aliases={0: 0, 1: 1, 2: 2},
        compiler_params=pltpu.CompilerParams(vmem_limit_bytes=67004006),
        name="keep",
    )(*outs)


def local(
    token_states,
    query_rows,
    key_weight,
    value_weight,
    out_weight,
    key_pool,
    value_pool,
    cached_len,
    page_table,
    migrations,
):
    groups = lax.axis_size("dec")
    pool_pages, _, page_len, head_dim = key_pool.shape
    slot_count, steps, _ = token_states.shape
    keys = key_pool.reshape(pool_pages, page_len, head_dim)
    values = value_pool.reshape(pool_pages, page_len, head_dim)
    table = jnp.swapaxes(page_table, 1, 2)
    pages = table.shape[1]
    inputs = (
        token_states,
        query_rows,
        key_weight,
        value_weight,
        out_weight,
        keys,
        values,
    )
    mixed, key_out, value_out = moved(migrations, cached_len, table, inputs)
    return mixed, key_out.reshape(key_pool.shape), value_out.reshape(value_pool.shape)


def solution(mesh):
    placed = (
        P(("rep", "dec"), None, None),
        P(("rep", "dec"), None, "tp"),
        P(None, "tp"),
        P(None, "tp"),
        P("tp", None),
        P(("rep", "dec"), "tp", None, None),
        P(("rep", "dec"), "tp", None, None),
        P("rep", None),
        P(("rep", "dec"), None, None),
        P("rep", None),
    )
    return jax.shard_map(
        local,
        mesh=mesh,
        in_specs=placed,
        out_specs=(
            P(("rep", "dec"), None, None),
            P(("rep", "dec"), "tp", None, None),
            P(("rep", "dec"), "tp", None, None),
        ),
        check_vma=False,
    )
```

```python
import functools

import jax
import jax.numpy as jnp
from jax import lax
from jax.experimental import pallas as pl
from jax.experimental.pallas import tpu as pltpu
from jax.sharding import PartitionSpec as P

F32 = jnp.float32
BF16 = jnp.bfloat16
PARTS = 4
SMEM = pl.BlockSpec(memory_space=pltpu.SMEM)
HBM = pl.BlockSpec(memory_space=pltpu.HBM)
ANY = pl.BlockSpec(memory_space=pl.ANY)
VMEM = pl.BlockSpec(memory_space=pltpu.VMEM)


def shifted(count, by):
    return [(i, (i + by) % count) for i in range(count)]


def outgoing(mig, me, groups):
    half = groups // 2
    near = far = jnp.int32(-1)
    for m in range(mig.shape[0]):
        mine = mig[m, 0] == me
        gap = lax.rem(mig[m, 2] - me + groups, groups)
        near = jnp.where(mine & (gap == half), mig[m, 1], near)
        far = jnp.where(mine & (gap != half), mig[m, 1], far)
    return near, far


def incoming(mig, lens, me, groups):
    half = groups // 2
    near = far = jnp.int32(-1)
    near_len = far_len = far_gap = jnp.int32(0)
    for m in range(mig.shape[0]):
        mine = mig[m, 2] == me
        gap = lax.rem(me - mig[m, 0] + groups, groups)
        length = lens[mig[m, 0], mig[m, 1]]
        is_near = mine & (gap == half)
        is_far = mine & (gap != half)
        near = jnp.where(is_near, mig[m, 3], near)
        near_len = jnp.where(is_near, length, near_len)
        far = jnp.where(is_far, mig[m, 3], far)
        far_len = jnp.where(is_far, length, far_len)
        far_gap = jnp.where(is_far, gap, far_gap)
    return (near, near_len), (far, far_len), far_gap


NUMBER, OUT_NEAR, OUT_FAR, IN_NEAR, NEAR_LEN, IN_FAR, FAR_LEN, FAR_GAP, LENGTHS = range(9)


def pack_kernel(groups, mig, lens, table, key_pool, value_pool, near_out, far_out, facts, sems):
    me = lax.axis_index("dec")
    _, pages, slot_count = table.shape
    outs = (near_out, far_out)
    slots = outgoing(mig, me, groups)

    def load(n, which, p):
        page = table[0, p, slots[n]]
        pool = (key_pool, value_pool)[which]
        return pltpu.make_async_copy(pool.at[page], outs[n].at[which * pages + p], sems.at[n, which, p])

    def each(do):
        for n in range(2):

            @pl.when(slots[n] >= 0)
            def _():
                for p in range(pages):
                    for which in range(2):
                        do(load(n, which, p))

    each(lambda copy: copy.start())
    half = groups // 2
    number = jnp.int32(0)
    if half == 2:
        for m in range(mig.shape[0]):
            number = number | jnp.where(mig[m, 0] >= half, mig[m, 0] - half + 1, 0)
    facts[NUMBER] = number
    facts[OUT_NEAR], facts[OUT_FAR] = slots
    near, far, far_gap = incoming(mig, lens, me, groups)
    facts[IN_NEAR], facts[NEAR_LEN] = near
    facts[IN_FAR], facts[FAR_LEN] = far
    facts[FAR_GAP] = far_gap
    for s in range(slot_count):
        facts[LENGTHS + s] = lens[me, s]
        for p in range(pages):
            facts[LENGTHS + slot_count + s * pages + p] = table[0, p, s]
    each(lambda copy: copy.wait())


def attend_kernel(
    facts,
    states_hbm,
    query_hbm,
    key_weight,
    value_weight,
    out_weight,
    kp,
    vp,
    mig,
    lens,
    table,
    key_out,
    value_out,
    partial,
    new_rows,
    states,
    query,
    wk,
    wv,
    wo,
    q_scr,
    a_scr,
    tiles,
    load_sems,
    store_sems,
    tile_sems,
):
    del mig, lens, table
    slot_count, steps, _ = states.shape
    rows = slot_count * steps
    page_len, head_dim = kp.shape[1:]
    pages = kp.shape[0] // slot_count
    heads = query.shape[2] // head_dim
    span = pages * page_len
    pools = ((kp, key_out, 0), (vp, value_out, head_dim))
    number = 0

    def split(source, target, parts):
        nonlocal number
        size = source.shape[0] // parts
        copies = []
        for part in range(parts):
            piece = pl.ds(part * size, size)
            copies.append(pltpu.make_async_copy(source.at[piece], target.at[piece], load_sems.at[number]))
            number += 1
        return copies

    (load_query,) = split(query_hbm, query, 1)
    (load_states,) = split(states_hbm, states, 1)
    load_wk = split(key_weight, wk, PARTS)
    load_wv = split(value_weight, wv, PARTS)
    loads = split(out_weight, wo, PARTS)
    stores = [pltpu.make_async_copy(pool, out, store_sems.at[n]) for n, (pool, out, _) in enumerate(pools)]
    for copy in [load_query, load_states] + load_wk + load_wv + loads + stores:
        copy.start()
    near, far = facts[OUT_NEAR], facts[OUT_FAR]
    lengths = [facts[LENGTHS + s] for s in range(slot_count)]
    first_page = [LENGTHS + slot_count + s * pages for s in range(slot_count)]
    numbers = [[facts[first_page[s] + p] for p in range(pages)] for s in range(slot_count)]

    load_query.wait()
    for s in range(slot_count):
        qf = query[s].astype(F32)
        for h in range(heads):
            q_scr[pl.ds(h * rows + s * steps, steps), :] = qf[:, h * head_dim : (h + 1) * head_dim]

    count = steps * heads
    nt = (((1,), (1,)), ((), ()))
    queries = jnp.concatenate(
        [q_scr[pl.ds(r, heads, stride=rows), :] for r in range(rows)], 0
    ).astype(BF16)
    position = lax.broadcasted_iota(jnp.int32, (count, span), 1)
    scaling = head_dim**-0.5
    scores = []
    for s in range(slot_count):
        keys = jnp.concatenate([kp[n] for n in numbers[s]], 0)
        cached = lax.dot_general(
            queries[s * count : (s + 1) * count], keys, nt, preferred_element_type=F32
        )
        scores.append(jnp.where(position < lengths[s], cached * scaling, -jnp.inf))
    cached = jnp.concatenate(scores, 0)

    load_states.wait()
    x = jnp.concatenate([states[s].astype(F32) for s in range(slot_count)], 0).astype(BF16)
    fresh_k = jnp.zeros((rows, head_dim), F32)
    fresh_v = jnp.zeros((rows, head_dim), F32)
    size = wk.shape[0] // PARTS
    for part in range(PARTS):
        piece = slice(part * size, (part + 1) * size)
        load_wk[part].wait()
        fresh_k = fresh_k + jnp.dot(x[:, piece], wk[piece, :], preferred_element_type=F32)
        load_wv[part].wait()
        fresh_v = fresh_v + jnp.dot(x[:, piece], wv[piece, :], preferred_element_type=F32)
    fresh_k = fresh_k.astype(BF16)
    fresh_v = fresh_v.astype(BF16)
    new_rows[:, :head_dim] = fresh_k
    new_rows[:, head_dim:] = fresh_v

    fresh = lax.dot_general(queries, fresh_k, nt, preferred_element_type=F32) * scaling
    fresh_row = lax.broadcasted_iota(jnp.int32, fresh.shape, 0)
    fresh_col = lax.broadcasted_iota(jnp.int32, fresh.shape, 1)
    first = fresh_row // count * steps
    allowed = (fresh_col >= first) & (fresh_col <= fresh_row // heads)
    fresh = jnp.where(allowed, fresh, -jnp.inf)
    peak = jnp.maximum(jnp.max(cached, 1, keepdims=True), jnp.max(fresh, 1, keepdims=True))
    cached = jnp.exp(cached - peak)
    fresh = jnp.exp(fresh - peak)
    share = 1.0 / (jnp.sum(cached, 1, keepdims=True) + jnp.sum(fresh, 1, keepdims=True))
    cached_w = (cached * share).astype(BF16)
    fresh_w = (fresh * share).astype(BF16)
    fresh_out = jnp.dot(fresh_w, fresh_v, preferred_element_type=F32)
    for s in range(slot_count):
        values = jnp.concatenate([vp[n] for n in numbers[s]], 0)
        piece = slice(s * count, (s + 1) * count)
        out = jnp.dot(cached_w[piece], values, preferred_element_type=F32) + fresh_out[piece]
        for t in range(steps):
            a_scr[pl.ds(s * steps + t, heads, stride=rows), :] = out[t * heads : (t + 1) * heads]

    tile = tiles.shape[3]
    row = lax.broadcasted_iota(jnp.int32, (tile, head_dim), 0)
    fresh_f = (fresh_k.astype(F32), fresh_v.astype(F32))
    places = []
    for s in range(slot_count):
        live = (lengths[s] > 0) & (s != near) & (s != far)
        for t in range(steps):
            at = lengths[s] + t
            page = facts[first_page[s] + at // page_len]
            low = at // tile * tile
            base = pl.multiple_of(lax.rem(low, page_len), tile)
            places.append((s, t, page, base, live & ((t == 0) | (lax.rem(at, tile) == 0))))
            for n, (pool, _, _) in enumerate(pools):
                merged = pool[page, pl.ds(base, tile), :].astype(F32)
                for u in range(steps):
                    line = fresh_f[n][s * steps + u : s * steps + u + 1]
                    merged = jnp.where(row + low == lengths[s] + u, line, merged)
                tiles[n, s, t] = merged.astype(BF16)
    for store in stores:
        store.wait()

    def put(n, s, t, page, base):
        return pltpu.make_async_copy(
            tiles.at[n, s, t], pools[n][1].at[page, pl.ds(base, tile), :], tile_sems.at[n, s, t]
        )

    for s, t, page, base, wanted in places:

        @pl.when(wanted)
        def _():
            for n in range(2):
                put(n, s, t, page, base).start()

    attention = jnp.concatenate([a_scr[h * rows : (h + 1) * rows, :].astype(BF16) for h in range(heads)], 1)
    result = jnp.zeros((rows, wo.shape[1]), F32)
    size = wo.shape[0] // PARTS
    for part in range(PARTS):
        piece = slice(part * size, (part + 1) * size)
        loads[part].wait()
        result = result + jnp.dot(attention[:, piece], wo[piece, :], preferred_element_type=F32)
    partial[...] = result.astype(BF16)
    for s, t, page, base, wanted in places:

        @pl.when(wanted)
        def _():
            for n in range(2):
                put(n, s, t, page, base).wait()


def finish_rows_kernel(facts, new_rows, *refs):
    *parts, mixed, near_out, far_out, scr = refs
    slots = facts[OUT_NEAR], facts[OUT_FAR]
    width = parts[0].shape[1]
    terms = [part[...].astype(F32) for part in parts]
    level = 1
    while level < len(terms):
        terms = [terms[n] + terms[n ^ level] for n in range(len(terms))]
        level *= 2
    total = terms[0]
    slot_count, steps, _ = scr.shape
    for s in range(slot_count):
        live = (facts[LENGTHS + s] > 0) & (s != slots[0]) & (s != slots[1])
        own = total[s * steps : (s + 1) * steps]
        scr[s, :, :width] = own
        scr[s, :, width:] = new_rows[s * steps : (s + 1) * steps, :].astype(F32)
        mixed[s] = jnp.where(live, own, 0.0).astype(BF16)
    for slot, out in zip(slots, (near_out, far_out)):
        out[...] = scr[jnp.maximum(slot, 0)].astype(BF16)


def place_kernel(ways, facts, *refs):
    near_pages, *far_pages = refs[: 1 + ways]
    near_rows, *far_rows = refs[1 + ways : 2 + 2 * ways]
    mixed_in, _, _, mixed, key_out, value_out, stage, out_sems, line_sems, own_sem = refs[2 + 2 * ways :]
    pages = stage.shape[1] // 2
    page_len, head_dim = stage.shape[2:]
    slot_count, steps, width = mixed.shape
    row = lax.broadcasted_iota(jnp.int32, (page_len, head_dim), 0)
    far_gap = facts[FAR_GAP]
    cases = [(0, facts[IN_NEAR], facts[NEAR_LEN], facts[IN_NEAR] >= 0, near_pages, near_rows)]
    for way in range(ways):
        came = facts[IN_FAR] >= 0
        if ways == 2:
            came = came & ((far_gap == 1) == (way == 0))
        cases.append((1, facts[IN_FAR], facts[FAR_LEN], came, far_pages[way], far_rows[way]))

    def store(n, slot, p, which, source):
        pool = (key_out, value_out)[which]
        page = facts[LENGTHS + slot_count + slot * pages + p]
        return pltpu.make_async_copy(source, pool.at[page], out_sems.at[n, which, p])

    def store_line(n, slot, rows):
        return pltpu.make_async_copy(rows.at[:, pl.ds(0, width)], mixed.at[slot], line_sems.at[n])

    own = pltpu.make_async_copy(mixed_in, mixed, own_sem)
    own.start()
    for n, slot, length, came, arrived, rows in cases:

        @pl.when(came)
        def _():
            fresh = rows[:, width:].astype(F32)
            for p in range(pages):
                whole = length >= (p + 1) * page_len

                @pl.when(whole)
                def _():
                    for which in range(2):
                        store(n, slot, p, which, arrived.at[which * pages + p]).start()

                @pl.when(jnp.logical_not(whole))
                def _():
                    at = row + p * page_len
                    for which in range(2):
                        page = jnp.where(at < length, arrived[which * pages + p].astype(F32), 0.0)
                        for t in range(steps):
                            line = fresh[t : t + 1, which * head_dim : (which + 1) * head_dim]
                            page = jnp.where(at == length + t, line, page)
                        stage[n, which * pages + p] = page.astype(BF16)
                        store(n, slot, p, which, stage.at[n, which * pages + p]).start()

    own.wait()
    for n, slot, _, came, _, rows in cases:

        @pl.when(came)
        def _():
            store_line(n, slot, rows).start()

    for n, slot, _, came, arrived, rows in cases:

        @pl.when(came)
        def _():
            for p in range(pages):
                for which in range(2):
                    store(n, slot, p, which, arrived.at[which * pages + p]).wait()
            store_line(n, slot, rows).wait()


def run(
    near_hops,
    far_hops,
    near,
    far,
    facts,
    scalars,
    token_states,
    query_rows,
    key_weight,
    value_weight,
    out_weight,
    keys,
    values,
):
    groups = lax.axis_size("dec")
    tp = lax.axis_size("tp")
    slot_count, steps, model = token_states.shape
    _, page_len, head_dim = keys.shape
    rows = slot_count * steps
    width = out_weight.shape[1]
    heads = query_rows.shape[2] // head_dim
    pool_shape = jax.ShapeDtypeStruct(keys.shape, BF16)
    limit = pltpu.CompilerParams(vmem_limit_bytes=63 * 2**20)

    pages_in = [lax.ppermute(near, "dec", near_hops)] + [lax.ppermute(far, "dec", hops) for hops in far_hops]

    key_mid, value_mid, partial, new_rows = pl.pallas_call(
        attend_kernel,
        out_shape=(
            pool_shape,
            pool_shape,
            jax.ShapeDtypeStruct((rows, width), BF16),
            jax.ShapeDtypeStruct((rows, 2 * head_dim), BF16),
        ),
        in_specs=[SMEM] + [ANY] * 5 + [VMEM] * 2 + [ANY] * 3,
        out_specs=(HBM, HBM, VMEM, VMEM),
        scratch_shapes=[
            pltpu.VMEM(token_states.shape, BF16),
            pltpu.VMEM(query_rows.shape, BF16),
            pltpu.VMEM(key_weight.shape, BF16),
            pltpu.VMEM(value_weight.shape, BF16),
            pltpu.VMEM(out_weight.shape, BF16),
            pltpu.VMEM((heads * rows, head_dim), F32),
            pltpu.VMEM((heads * rows, head_dim), F32),
            pltpu.VMEM((2, slot_count, steps, 16, head_dim), BF16),
            pltpu.SemaphoreType.DMA((2 + 3 * PARTS,)),
            pltpu.SemaphoreType.DMA((2,)),
            pltpu.SemaphoreType.DMA((2, slot_count, steps)),
        ],
        compiler_params=pltpu.CompilerParams(vmem_limit_bytes=40 * 2**20),
        cost_estimate=pl.CostEstimate(flops=1_000_000, bytes_accessed=1_000_000, transcendentals=0),
        name="attend",
    )(
        facts,
        token_states,
        query_rows,
        key_weight,
        value_weight,
        out_weight,
        keys,
        values,
        *scalars,
    )

    others = [lax.ppermute(partial, "tp", [(i, i ^ n) for i in range(tp)]) for n in range(1, tp)]
    row_shape = jax.ShapeDtypeStruct((steps, width + 2 * head_dim), BF16)
    mixed_mid, near_row, far_row = pl.pallas_call(
        finish_rows_kernel,
        out_shape=(jax.ShapeDtypeStruct((slot_count, steps, width), BF16), row_shape, row_shape),
        in_specs=[SMEM, VMEM] + [VMEM] * tp,
        out_specs=(VMEM, VMEM, VMEM),
        scratch_shapes=[pltpu.VMEM((slot_count, steps, width + 2 * head_dim), F32)],
        compiler_params=pltpu.CompilerParams(vmem_limit_bytes=8 * 2**20),
        name="rows",
    )(facts, new_rows, partial, *others)
    rows_in = [lax.ppermute(near_row, "dec", near_hops)] + [lax.ppermute(far_row, "dec", hops) for hops in far_hops]
    pages = keys.shape[0] // slot_count
    ways = len(pages_in) - 1
    mixed_shape = jax.ShapeDtypeStruct((slot_count, steps, width), BF16)
    mixed, key_out, value_out = pl.pallas_call(
        functools.partial(place_kernel, ways),
        out_shape=(mixed_shape, pool_shape, pool_shape),
        in_specs=[SMEM] + [VMEM] * (2 + 2 * ways) + [VMEM] + [HBM] * 2,
        out_specs=(HBM, HBM, HBM),
        scratch_shapes=[
            pltpu.VMEM((2, 2 * pages, page_len, head_dim), BF16),
            pltpu.SemaphoreType.DMA((2, 2, pages)),
            pltpu.SemaphoreType.DMA((2,)),
            pltpu.SemaphoreType.DMA,
        ],
        input_output_aliases={4 + 2 * ways: 1, 5 + 2 * ways: 2},
        compiler_params=pltpu.CompilerParams(vmem_limit_bytes=41943040),
        name="place",
    )(facts, *pages_in, *rows_in, mixed_mid, key_mid, value_mid)
    return mixed, key_out, value_out


def moved(migrations, cached_len, table, inputs):
    groups = lax.axis_size("dec")
    half = groups // 2
    keys, values = inputs[-2:]
    scalars = (migrations, cached_len, table)
    _, page_len, head_dim = keys.shape
    pages, slot_count = table.shape[1:]
    facts_shape = jax.ShapeDtypeStruct((LENGTHS + slot_count + slot_count * pages,), jnp.int32)
    moved_shape = jax.ShapeDtypeStruct((2 * pages, page_len, head_dim), BF16)
    near, far, facts = pl.pallas_call(
        functools.partial(pack_kernel, groups),
        out_shape=(moved_shape, moved_shape, facts_shape),
        in_specs=[SMEM, SMEM, SMEM, HBM, HBM],
        out_specs=(VMEM, VMEM, SMEM),
        scratch_shapes=[pltpu.SemaphoreType.DMA((2, 2, pages))],
        compiler_params=pltpu.CompilerParams(vmem_limit_bytes=40 * 2**20),
        cost_estimate=pl.CostEstimate(flops=0, bytes_accessed=1_000_000, transcendentals=0),
        name="pack",
    )(migrations, cached_len, table, keys, values)
    if half != 2:
        far_hops = (shifted(groups, 1), shifted(groups, 1 + half))
        return run(shifted(groups, half), far_hops, near, far, facts, scalars, *inputs)
    branches = []
    for case in range(2**half):
        senders = [pair + half * (case >> pair & 1) for pair in range(half)]
        receivers = [(sender + half) % groups for sender in senders]
        near_hops = [(senders[pair], receivers[pair]) for pair in range(half)]
        far_hops = [(senders[pair], receivers[(pair + 1) % half]) for pair in range(half)]
        if len({sender < half for sender in senders}) > 1:
            near_hops += [(b, a) for a, b in near_hops]
            far_hops += [(b, a) for a, b in far_hops]
        branches.append(functools.partial(run, near_hops, (far_hops,)))
    outs = lax.switch(facts[NUMBER], branches, near, far, facts, scalars, *inputs)
    return pl.pallas_call(
        lambda *refs: None,
        out_shape=tuple(jax.ShapeDtypeStruct(out.shape, out.dtype) for out in outs),
        in_specs=[HBM] * 3,
        out_specs=(HBM,) * 3,
        input_output_aliases={0: 0, 1: 1, 2: 2},
        compiler_params=pltpu.CompilerParams(vmem_limit_bytes=67004006),
        name="keep",
    )(*outs)


def local(
    token_states,
    query_rows,
    key_weight,
    value_weight,
    out_weight,
    key_pool,
    value_pool,
    cached_len,
    page_table,
    migrations,
):
    groups = lax.axis_size("dec")
    pool_pages, _, page_len, head_dim = key_pool.shape
    slot_count, steps, _ = token_states.shape
    keys = key_pool.reshape(pool_pages, page_len, head_dim)
    values = value_pool.reshape(pool_pages, page_len, head_dim)
    table = jnp.swapaxes(page_table, 1, 2)
    pages = table.shape[1]
    inputs = (
        token_states,
        query_rows,
        key_weight,
        value_weight,
        out_weight,
        keys,
        values,
    )
    mixed, key_out, value_out = moved(migrations, cached_len, table, inputs)
    return mixed, key_out.reshape(key_pool.shape), value_out.reshape(value_pool.shape)


def solution(mesh):
    placed = (
        P(("rep", "dec"), None, None),
        P(("rep", "dec"), None, "tp"),
        P(None, "tp"),
        P(None, "tp"),
        P("tp", None),
        P(("rep", "dec"), "tp", None, None),
        P(("rep", "dec"), "tp", None, None),
        P("rep", None),
        P(("rep", "dec"), None, None),
        P("rep", None),
    )
    return jax.shard_map(
        local,
        mesh=mesh,
        in_specs=placed,
        out_specs=(
            P(("rep", "dec"), None, None),
            P(("rep", "dec"), "tp", None, None),
            P(("rep", "dec"), "tp", None, None),
        ),
        check_vma=False,
    )
```

```python
import functools

import jax
import jax.numpy as jnp
from jax import lax
from jax.experimental import pallas as pl
from jax.experimental.pallas import tpu as pltpu
from jax.sharding import PartitionSpec as P

F32 = jnp.float32
BF16 = jnp.bfloat16
PARTS = 4
SMEM = pl.BlockSpec(memory_space=pltpu.SMEM)
HBM = pl.BlockSpec(memory_space=pltpu.HBM)
ANY = pl.BlockSpec(memory_space=pl.ANY)
VMEM = pl.BlockSpec(memory_space=pltpu.VMEM)


def shifted(count, by):
    return [(i, (i + by) % count) for i in range(count)]


def outgoing(mig, me, groups):
    half = groups // 2
    near = far = jnp.int32(-1)
    for m in range(mig.shape[0]):
        mine = mig[m, 0] == me
        gap = lax.rem(mig[m, 2] - me + groups, groups)
        near = jnp.where(mine & (gap == half), mig[m, 1], near)
        far = jnp.where(mine & (gap != half), mig[m, 1], far)
    return near, far


def incoming(mig, lens, me, groups):
    half = groups // 2
    near = far = jnp.int32(-1)
    near_len = far_len = far_gap = jnp.int32(0)
    for m in range(mig.shape[0]):
        mine = mig[m, 2] == me
        gap = lax.rem(me - mig[m, 0] + groups, groups)
        length = lens[mig[m, 0], mig[m, 1]]
        is_near = mine & (gap == half)
        is_far = mine & (gap != half)
        near = jnp.where(is_near, mig[m, 3], near)
        near_len = jnp.where(is_near, length, near_len)
        far = jnp.where(is_far, mig[m, 3], far)
        far_len = jnp.where(is_far, length, far_len)
        far_gap = jnp.where(is_far, gap, far_gap)
    return (near, near_len), (far, far_len), far_gap


NUMBER, OUT_NEAR, OUT_FAR, IN_NEAR, NEAR_LEN, IN_FAR, FAR_LEN, FAR_GAP, LENGTHS = range(9)


def pack_kernel(groups, mig, lens, table, key_pool, value_pool, near_out, far_out, facts, sems):
    me = lax.axis_index("dec")
    _, pages, slot_count = table.shape
    outs = (near_out, far_out)
    slots = outgoing(mig, me, groups)

    def load(n, which, p):
        page = table[0, p, slots[n]]
        pool = (key_pool, value_pool)[which]
        return pltpu.make_async_copy(pool.at[page], outs[n].at[which * pages + p], sems.at[n, which, p])

    def each(do):
        for n in range(2):

            @pl.when(slots[n] >= 0)
            def _():
                for p in range(pages):
                    for which in range(2):
                        do(load(n, which, p))

    each(lambda copy: copy.start())
    half = groups // 2
    number = jnp.int32(0)
    if half == 2:
        for m in range(mig.shape[0]):
            number = number | jnp.where(mig[m, 0] >= half, mig[m, 0] - half + 1, 0)
    facts[NUMBER] = number
    facts[OUT_NEAR], facts[OUT_FAR] = slots
    near, far, far_gap = incoming(mig, lens, me, groups)
    facts[IN_NEAR], facts[NEAR_LEN] = near
    facts[IN_FAR], facts[FAR_LEN] = far
    facts[FAR_GAP] = far_gap
    for s in range(slot_count):
        facts[LENGTHS + s] = lens[me, s]
        for p in range(pages):
            facts[LENGTHS + slot_count + s * pages + p] = table[0, p, s]
    each(lambda copy: copy.wait())


def attend_kernel(
    facts,
    states_hbm,
    query_hbm,
    key_weight,
    value_weight,
    out_weight,
    kp,
    vp,
    mig,
    lens,
    table,
    key_out,
    value_out,
    partial,
    new_rows,
    states,
    query,
    wk,
    wv,
    wo,
    q_scr,
    a_scr,
    tiles,
    load_sems,
    store_sems,
    tile_sems,
):
    del mig, lens, table
    slot_count, steps, _ = states.shape
    rows = slot_count * steps
    page_len, head_dim = kp.shape[1:]
    pages = kp.shape[0] // slot_count
    heads = query.shape[2] // head_dim
    span = pages * page_len
    pools = ((kp, key_out, 0), (vp, value_out, head_dim))
    number = 0

    def split(source, target, parts):
        nonlocal number
        size = source.shape[0] // parts
        copies = []
        for part in range(parts):
            piece = pl.ds(part * size, size)
            copies.append(pltpu.make_async_copy(source.at[piece], target.at[piece], load_sems.at[number]))
            number += 1
        return copies

    (load_query,) = split(query_hbm, query, 1)
    (load_states,) = split(states_hbm, states, 1)
    load_wk = split(key_weight, wk, PARTS)
    load_wv = split(value_weight, wv, PARTS)
    loads = split(out_weight, wo, PARTS)
    stores = [pltpu.make_async_copy(pool, out, store_sems.at[n]) for n, (pool, out, _) in enumerate(pools)]
    for copy in [load_query, load_states] + load_wk + load_wv + loads + stores:
        copy.start()
    near, far = facts[OUT_NEAR], facts[OUT_FAR]
    lengths = [facts[LENGTHS + s] for s in range(slot_count)]
    first_page = [LENGTHS + slot_count + s * pages for s in range(slot_count)]
    numbers = [[facts[first_page[s] + p] for p in range(pages)] for s in range(slot_count)]

    load_query.wait()
    for s in range(slot_count):
        qf = query[s].astype(F32)
        for h in range(heads):
            q_scr[pl.ds(h * rows + s * steps, steps), :] = qf[:, h * head_dim : (h + 1) * head_dim]

    count = steps * heads
    nt = (((1,), (1,)), ((), ()))
    queries = jnp.concatenate(
        [q_scr[pl.ds(r, heads, stride=rows), :] for r in range(rows)], 0
    ).astype(BF16)
    position = lax.broadcasted_iota(jnp.int32, (count, span), 1)
    scaling = head_dim**-0.5
    scores = []
    for s in range(slot_count):
        keys = jnp.concatenate([kp[n] for n in numbers[s]], 0)
        cached = lax.dot_general(
            queries[s * count : (s + 1) * count], keys, nt, preferred_element_type=F32
        )
        scores.append(jnp.where(position < lengths[s], cached * scaling, -jnp.inf))
    cached = jnp.concatenate(scores, 0)

    load_states.wait()
    x = jnp.concatenate([states[s].astype(F32) for s in range(slot_count)], 0).astype(BF16)
    fresh_k = jnp.zeros((rows, head_dim), F32)
    fresh_v = jnp.zeros((rows, head_dim), F32)
    size = wk.shape[0] // PARTS
    for part in range(PARTS):
        piece = slice(part * size, (part + 1) * size)
        load_wk[part].wait()
        fresh_k = fresh_k + jnp.dot(x[:, piece], wk[piece, :], preferred_element_type=F32)
        load_wv[part].wait()
        fresh_v = fresh_v + jnp.dot(x[:, piece], wv[piece, :], preferred_element_type=F32)
    fresh_k = fresh_k.astype(BF16)
    fresh_v = fresh_v.astype(BF16)
    new_rows[:, :head_dim] = fresh_k
    new_rows[:, head_dim:] = fresh_v

    fresh = lax.dot_general(queries, fresh_k, nt, preferred_element_type=F32) * scaling
    fresh_row = lax.broadcasted_iota(jnp.int32, fresh.shape, 0)
    fresh_col = lax.broadcasted_iota(jnp.int32, fresh.shape, 1)
    first = fresh_row // count * steps
    allowed = (fresh_col >= first) & (fresh_col <= fresh_row // heads)
    fresh = jnp.where(allowed, fresh, -jnp.inf)
    peak = jnp.maximum(jnp.max(cached, 1, keepdims=True), jnp.max(fresh, 1, keepdims=True))
    cached = jnp.exp(cached - peak)
    fresh = jnp.exp(fresh - peak)
    share = 1.0 / (jnp.sum(cached, 1, keepdims=True) + jnp.sum(fresh, 1, keepdims=True))
    cached_w = (cached * share).astype(BF16)
    fresh_w = (fresh * share).astype(BF16)
    fresh_out = jnp.dot(fresh_w, fresh_v, preferred_element_type=F32)
    for s in range(slot_count):
        values = jnp.concatenate([vp[n] for n in numbers[s]], 0)
        piece = slice(s * count, (s + 1) * count)
        out = jnp.dot(cached_w[piece], values, preferred_element_type=F32) + fresh_out[piece]
        for t in range(steps):
            a_scr[pl.ds(s * steps + t, heads, stride=rows), :] = out[t * heads : (t + 1) * heads]

    tile = tiles.shape[3]
    row = lax.broadcasted_iota(jnp.int32, (tile, head_dim), 0)
    fresh_f = (fresh_k.astype(F32), fresh_v.astype(F32))
    places = []
    for s in range(slot_count):
        live = (lengths[s] > 0) & (s != near) & (s != far)
        for t in range(steps):
            at = lengths[s] + t
            page = facts[first_page[s] + at // page_len]
            low = at // tile * tile
            base = pl.multiple_of(lax.rem(low, page_len), tile)
            places.append((s, t, page, base, live & ((t == 0) | (lax.rem(at, tile) == 0))))
            for n, (pool, _, _) in enumerate(pools):
                merged = pool[page, pl.ds(base, tile), :].astype(F32)
                for u in range(steps):
                    line = fresh_f[n][s * steps + u : s * steps + u + 1]
                    merged = jnp.where(row + low == lengths[s] + u, line, merged)
                tiles[n, s, t] = merged.astype(BF16)
    for store in stores:
        store.wait()

    def put(n, s, t, page, base):
        return pltpu.make_async_copy(
            tiles.at[n, s, t], pools[n][1].at[page, pl.ds(base, tile), :], tile_sems.at[n, s, t]
        )

    for s, t, page, base, wanted in places:

        @pl.when(wanted)
        def _():
            for n in range(2):
                put(n, s, t, page, base).start()

    attention = jnp.concatenate([a_scr[h * rows : (h + 1) * rows, :].astype(BF16) for h in range(heads)], 1)
    result = jnp.zeros((rows, wo.shape[1]), F32)
    size = wo.shape[0] // PARTS
    for part in range(PARTS):
        piece = slice(part * size, (part + 1) * size)
        loads[part].wait()
        result = result + jnp.dot(attention[:, piece], wo[piece, :], preferred_element_type=F32)
    partial[...] = result.astype(BF16)
    for s, t, page, base, wanted in places:

        @pl.when(wanted)
        def _():
            for n in range(2):
                put(n, s, t, page, base).wait()


def finish_rows_kernel(facts, new_rows, *refs):
    *parts, mixed, near_out, far_out, scr = refs
    slots = facts[OUT_NEAR], facts[OUT_FAR]
    width = parts[0].shape[1]
    terms = [part[...].astype(F32) for part in parts]
    level = 1
    while level < len(terms):
        terms = [terms[n] + terms[n ^ level] for n in range(len(terms))]
        level *= 2
    total = terms[0]
    slot_count, steps, _ = scr.shape
    for s in range(slot_count):
        live = (facts[LENGTHS + s] > 0) & (s != slots[0]) & (s != slots[1])
        own = total[s * steps : (s + 1) * steps]
        scr[s, :, :width] = own
        scr[s, :, width:] = new_rows[s * steps : (s + 1) * steps, :].astype(F32)
        mixed[s] = jnp.where(live, own, 0.0).astype(BF16)
    for slot, out in zip(slots, (near_out, far_out)):
        out[...] = scr[jnp.maximum(slot, 0)].astype(BF16)


def place_kernel(ways, facts, *refs):
    near_pages, *far_pages = refs[: 1 + ways]
    near_rows, *far_rows = refs[1 + ways : 2 + 2 * ways]
    mixed_in, _, _, mixed, key_out, value_out, stage, out_sems, line_sems, own_sem = refs[2 + 2 * ways :]
    pages = stage.shape[1] // 2
    page_len, head_dim = stage.shape[2:]
    slot_count, steps, width = mixed.shape
    row = lax.broadcasted_iota(jnp.int32, (page_len, head_dim), 0)
    far_gap = facts[FAR_GAP]
    cases = [(0, facts[IN_NEAR], facts[NEAR_LEN], facts[IN_NEAR] >= 0, near_pages, near_rows)]
    for way in range(ways):
        came = facts[IN_FAR] >= 0
        if ways == 2:
            came = came & ((far_gap == 1) == (way == 0))
        cases.append((1, facts[IN_FAR], facts[FAR_LEN], came, far_pages[way], far_rows[way]))

    def store(n, slot, p, which, source):
        pool = (key_out, value_out)[which]
        page = facts[LENGTHS + slot_count + slot * pages + p]
        return pltpu.make_async_copy(source, pool.at[page], out_sems.at[n, which, p])

    def store_line(n, slot, rows):
        return pltpu.make_async_copy(rows.at[:, pl.ds(0, width)], mixed.at[slot], line_sems.at[n])

    own = pltpu.make_async_copy(mixed_in, mixed, own_sem)
    own.start()
    for n, slot, length, came, arrived, rows in cases:

        @pl.when(came)
        def _():
            fresh = rows[:, width:].astype(F32)
            for p in range(pages):
                whole = length >= (p + 1) * page_len

                @pl.when(whole)
                def _():
                    for which in range(2):
                        store(n, slot, p, which, arrived.at[which * pages + p]).start()

                @pl.when(jnp.logical_not(whole))
                def _():
                    at = row + p * page_len
                    for which in range(2):
                        page = jnp.where(at < length, arrived[which * pages + p].astype(F32), 0.0)
                        for t in range(steps):
                            line = fresh[t : t + 1, which * head_dim : (which + 1) * head_dim]
                            page = jnp.where(at == length + t, line, page)
                        stage[n, which * pages + p] = page.astype(BF16)
                        store(n, slot, p, which, stage.at[n, which * pages + p]).start()

    own.wait()
    for n, slot, _, came, _, rows in cases:

        @pl.when(came)
        def _():
            store_line(n, slot, rows).start()

    for n, slot, _, came, arrived, rows in cases:

        @pl.when(came)
        def _():
            for p in range(pages):
                for which in range(2):
                    store(n, slot, p, which, arrived.at[which * pages + p]).wait()
            store_line(n, slot, rows).wait()


def run(
    near_hops,
    far_hops,
    near,
    far,
    facts,
    scalars,
    token_states,
    query_rows,
    key_weight,
    value_weight,
    out_weight,
    keys,
    values,
):
    groups = lax.axis_size("dec")
    tp = lax.axis_size("tp")
    slot_count, steps, model = token_states.shape
    _, page_len, head_dim = keys.shape
    rows = slot_count * steps
    width = out_weight.shape[1]
    heads = query_rows.shape[2] // head_dim
    pool_shape = jax.ShapeDtypeStruct(keys.shape, BF16)
    limit = pltpu.CompilerParams(vmem_limit_bytes=63 * 2**20)

    pages_in = [lax.ppermute(near, "dec", near_hops)] + [lax.ppermute(far, "dec", hops) for hops in far_hops]

    key_mid, value_mid, partial, new_rows = pl.pallas_call(
        attend_kernel,
        out_shape=(
            pool_shape,
            pool_shape,
            jax.ShapeDtypeStruct((rows, width), BF16),
            jax.ShapeDtypeStruct((rows, 2 * head_dim), BF16),
        ),
        in_specs=[SMEM] + [ANY] * 5 + [VMEM] * 2 + [ANY] * 3,
        out_specs=(HBM, HBM, VMEM, VMEM),
        scratch_shapes=[
            pltpu.VMEM(token_states.shape, BF16),
            pltpu.VMEM(query_rows.shape, BF16),
            pltpu.VMEM(key_weight.shape, BF16),
            pltpu.VMEM(value_weight.shape, BF16),
            pltpu.VMEM(out_weight.shape, BF16),
            pltpu.VMEM(((heads + 1) * rows, head_dim), F32),
            pltpu.VMEM(((heads + 1) * rows, head_dim), F32),
            pltpu.VMEM((2, slot_count, steps, 16, head_dim), BF16),
            pltpu.SemaphoreType.DMA((2 + 3 * PARTS,)),
            pltpu.SemaphoreType.DMA((2,)),
            pltpu.SemaphoreType.DMA((2, slot_count, steps)),
        ],
        compiler_params=pltpu.CompilerParams(vmem_limit_bytes=40 * 2**20),
        cost_estimate=pl.CostEstimate(flops=1_000_000, bytes_accessed=1_000_000, transcendentals=0),
        name="attend",
    )(
        facts,
        token_states,
        query_rows,
        key_weight,
        value_weight,
        out_weight,
        keys,
        values,
        *scalars,
    )

    others = [lax.ppermute(partial, "tp", [(i, i ^ n) for i in range(tp)]) for n in range(1, tp)]
    row_shape = jax.ShapeDtypeStruct((steps, width + 2 * head_dim), BF16)
    mixed_mid, near_row, far_row = pl.pallas_call(
        finish_rows_kernel,
        out_shape=(jax.ShapeDtypeStruct((slot_count, steps, width), BF16), row_shape, row_shape),
        in_specs=[SMEM, VMEM] + [VMEM] * tp,
        out_specs=(VMEM, VMEM, VMEM),
        scratch_shapes=[pltpu.VMEM((slot_count, steps, width + 2 * head_dim), F32)],
        compiler_params=pltpu.CompilerParams(vmem_limit_bytes=8 * 2**20),
        name="rows",
    )(facts, new_rows, partial, *others)
    rows_in = [lax.ppermute(near_row, "dec", near_hops)] + [lax.ppermute(far_row, "dec", hops) for hops in far_hops]
    pages = keys.shape[0] // slot_count
    ways = len(pages_in) - 1
    mixed_shape = jax.ShapeDtypeStruct((slot_count, steps, width), BF16)
    mixed, key_out, value_out = pl.pallas_call(
        functools.partial(place_kernel, ways),
        out_shape=(mixed_shape, pool_shape, pool_shape),
        in_specs=[SMEM] + [VMEM] * (2 + 2 * ways) + [VMEM] + [HBM] * 2,
        out_specs=(HBM, HBM, HBM),
        scratch_shapes=[
            pltpu.VMEM((2, 2 * pages, page_len, head_dim), BF16),
            pltpu.SemaphoreType.DMA((2, 2, pages)),
            pltpu.SemaphoreType.DMA((2,)),
            pltpu.SemaphoreType.DMA,
        ],
        input_output_aliases={4 + 2 * ways: 1, 5 + 2 * ways: 2},
        compiler_params=pltpu.CompilerParams(vmem_limit_bytes=41943040),
        name="place",
    )(facts, *pages_in, *rows_in, mixed_mid, key_mid, value_mid)
    return mixed, key_out, value_out


def moved(migrations, cached_len, table, inputs):
    groups = lax.axis_size("dec")
    half = groups // 2
    keys, values = inputs[-2:]
    scalars = (migrations, cached_len, table)
    _, page_len, head_dim = keys.shape
    pages, slot_count = table.shape[1:]
    facts_shape = jax.ShapeDtypeStruct((LENGTHS + slot_count + slot_count * pages,), jnp.int32)
    moved_shape = jax.ShapeDtypeStruct((2 * pages, page_len, head_dim), BF16)
    near, far, facts = pl.pallas_call(
        functools.partial(pack_kernel, groups),
        out_shape=(moved_shape, moved_shape, facts_shape),
        in_specs=[SMEM, SMEM, SMEM, HBM, HBM],
        out_specs=(VMEM, VMEM, SMEM),
        scratch_shapes=[pltpu.SemaphoreType.DMA((2, 2, pages))],
        compiler_params=pltpu.CompilerParams(vmem_limit_bytes=40 * 2**20),
        cost_estimate=pl.CostEstimate(flops=0, bytes_accessed=1_000_000, transcendentals=0),
        name="pack",
    )(migrations, cached_len, table, keys, values)
    if half != 2:
        far_hops = (shifted(groups, 1), shifted(groups, 1 + half))
        return run(shifted(groups, half), far_hops, near, far, facts, scalars, *inputs)
    branches = []
    for case in range(2**half):
        senders = [pair + half * (case >> pair & 1) for pair in range(half)]
        receivers = [(sender + half) % groups for sender in senders]
        near_hops = [(senders[pair], receivers[pair]) for pair in range(half)]
        far_hops = [(senders[pair], receivers[(pair + 1) % half]) for pair in range(half)]
        near_hops += [(b, a) for a, b in near_hops]
        far_hops += [(b, a) for a, b in far_hops]
        branches.append(functools.partial(run, near_hops, (far_hops,)))
    outs = lax.switch(facts[NUMBER], branches, near, far, facts, scalars, *inputs)
    return pl.pallas_call(
        lambda *refs: None,
        out_shape=tuple(jax.ShapeDtypeStruct(out.shape, out.dtype) for out in outs),
        in_specs=[HBM] * 3,
        out_specs=(HBM,) * 3,
        input_output_aliases={0: 0, 1: 1, 2: 2},
        compiler_params=pltpu.CompilerParams(vmem_limit_bytes=67004006),
        name="keep",
    )(*outs)


def local(
    token_states,
    query_rows,
    key_weight,
    value_weight,
    out_weight,
    key_pool,
    value_pool,
    cached_len,
    page_table,
    migrations,
):
    groups = lax.axis_size("dec")
    pool_pages, _, page_len, head_dim = key_pool.shape
    slot_count, steps, _ = token_states.shape
    keys = key_pool.reshape(pool_pages, page_len, head_dim)
    values = value_pool.reshape(pool_pages, page_len, head_dim)
    table = jnp.swapaxes(page_table, 1, 2)
    pages = table.shape[1]
    inputs = (
        token_states,
        query_rows,
        key_weight,
        value_weight,
        out_weight,
        keys,
        values,
    )
    mixed, key_out, value_out = moved(migrations, cached_len, table, inputs)
    return mixed, key_out.reshape(key_pool.shape), value_out.reshape(value_pool.shape)


def solution(mesh):
    placed = (
        P(("rep", "dec"), None, None),
        P(("rep", "dec"), None, "tp"),
        P(None, "tp"),
        P(None, "tp"),
        P("tp", None),
        P(("rep", "dec"), "tp", None, None),
        P(("rep", "dec"), "tp", None, None),
        P("rep", None),
        P(("rep", "dec"), None, None),
        P("rep", None),
    )
    return jax.shard_map(
        local,
        mesh=mesh,
        in_specs=placed,
        out_specs=(
            P(("rep", "dec"), None, None),
            P(("rep", "dec"), "tp", None, None),
            P(("rep", "dec"), "tp", None, None),
        ),
        check_vma=False,
    )
```

```python
import functools

import jax
import jax.numpy as jnp
from jax import lax
from jax.experimental import pallas as pl
from jax.experimental.pallas import tpu as pltpu
from jax.sharding import PartitionSpec as P

F32 = jnp.float32
BF16 = jnp.bfloat16
PARTS = 4
SMEM = pl.BlockSpec(memory_space=pltpu.SMEM)
HBM = pl.BlockSpec(memory_space=pltpu.HBM)
ANY = pl.BlockSpec(memory_space=pl.ANY)
VMEM = pl.BlockSpec(memory_space=pltpu.VMEM)


def shifted(count, by):
    return [(i, (i + by) % count) for i in range(count)]


def outgoing(mig, me, groups):
    half = groups // 2
    near = far = jnp.int32(-1)
    for m in range(mig.shape[0]):
        mine = mig[m, 0] == me
        gap = lax.rem(mig[m, 2] - me + groups, groups)
        near = jnp.where(mine & (gap == half), mig[m, 1], near)
        far = jnp.where(mine & (gap != half), mig[m, 1], far)
    return near, far


def incoming(mig, lens, me, groups):
    half = groups // 2
    near = far = jnp.int32(-1)
    near_len = far_len = far_gap = jnp.int32(0)
    for m in range(mig.shape[0]):
        mine = mig[m, 2] == me
        gap = lax.rem(me - mig[m, 0] + groups, groups)
        length = lens[mig[m, 0], mig[m, 1]]
        is_near = mine & (gap == half)
        is_far = mine & (gap != half)
        near = jnp.where(is_near, mig[m, 3], near)
        near_len = jnp.where(is_near, length, near_len)
        far = jnp.where(is_far, mig[m, 3], far)
        far_len = jnp.where(is_far, length, far_len)
        far_gap = jnp.where(is_far, gap, far_gap)
    return (near, near_len), (far, far_len), far_gap


NUMBER, OUT_NEAR, OUT_FAR, IN_NEAR, NEAR_LEN, IN_FAR, FAR_LEN, FAR_GAP, LENGTHS = range(9)


def pack_kernel(groups, mig, lens, table, key_pool, value_pool, near_out, far_out, facts, sems):
    me = lax.axis_index("dec")
    _, pages, slot_count = table.shape
    outs = (near_out, far_out)
    slots = outgoing(mig, me, groups)

    def load(n, which, p):
        page = table[0, p, slots[n]]
        pool = (key_pool, value_pool)[which]
        return pltpu.make_async_copy(pool.at[page], outs[n].at[which * pages + p], sems.at[n, which, p])

    def each(do):
        for n in range(2):

            @pl.when(slots[n] >= 0)
            def _():
                for p in range(pages):
                    for which in range(2):
                        do(load(n, which, p))

    each(lambda copy: copy.start())
    half = groups // 2
    number = jnp.int32(0)
    if half == 2:
        for m in range(mig.shape[0]):
            number = number | jnp.where(mig[m, 0] >= half, mig[m, 0] - half + 1, 0)
    facts[NUMBER] = number
    facts[OUT_NEAR], facts[OUT_FAR] = slots
    near, far, far_gap = incoming(mig, lens, me, groups)
    facts[IN_NEAR], facts[NEAR_LEN] = near
    facts[IN_FAR], facts[FAR_LEN] = far
    facts[FAR_GAP] = far_gap
    for s in range(slot_count):
        facts[LENGTHS + s] = lens[me, s]
        for p in range(pages):
            facts[LENGTHS + slot_count + s * pages + p] = table[0, p, s]
    each(lambda copy: copy.wait())


def attend_kernel(
    facts,
    states_hbm,
    query_hbm,
    key_weight,
    value_weight,
    out_weight,
    kp,
    vp,
    mig,
    lens,
    table,
    key_out,
    value_out,
    partial,
    new_rows,
    states,
    query,
    wk,
    wv,
    wo,
    q_scr,
    a_scr,
    tiles,
    load_sems,
    store_sems,
    tile_sems,
):
    del mig, lens, table
    slot_count, steps, _ = states.shape
    rows = slot_count * steps
    page_len, head_dim = kp.shape[1:]
    pages = kp.shape[0] // slot_count
    heads = query.shape[2] // head_dim
    span = pages * page_len
    pools = ((kp, key_out, 0), (vp, value_out, head_dim))
    number = 0

    def split(source, target, parts):
        nonlocal number
        size = source.shape[0] // parts
        copies = []
        for part in range(parts):
            piece = pl.ds(part * size, size)
            copies.append(pltpu.make_async_copy(source.at[piece], target.at[piece], load_sems.at[number]))
            number += 1
        return copies

    (load_query,) = split(query_hbm, query, 1)
    (load_states,) = split(states_hbm, states, 1)
    load_wk = split(key_weight, wk, PARTS)
    load_wv = split(value_weight, wv, PARTS)
    loads = split(out_weight, wo, PARTS)
    stores = [pltpu.make_async_copy(pool, out, store_sems.at[n]) for n, (pool, out, _) in enumerate(pools)]
    for copy in [load_query, load_states] + load_wk + load_wv + loads:
        copy.start()
    near, far = facts[OUT_NEAR], facts[OUT_FAR]
    lengths = [facts[LENGTHS + s] for s in range(slot_count)]
    first_page = [LENGTHS + slot_count + s * pages for s in range(slot_count)]
    numbers = [[facts[first_page[s] + p] for p in range(pages)] for s in range(slot_count)]

    load_query.wait()
    for s in range(slot_count):
        qf = query[s].astype(F32)
        for h in range(heads):
            q_scr[pl.ds(h * rows + s * steps, steps), :] = qf[:, h * head_dim : (h + 1) * head_dim]

    count = steps * heads
    nt = (((1,), (1,)), ((), ()))
    queries = jnp.concatenate(
        [q_scr[pl.ds(r, heads, stride=rows), :] for r in range(rows)], 0
    ).astype(BF16)
    position = lax.broadcasted_iota(jnp.int32, (count, span), 1)
    scaling = head_dim**-0.5
    scores = []
    for s in range(slot_count):
        keys = jnp.concatenate([kp[n] for n in numbers[s]], 0)
        cached = lax.dot_general(
            queries[s * count : (s + 1) * count], keys, nt, preferred_element_type=F32
        )
        scores.append(jnp.where(position < lengths[s], cached * scaling, -jnp.inf))
    cached = jnp.concatenate(scores, 0)

    for store in stores:
        store.start()
    load_states.wait()
    x = jnp.concatenate([states[s].astype(F32) for s in range(slot_count)], 0).astype(BF16)
    fresh_k = jnp.zeros((rows, head_dim), F32)
    fresh_v = jnp.zeros((rows, head_dim), F32)
    size = wk.shape[0] // PARTS
    for part in range(PARTS):
        piece = slice(part * size, (part + 1) * size)
        load_wk[part].wait()
        fresh_k = fresh_k + jnp.dot(x[:, piece], wk[piece, :], preferred_element_type=F32)
        load_wv[part].wait()
        fresh_v = fresh_v + jnp.dot(x[:, piece], wv[piece, :], preferred_element_type=F32)
    fresh_k = fresh_k.astype(BF16)
    fresh_v = fresh_v.astype(BF16)
    new_rows[:, :head_dim] = fresh_k
    new_rows[:, head_dim:] = fresh_v

    fresh = lax.dot_general(queries, fresh_k, nt, preferred_element_type=F32) * scaling
    fresh_row = lax.broadcasted_iota(jnp.int32, fresh.shape, 0)
    fresh_col = lax.broadcasted_iota(jnp.int32, fresh.shape, 1)
    first = fresh_row // count * steps
    allowed = (fresh_col >= first) & (fresh_col <= fresh_row // heads)
    fresh = jnp.where(allowed, fresh, -jnp.inf)
    peak = jnp.maximum(jnp.max(cached, 1, keepdims=True), jnp.max(fresh, 1, keepdims=True))
    cached = jnp.exp(cached - peak)
    fresh = jnp.exp(fresh - peak)
    share = 1.0 / (jnp.sum(cached, 1, keepdims=True) + jnp.sum(fresh, 1, keepdims=True))
    cached_w = (cached * share).astype(BF16)
    fresh_w = (fresh * share).astype(BF16)
    fresh_out = jnp.dot(fresh_w, fresh_v, preferred_element_type=F32)
    for s in range(slot_count):
        values = jnp.concatenate([vp[n] for n in numbers[s]], 0)
        piece = slice(s * count, (s + 1) * count)
        out = jnp.dot(cached_w[piece], values, preferred_element_type=F32) + fresh_out[piece]
        for t in range(steps):
            a_scr[pl.ds(s * steps + t, heads, stride=rows), :] = out[t * heads : (t + 1) * heads]

    tile = tiles.shape[3]
    row = lax.broadcasted_iota(jnp.int32, (tile, head_dim), 0)
    fresh_f = (fresh_k.astype(F32), fresh_v.astype(F32))
    places = []
    for s in range(slot_count):
        live = (lengths[s] > 0) & (s != near) & (s != far)
        for t in range(steps):
            at = lengths[s] + t
            page = facts[first_page[s] + at // page_len]
            low = at // tile * tile
            base = pl.multiple_of(lax.rem(low, page_len), tile)
            places.append((s, t, page, base, live & ((t == 0) | (lax.rem(at, tile) == 0))))
            for n, (pool, _, _) in enumerate(pools):
                merged = pool[page, pl.ds(base, tile), :].astype(F32)
                for u in range(steps):
                    line = fresh_f[n][s * steps + u : s * steps + u + 1]
                    merged = jnp.where(row + low == lengths[s] + u, line, merged)
                tiles[n, s, t] = merged.astype(BF16)
    for store in stores:
        store.wait()

    def put(n, s, t, page, base):
        return pltpu.make_async_copy(
            tiles.at[n, s, t], pools[n][1].at[page, pl.ds(base, tile), :], tile_sems.at[n, s, t]
        )

    for s, t, page, base, wanted in places:

        @pl.when(wanted)
        def _():
            for n in range(2):
                put(n, s, t, page, base).start()

    attention = jnp.concatenate([a_scr[h * rows : (h + 1) * rows, :].astype(BF16) for h in range(heads)], 1)
    result = jnp.zeros((rows, wo.shape[1]), F32)
    size = wo.shape[0] // PARTS
    for part in range(PARTS):
        piece = slice(part * size, (part + 1) * size)
        loads[part].wait()
        result = result + jnp.dot(attention[:, piece], wo[piece, :], preferred_element_type=F32)
    partial[...] = result.astype(BF16)
    for s, t, page, base, wanted in places:

        @pl.when(wanted)
        def _():
            for n in range(2):
                put(n, s, t, page, base).wait()


def finish_rows_kernel(facts, new_rows, *refs):
    *parts, mixed, near_out, far_out, scr = refs
    slots = facts[OUT_NEAR], facts[OUT_FAR]
    width = parts[0].shape[1]
    terms = [part[...].astype(F32) for part in parts]
    level = 1
    while level < len(terms):
        terms = [terms[n] + terms[n ^ level] for n in range(len(terms))]
        level *= 2
    total = terms[0]
    slot_count, steps, _ = scr.shape
    for s in range(slot_count):
        live = (facts[LENGTHS + s] > 0) & (s != slots[0]) & (s != slots[1])
        own = total[s * steps : (s + 1) * steps]
        scr[s, :, :width] = own
        scr[s, :, width:] = new_rows[s * steps : (s + 1) * steps, :].astype(F32)
        mixed[s] = jnp.where(live, own, 0.0).astype(BF16)
    for slot, out in zip(slots, (near_out, far_out)):
        out[...] = scr[jnp.maximum(slot, 0)].astype(BF16)


def place_kernel(ways, facts, *refs):
    near_pages, *far_pages = refs[: 1 + ways]
    near_rows, *far_rows = refs[1 + ways : 2 + 2 * ways]
    mixed_in, _, _, mixed, key_out, value_out, stage, out_sems, line_sems, own_sem = refs[2 + 2 * ways :]
    pages = stage.shape[1] // 2
    page_len, head_dim = stage.shape[2:]
    slot_count, steps, width = mixed.shape
    row = lax.broadcasted_iota(jnp.int32, (page_len, head_dim), 0)
    far_gap = facts[FAR_GAP]
    cases = [(0, facts[IN_NEAR], facts[NEAR_LEN], facts[IN_NEAR] >= 0, near_pages, near_rows)]
    for way in range(ways):
        came = facts[IN_FAR] >= 0
        if ways == 2:
            came = came & ((far_gap == 1) == (way == 0))
        cases.append((1, facts[IN_FAR], facts[FAR_LEN], came, far_pages[way], far_rows[way]))

    def store(n, slot, p, which, source):
        pool = (key_out, value_out)[which]
        page = facts[LENGTHS + slot_count + slot * pages + p]
        return pltpu.make_async_copy(source, pool.at[page], out_sems.at[n, which, p])

    def store_line(n, slot, rows):
        return pltpu.make_async_copy(rows.at[:, pl.ds(0, width)], mixed.at[slot], line_sems.at[n])

    own = pltpu.make_async_copy(mixed_in, mixed, own_sem)
    own.start()
    for n, slot, length, came, arrived, rows in cases:

        @pl.when(came)
        def _():
            fresh = rows[:, width:].astype(F32)
            for p in range(pages):
                whole = length >= (p + 1) * page_len

                @pl.when(whole)
                def _():
                    for which in range(2):
                        store(n, slot, p, which, arrived.at[which * pages + p]).start()

                @pl.when(jnp.logical_not(whole))
                def _():
                    at = row + p * page_len
                    for which in range(2):
                        page = jnp.where(at < length, arrived[which * pages + p].astype(F32), 0.0)
                        for t in range(steps):
                            line = fresh[t : t + 1, which * head_dim : (which + 1) * head_dim]
                            page = jnp.where(at == length + t, line, page)
                        stage[n, which * pages + p] = page.astype(BF16)
                        store(n, slot, p, which, stage.at[n, which * pages + p]).start()

    own.wait()
    for n, slot, _, came, _, rows in cases:

        @pl.when(came)
        def _():
            store_line(n, slot, rows).start()

    for n, slot, _, came, arrived, rows in cases:

        @pl.when(came)
        def _():
            for p in range(pages):
                for which in range(2):
                    store(n, slot, p, which, arrived.at[which * pages + p]).wait()
            store_line(n, slot, rows).wait()


def run(
    near_hops,
    far_hops,
    near,
    far,
    facts,
    scalars,
    token_states,
    query_rows,
    key_weight,
    value_weight,
    out_weight,
    keys,
    values,
):
    groups = lax.axis_size("dec")
    tp = lax.axis_size("tp")
    slot_count, steps, model = token_states.shape
    _, page_len, head_dim = keys.shape
    rows = slot_count * steps
    width = out_weight.shape[1]
    heads = query_rows.shape[2] // head_dim
    pool_shape = jax.ShapeDtypeStruct(keys.shape, BF16)
    limit = pltpu.CompilerParams(vmem_limit_bytes=63 * 2**20)

    pages_in = [lax.ppermute(near, "dec", near_hops)] + [lax.ppermute(far, "dec", hops) for hops in far_hops]

    key_mid, value_mid, partial, new_rows = pl.pallas_call(
        attend_kernel,
        out_shape=(
            pool_shape,
            pool_shape,
            jax.ShapeDtypeStruct((rows, width), BF16),
            jax.ShapeDtypeStruct((rows, 2 * head_dim), BF16),
        ),
        in_specs=[SMEM] + [ANY] * 5 + [VMEM] * 2 + [ANY] * 3,
        out_specs=(HBM, HBM, VMEM, VMEM),
        scratch_shapes=[
            pltpu.VMEM(token_states.shape, BF16),
            pltpu.VMEM(query_rows.shape, BF16),
            pltpu.VMEM(key_weight.shape, BF16),
            pltpu.VMEM(value_weight.shape, BF16),
            pltpu.VMEM(out_weight.shape, BF16),
            pltpu.VMEM(((heads + 1) * rows, head_dim), F32),
            pltpu.VMEM(((heads + 1) * rows, head_dim), F32),
            pltpu.VMEM((2, slot_count, steps, 16, head_dim), BF16),
            pltpu.SemaphoreType.DMA((2 + 3 * PARTS,)),
            pltpu.SemaphoreType.DMA((2,)),
            pltpu.SemaphoreType.DMA((2, slot_count, steps)),
        ],
        compiler_params=pltpu.CompilerParams(vmem_limit_bytes=40 * 2**20),
        cost_estimate=pl.CostEstimate(flops=1_000_000, bytes_accessed=1_000_000, transcendentals=0),
        name="attend",
    )(
        facts,
        token_states,
        query_rows,
        key_weight,
        value_weight,
        out_weight,
        keys,
        values,
        *scalars,
    )

    others = [lax.ppermute(partial, "tp", [(i, i ^ n) for i in range(tp)]) for n in range(1, tp)]
    row_shape = jax.ShapeDtypeStruct((steps, width + 2 * head_dim), BF16)
    mixed_mid, near_row, far_row = pl.pallas_call(
        finish_rows_kernel,
        out_shape=(jax.ShapeDtypeStruct((slot_count, steps, width), BF16), row_shape, row_shape),
        in_specs=[SMEM, VMEM] + [VMEM] * tp,
        out_specs=(VMEM, VMEM, VMEM),
        scratch_shapes=[pltpu.VMEM((slot_count, steps, width + 2 * head_dim), F32)],
        compiler_params=pltpu.CompilerParams(vmem_limit_bytes=8 * 2**20),
        name="rows",
    )(facts, new_rows, partial, *others)
    rows_in = [lax.ppermute(near_row, "dec", near_hops)] + [lax.ppermute(far_row, "dec", hops) for hops in far_hops]
    pages = keys.shape[0] // slot_count
    ways = len(pages_in) - 1
    mixed_shape = jax.ShapeDtypeStruct((slot_count, steps, width), BF16)
    mixed, key_out, value_out = pl.pallas_call(
        functools.partial(place_kernel, ways),
        out_shape=(mixed_shape, pool_shape, pool_shape),
        in_specs=[SMEM] + [VMEM] * (2 + 2 * ways) + [VMEM] + [HBM] * 2,
        out_specs=(HBM, HBM, HBM),
        scratch_shapes=[
            pltpu.VMEM((2, 2 * pages, page_len, head_dim), BF16),
            pltpu.SemaphoreType.DMA((2, 2, pages)),
            pltpu.SemaphoreType.DMA((2,)),
            pltpu.SemaphoreType.DMA,
        ],
        input_output_aliases={4 + 2 * ways: 1, 5 + 2 * ways: 2},
        compiler_params=pltpu.CompilerParams(vmem_limit_bytes=41943040),
        name="place",
    )(facts, *pages_in, *rows_in, mixed_mid, key_mid, value_mid)
    return mixed, key_out, value_out


def moved(migrations, cached_len, table, inputs):
    groups = lax.axis_size("dec")
    half = groups // 2
    keys, values = inputs[-2:]
    scalars = (migrations, cached_len, table)
    _, page_len, head_dim = keys.shape
    pages, slot_count = table.shape[1:]
    facts_shape = jax.ShapeDtypeStruct((LENGTHS + slot_count + slot_count * pages,), jnp.int32)
    moved_shape = jax.ShapeDtypeStruct((2 * pages, page_len, head_dim), BF16)
    near, far, facts = pl.pallas_call(
        functools.partial(pack_kernel, groups),
        out_shape=(moved_shape, moved_shape, facts_shape),
        in_specs=[SMEM, SMEM, SMEM, HBM, HBM],
        out_specs=(VMEM, VMEM, SMEM),
        scratch_shapes=[pltpu.SemaphoreType.DMA((2, 2, pages))],
        compiler_params=pltpu.CompilerParams(vmem_limit_bytes=40 * 2**20),
        cost_estimate=pl.CostEstimate(flops=0, bytes_accessed=1_000_000, transcendentals=0),
        name="pack",
    )(migrations, cached_len, table, keys, values)
    if half != 2:
        far_hops = (shifted(groups, 1), shifted(groups, 1 + half))
        return run(shifted(groups, half), far_hops, near, far, facts, scalars, *inputs)
    branches = []
    for case in range(2**half):
        senders = [pair + half * (case >> pair & 1) for pair in range(half)]
        receivers = [(sender + half) % groups for sender in senders]
        near_hops = [(senders[pair], receivers[pair]) for pair in range(half)]
        far_hops = [(senders[pair], receivers[(pair + 1) % half]) for pair in range(half)]
        if max(senders) >= half:
            near_hops += [(b, a) for a, b in near_hops]
            far_hops += [(b, a) for a, b in far_hops]
        branches.append(functools.partial(run, near_hops, (far_hops,)))
    outs = lax.switch(facts[NUMBER], branches, near, far, facts, scalars, *inputs)
    return pl.pallas_call(
        lambda *refs: None,
        out_shape=tuple(jax.ShapeDtypeStruct(out.shape, out.dtype) for out in outs),
        in_specs=[HBM] * 3,
        out_specs=(HBM,) * 3,
        input_output_aliases={0: 0, 1: 1, 2: 2},
        compiler_params=pltpu.CompilerParams(vmem_limit_bytes=67004006),
        name="keep",
    )(*outs)


def local(
    token_states,
    query_rows,
    key_weight,
    value_weight,
    out_weight,
    key_pool,
    value_pool,
    cached_len,
    page_table,
    migrations,
):
    groups = lax.axis_size("dec")
    pool_pages, _, page_len, head_dim = key_pool.shape
    slot_count, steps, _ = token_states.shape
    keys = key_pool.reshape(pool_pages, page_len, head_dim)
    values = value_pool.reshape(pool_pages, page_len, head_dim)
    table = jnp.swapaxes(page_table, 1, 2)
    pages = table.shape[1]
    inputs = (
        token_states,
        query_rows,
        key_weight,
        value_weight,
        out_weight,
        keys,
        values,
    )
    mixed, key_out, value_out = moved(migrations, cached_len, table, inputs)
    return mixed, key_out.reshape(key_pool.shape), value_out.reshape(value_pool.shape)


def solution(mesh):
    placed = (
        P(("rep", "dec"), None, None),
        P(("rep", "dec"), None, "tp"),
        P(None, "tp"),
        P(None, "tp"),
        P("tp", None),
        P(("rep", "dec"), "tp", None, None),
        P(("rep", "dec"), "tp", None, None),
        P("rep", None),
        P(("rep", "dec"), None, None),
        P("rep", None),
    )
    return jax.shard_map(
        local,
        mesh=mesh,
        in_specs=placed,
        out_specs=(
            P(("rep", "dec"), None, None),
            P(("rep", "dec"), "tp", None, None),
            P(("rep", "dec"), "tp", None, None),
        ),
        check_vma=False,
    )
```

```python
import functools

import jax
import jax.numpy as jnp
from jax import lax
from jax.experimental import pallas as pl
from jax.experimental.pallas import tpu as pltpu
from jax.sharding import PartitionSpec as P

F32 = jnp.float32
BF16 = jnp.bfloat16
PARTS = 4
SMEM = pl.BlockSpec(memory_space=pltpu.SMEM)
HBM = pl.BlockSpec(memory_space=pltpu.HBM)
ANY = pl.BlockSpec(memory_space=pl.ANY)
VMEM = pl.BlockSpec(memory_space=pltpu.VMEM)


def shifted(count, by):
    return [(i, (i + by) % count) for i in range(count)]


def outgoing(mig, me, groups):
    half = groups // 2
    near = far = jnp.int32(-1)
    for m in range(mig.shape[0]):
        mine = mig[m, 0] == me
        gap = lax.rem(mig[m, 2] - me + groups, groups)
        near = jnp.where(mine & (gap == half), mig[m, 1], near)
        far = jnp.where(mine & (gap != half), mig[m, 1], far)
    return near, far


def incoming(mig, lens, me, groups):
    half = groups // 2
    near = far = jnp.int32(-1)
    near_len = far_len = far_gap = jnp.int32(0)
    for m in range(mig.shape[0]):
        mine = mig[m, 2] == me
        gap = lax.rem(me - mig[m, 0] + groups, groups)
        length = lens[mig[m, 0], mig[m, 1]]
        is_near = mine & (gap == half)
        is_far = mine & (gap != half)
        near = jnp.where(is_near, mig[m, 3], near)
        near_len = jnp.where(is_near, length, near_len)
        far = jnp.where(is_far, mig[m, 3], far)
        far_len = jnp.where(is_far, length, far_len)
        far_gap = jnp.where(is_far, gap, far_gap)
    return (near, near_len), (far, far_len), far_gap


NUMBER, OUT_NEAR, OUT_FAR, IN_NEAR, NEAR_LEN, IN_FAR, FAR_LEN, FAR_GAP, LENGTHS = range(9)


def pack_kernel(groups, mig, lens, table, key_pool, value_pool, near_out, far_out, facts, sems):
    me = lax.axis_index("dec")
    _, pages, slot_count = table.shape
    outs = (near_out, far_out)
    slots = outgoing(mig, me, groups)

    def load(n, which, p):
        page = table[0, p, slots[n]]
        pool = (key_pool, value_pool)[which]
        return pltpu.make_async_copy(pool.at[page], outs[n].at[which * pages + p], sems.at[n, which, p])

    def each(do):
        for n in range(2):

            @pl.when(slots[n] >= 0)
            def _():
                for p in range(pages):
                    for which in range(2):
                        do(load(n, which, p))

    each(lambda copy: copy.start())
    half = groups // 2
    number = jnp.int32(0)
    if half == 2:
        for m in range(mig.shape[0]):
            number = number | jnp.where(mig[m, 0] >= half, mig[m, 0] - half + 1, 0)
    facts[NUMBER] = number
    facts[OUT_NEAR], facts[OUT_FAR] = slots
    near, far, far_gap = incoming(mig, lens, me, groups)
    facts[IN_NEAR], facts[NEAR_LEN] = near
    facts[IN_FAR], facts[FAR_LEN] = far
    facts[FAR_GAP] = far_gap
    for s in range(slot_count):
        facts[LENGTHS + s] = lens[me, s]
        for p in range(pages):
            facts[LENGTHS + slot_count + s * pages + p] = table[0, p, s]
    each(lambda copy: copy.wait())


def attend_kernel(
    facts,
    states_hbm,
    query_hbm,
    key_weight,
    value_weight,
    out_weight,
    kp,
    vp,
    mig,
    lens,
    table,
    key_out,
    value_out,
    partial,
    new_rows,
    states,
    query,
    wk,
    wv,
    wo,
    q_scr,
    a_scr,
    tiles,
    load_sems,
    store_sems,
    tile_sems,
):
    del mig, lens, table
    slot_count, steps, _ = states.shape
    rows = slot_count * steps
    page_len, head_dim = kp.shape[1:]
    pages = kp.shape[0] // slot_count
    heads = query.shape[2] // head_dim
    span = pages * page_len
    pools = ((kp, key_out, 0), (vp, value_out, head_dim))
    number = 0

    def split(source, target, parts):
        nonlocal number
        size = source.shape[0] // parts
        copies = []
        for part in range(parts):
            piece = pl.ds(part * size, size)
            copies.append(pltpu.make_async_copy(source.at[piece], target.at[piece], load_sems.at[number]))
            number += 1
        return copies

    (load_query,) = split(query_hbm, query, 1)
    (load_states,) = split(states_hbm, states, 1)
    load_wk = split(key_weight, wk, PARTS)
    load_wv = split(value_weight, wv, PARTS)
    loads = split(out_weight, wo, PARTS)
    stores = [pltpu.make_async_copy(pool, out, store_sems.at[n]) for n, (pool, out, _) in enumerate(pools)]
    for copy in [load_query, load_states] + load_wk + load_wv + loads:
        copy.start()
    near, far = facts[OUT_NEAR], facts[OUT_FAR]
    lengths = [facts[LENGTHS + s] for s in range(slot_count)]
    first_page = [LENGTHS + slot_count + s * pages for s in range(slot_count)]
    numbers = [[facts[first_page[s] + p] for p in range(pages)] for s in range(slot_count)]

    load_query.wait()
    for s in range(slot_count):
        qf = query[s].astype(F32)
        for h in range(heads):
            q_scr[pl.ds(h * rows + s * steps, steps), :] = qf[:, h * head_dim : (h + 1) * head_dim]

    count = steps * heads
    nt = (((1,), (1,)), ((), ()))
    queries = jnp.concatenate(
        [q_scr[pl.ds(r, heads, stride=rows), :] for r in range(rows)], 0
    ).astype(BF16)
    position = lax.broadcasted_iota(jnp.int32, (count, span), 1)
    scaling = head_dim**-0.5
    scores = []
    for s in range(slot_count):
        keys = jnp.concatenate([kp[n] for n in numbers[s]], 0)
        cached = lax.dot_general(
            queries[s * count : (s + 1) * count], keys, nt, preferred_element_type=F32
        )
        scores.append(jnp.where(position < lengths[s], cached * scaling, -jnp.inf))
    cached = jnp.concatenate(scores, 0)

    for store in stores:
        store.start()
    load_states.wait()
    x = jnp.concatenate([states[s].astype(F32) for s in range(slot_count)], 0).astype(BF16)
    fresh_k = jnp.zeros((rows, head_dim), F32)
    fresh_v = jnp.zeros((rows, head_dim), F32)
    size = wk.shape[0] // PARTS
    for part in range(PARTS):
        piece = slice(part * size, (part + 1) * size)
        load_wk[part].wait()
        fresh_k = fresh_k + jnp.dot(x[:, piece], wk[piece, :], preferred_element_type=F32)
        load_wv[part].wait()
        fresh_v = fresh_v + jnp.dot(x[:, piece], wv[piece, :], preferred_element_type=F32)
    fresh_k = fresh_k.astype(BF16)
    fresh_v = fresh_v.astype(BF16)
    new_rows[:, :head_dim] = fresh_k
    new_rows[:, head_dim:] = fresh_v

    fresh = lax.dot_general(queries, fresh_k, nt, preferred_element_type=F32) * scaling
    fresh_row = lax.broadcasted_iota(jnp.int32, fresh.shape, 0)
    fresh_col = lax.broadcasted_iota(jnp.int32, fresh.shape, 1)
    first = fresh_row // count * steps
    allowed = (fresh_col >= first) & (fresh_col <= fresh_row // heads)
    fresh = jnp.where(allowed, fresh, -jnp.inf)
    peak = jnp.maximum(jnp.max(cached, 1, keepdims=True), jnp.max(fresh, 1, keepdims=True))
    cached = jnp.exp(cached - peak)
    fresh = jnp.exp(fresh - peak)
    share = 1.0 / (jnp.sum(cached, 1, keepdims=True) + jnp.sum(fresh, 1, keepdims=True))
    cached_w = (cached * share).astype(BF16)
    fresh_w = (fresh * share).astype(BF16)
    fresh_out = jnp.dot(fresh_w, fresh_v, preferred_element_type=F32)
    for s in range(slot_count):
        values = jnp.concatenate([vp[n] for n in numbers[s]], 0)
        piece = slice(s * count, (s + 1) * count)
        out = jnp.dot(cached_w[piece], values, preferred_element_type=F32) + fresh_out[piece]
        for t in range(steps):
            a_scr[pl.ds(s * steps + t, heads, stride=rows), :] = out[t * heads : (t + 1) * heads]

    tile = tiles.shape[3]
    row = lax.broadcasted_iota(jnp.int32, (tile, head_dim), 0)
    fresh_f = (fresh_k.astype(F32), fresh_v.astype(F32))
    places = []
    for s in range(slot_count):
        live = (lengths[s] > 0) & (s != near) & (s != far)
        for t in range(steps):
            at = lengths[s] + t
            page = facts[first_page[s] + at // page_len]
            low = at // tile * tile
            base = pl.multiple_of(lax.rem(low, page_len), tile)
            places.append((s, t, page, base, live & ((t == 0) | (lax.rem(at, tile) == 0))))
            for n, (pool, _, _) in enumerate(pools):
                merged = pool[page, pl.ds(base, tile), :].astype(F32)
                for u in range(steps):
                    line = fresh_f[n][s * steps + u : s * steps + u + 1]
                    merged = jnp.where(row + low == lengths[s] + u, line, merged)
                tiles[n, s, t] = merged.astype(BF16)
    for store in stores:
        store.wait()

    def put(n, s, t, page, base):
        return pltpu.make_async_copy(
            tiles.at[n, s, t], pools[n][1].at[page, pl.ds(base, tile), :], tile_sems.at[n, s, t]
        )

    for s, t, page, base, wanted in places:

        @pl.when(wanted)
        def _():
            for n in range(2):
                put(n, s, t, page, base).start()

    attention = jnp.concatenate([a_scr[h * rows : (h + 1) * rows, :].astype(BF16) for h in range(heads)], 1)
    result = jnp.zeros((rows, wo.shape[1]), F32)
    size = wo.shape[0] // PARTS
    for part in range(PARTS):
        piece = slice(part * size, (part + 1) * size)
        loads[part].wait()
        result = result + jnp.dot(attention[:, piece], wo[piece, :], preferred_element_type=F32)
    partial[...] = result.astype(BF16)
    for s, t, page, base, wanted in places:

        @pl.when(wanted)
        def _():
            for n in range(2):
                put(n, s, t, page, base).wait()


def finish_rows_kernel(facts, new_rows, *refs):
    *parts, mixed, near_out, far_out, scr = refs
    slots = facts[OUT_NEAR], facts[OUT_FAR]
    width = parts[0].shape[1]
    terms = [part[...].astype(F32) for part in parts]
    level = 1
    while level < len(terms):
        terms = [terms[n] + terms[n ^ level] for n in range(len(terms))]
        level *= 2
    total = terms[0]
    slot_count, steps, _ = scr.shape
    for s in range(slot_count):
        live = (facts[LENGTHS + s] > 0) & (s != slots[0]) & (s != slots[1])
        own = total[s * steps : (s + 1) * steps]
        scr[s, :, :width] = own
        scr[s, :, width:] = new_rows[s * steps : (s + 1) * steps, :].astype(F32)
        mixed[s] = jnp.where(live, own, 0.0).astype(BF16)
    for slot, out in zip(slots, (near_out, far_out)):
        out[...] = scr[jnp.maximum(slot, 0)].astype(BF16)


def place_kernel(ways, facts, *refs):
    near_pages, *far_pages = refs[: 1 + ways]
    near_rows, *far_rows = refs[1 + ways : 2 + 2 * ways]
    mixed_in, _, _, mixed, key_out, value_out, stage, out_sems, line_sems, own_sem = refs[2 + 2 * ways :]
    pages = stage.shape[1] // 2
    page_len, head_dim = stage.shape[2:]
    slot_count, steps, width = mixed.shape
    row = lax.broadcasted_iota(jnp.int32, (page_len, head_dim), 0)
    far_gap = facts[FAR_GAP]
    cases = [(0, facts[IN_NEAR], facts[NEAR_LEN], facts[IN_NEAR] >= 0, near_pages, near_rows)]
    for way in range(ways):
        came = facts[IN_FAR] >= 0
        if ways == 2:
            came = came & ((far_gap == 1) == (way == 0))
        cases.append((1, facts[IN_FAR], facts[FAR_LEN], came, far_pages[way], far_rows[way]))

    def store(n, slot, p, which, source):
        pool = (key_out, value_out)[which]
        page = facts[LENGTHS + slot_count + slot * pages + p]
        return pltpu.make_async_copy(source, pool.at[page], out_sems.at[n, which, p])

    def store_line(n, slot, rows):
        return pltpu.make_async_copy(rows.at[:, pl.ds(0, width)], mixed.at[slot], line_sems.at[n])

    own = pltpu.make_async_copy(mixed_in, mixed, own_sem)
    own.start()
    for n, slot, length, came, arrived, rows in cases:

        @pl.when(came)
        def _():
            fresh = rows[:, width:].astype(F32)
            for p in range(pages):
                whole = length >= (p + 1) * page_len

                @pl.when(whole)
                def _():
                    for which in range(2):
                        store(n, slot, p, which, arrived.at[which * pages + p]).start()

                @pl.when(jnp.logical_not(whole))
                def _():
                    at = row + p * page_len
                    for which in range(2):
                        page = jnp.where(at < length, arrived[which * pages + p].astype(F32), 0.0)
                        for t in range(steps):
                            line = fresh[t : t + 1, which * head_dim : (which + 1) * head_dim]
                            page = jnp.where(at == length + t, line, page)
                        stage[n, which * pages + p] = page.astype(BF16)
                        store(n, slot, p, which, stage.at[n, which * pages + p]).start()

    own.wait()
    for n, slot, _, came, _, rows in cases:

        @pl.when(came)
        def _():
            store_line(n, slot, rows).start()

    for n, slot, _, came, arrived, rows in cases:

        @pl.when(came)
        def _():
            for p in range(pages):
                for which in range(2):
                    store(n, slot, p, which, arrived.at[which * pages + p]).wait()
            store_line(n, slot, rows).wait()


def run(
    near_hops,
    far_hops,
    near,
    far,
    facts,
    scalars,
    token_states,
    query_rows,
    key_weight,
    value_weight,
    out_weight,
    keys,
    values,
):
    groups = lax.axis_size("dec")
    tp = lax.axis_size("tp")
    slot_count, steps, model = token_states.shape
    _, page_len, head_dim = keys.shape
    rows = slot_count * steps
    width = out_weight.shape[1]
    heads = query_rows.shape[2] // head_dim
    pool_shape = jax.ShapeDtypeStruct(keys.shape, BF16)
    limit = pltpu.CompilerParams(vmem_limit_bytes=63 * 2**20)

    pages_in = [lax.ppermute(near, "dec", near_hops)] + [lax.ppermute(far, "dec", hops) for hops in far_hops]

    key_mid, value_mid, partial, new_rows = pl.pallas_call(
        attend_kernel,
        out_shape=(
            pool_shape,
            pool_shape,
            jax.ShapeDtypeStruct((rows, width), BF16),
            jax.ShapeDtypeStruct((rows, 2 * head_dim), BF16),
        ),
        in_specs=[SMEM] + [ANY] * 5 + [VMEM] * 2 + [ANY] * 3,
        out_specs=(HBM, HBM, VMEM, VMEM),
        scratch_shapes=[
            pltpu.VMEM(token_states.shape, BF16),
            pltpu.VMEM(query_rows.shape, BF16),
            pltpu.VMEM(key_weight.shape, BF16),
            pltpu.VMEM(value_weight.shape, BF16),
            pltpu.VMEM(out_weight.shape, BF16),
            pltpu.VMEM(((heads + 1) * rows, head_dim), F32),
            pltpu.VMEM(((heads + 1) * rows, head_dim), F32),
            pltpu.VMEM((2, slot_count, steps, 16, head_dim), BF16),
            pltpu.SemaphoreType.DMA((2 + 3 * PARTS,)),
            pltpu.SemaphoreType.DMA((2,)),
            pltpu.SemaphoreType.DMA((2, slot_count, steps)),
        ],
        compiler_params=pltpu.CompilerParams(vmem_limit_bytes=40 * 2**20),
        cost_estimate=pl.CostEstimate(flops=1_000_000, bytes_accessed=1_000_000, transcendentals=0),
        name="attend",
    )(
        facts,
        token_states,
        query_rows,
        key_weight,
        value_weight,
        out_weight,
        keys,
        values,
        *scalars,
    )

    others = [lax.ppermute(partial, "tp", [(i, i ^ n) for i in range(tp)]) for n in range(1, tp)]
    row_shape = jax.ShapeDtypeStruct((steps, width + 2 * head_dim), BF16)
    mixed_mid, near_row, far_row = pl.pallas_call(
        finish_rows_kernel,
        out_shape=(jax.ShapeDtypeStruct((slot_count, steps, width), BF16), row_shape, row_shape),
        in_specs=[SMEM, VMEM] + [VMEM] * tp,
        out_specs=(VMEM, VMEM, VMEM),
        scratch_shapes=[pltpu.VMEM((slot_count, steps, width + 2 * head_dim), F32)],
        compiler_params=pltpu.CompilerParams(vmem_limit_bytes=8 * 2**20),
        name="rows",
    )(facts, new_rows, partial, *others)
    rows_in = [lax.ppermute(near_row, "dec", near_hops)] + [lax.ppermute(far_row, "dec", hops) for hops in far_hops]
    pages = keys.shape[0] // slot_count
    ways = len(pages_in) - 1
    mixed_shape = jax.ShapeDtypeStruct((slot_count, steps, width), BF16)
    mixed, key_out, value_out = pl.pallas_call(
        functools.partial(place_kernel, ways),
        out_shape=(mixed_shape, pool_shape, pool_shape),
        in_specs=[SMEM] + [VMEM] * (2 + 2 * ways) + [VMEM] + [HBM] * 2,
        out_specs=(HBM, HBM, HBM),
        scratch_shapes=[
            pltpu.VMEM((2, 2 * pages, page_len, head_dim), BF16),
            pltpu.SemaphoreType.DMA((2, 2, pages)),
            pltpu.SemaphoreType.DMA((2,)),
            pltpu.SemaphoreType.DMA,
        ],
        input_output_aliases={4 + 2 * ways: 1, 5 + 2 * ways: 2},
        compiler_params=pltpu.CompilerParams(vmem_limit_bytes=41943040),
        name="place",
    )(facts, *pages_in, *rows_in, mixed_mid, key_mid, value_mid)
    return mixed, key_out, value_out


def moved(migrations, cached_len, table, inputs):
    groups = lax.axis_size("dec")
    half = groups // 2
    keys, values = inputs[-2:]
    scalars = (migrations, cached_len, table)
    _, page_len, head_dim = keys.shape
    pages, slot_count = table.shape[1:]
    facts_shape = jax.ShapeDtypeStruct((LENGTHS + slot_count + slot_count * pages,), jnp.int32)
    moved_shape = jax.ShapeDtypeStruct((2 * pages, page_len, head_dim), BF16)
    near, far, facts = pl.pallas_call(
        functools.partial(pack_kernel, groups),
        out_shape=(moved_shape, moved_shape, facts_shape),
        in_specs=[SMEM, SMEM, SMEM, HBM, HBM],
        out_specs=(VMEM, VMEM, SMEM),
        scratch_shapes=[pltpu.SemaphoreType.DMA((2, 2, pages))],
        compiler_params=pltpu.CompilerParams(vmem_limit_bytes=40 * 2**20),
        cost_estimate=pl.CostEstimate(flops=0, bytes_accessed=1_000_000, transcendentals=0),
        name="pack",
    )(migrations, cached_len, table, keys, values)
    if half != 2:
        far_hops = (shifted(groups, 1), shifted(groups, 1 + half))
        return run(shifted(groups, half), far_hops, near, far, facts, scalars, *inputs)
    branches = []
    for case in range(2**half):
        senders = [pair + half * (case >> pair & 1) for pair in range(half)]
        receivers = [(sender + half) % groups for sender in senders]
        near_hops = [(senders[pair], receivers[pair]) for pair in range(half)]
        far_hops = [(senders[pair], receivers[(pair + 1) % half]) for pair in range(half)]
        near_hops += [(b, a) for a, b in near_hops]
        far_hops += [(b, a) for a, b in far_hops]
        branches.append(functools.partial(run, near_hops, (far_hops,)))
    outs = lax.switch(facts[NUMBER], branches, near, far, facts, scalars, *inputs)
    return pl.pallas_call(
        lambda *refs: None,
        out_shape=tuple(jax.ShapeDtypeStruct(out.shape, out.dtype) for out in outs),
        in_specs=[HBM] * 3,
        out_specs=(HBM,) * 3,
        input_output_aliases={0: 0, 1: 1, 2: 2},
        compiler_params=pltpu.CompilerParams(vmem_limit_bytes=67004006),
        name="keep",
    )(*outs)


def local(
    token_states,
    query_rows,
    key_weight,
    value_weight,
    out_weight,
    key_pool,
    value_pool,
    cached_len,
    page_table,
    migrations,
):
    groups = lax.axis_size("dec")
    pool_pages, _, page_len, head_dim = key_pool.shape
    slot_count, steps, _ = token_states.shape
    keys = key_pool.reshape(pool_pages, page_len, head_dim)
    values = value_pool.reshape(pool_pages, page_len, head_dim)
    table = jnp.swapaxes(page_table, 1, 2)
    pages = table.shape[1]
    inputs = (
        token_states,
        query_rows,
        key_weight,
        value_weight,
        out_weight,
        keys,
        values,
    )
    mixed, key_out, value_out = moved(migrations, cached_len, table, inputs)
    return mixed, key_out.reshape(key_pool.shape), value_out.reshape(value_pool.shape)


def solution(mesh):
    placed = (
        P(("rep", "dec"), None, None),
        P(("rep", "dec"), None, "tp"),
        P(None, "tp"),
        P(None, "tp"),
        P("tp", None),
        P(("rep", "dec"), "tp", None, None),
        P(("rep", "dec"), "tp", None, None),
        P("rep", None),
        P(("rep", "dec"), None, None),
        P("rep", None),
    )
    return jax.shard_map(
        local,
        mesh=mesh,
        in_specs=placed,
        out_specs=(
            P(("rep", "dec"), None, None),
            P(("rep", "dec"), "tp", None, None),
            P(("rep", "dec"), "tp", None, None),
        ),
        check_vma=False,
    )
```
